256 devices in a mesh: seq: 16 (over y, x), tp: 8 (over z), dp: 2 (over core).
Axes of the slice: x: 4, y: 4, z: 8, core: 2. Of those that a mesh axis runs over, the one named last changes fastest.
Arguments:
- queries: bfloat16 [8192, 8192], P(('dp', 'seq'), 'tp'), parts along dimension 0, may hold values from -40 to 40
- d_out: bfloat16 [8192, 8192], P(('dp', 'seq'), 'tp'), parts along dimension 0, may hold values from -6 to 6
- image_feats: bfloat16 [32, 896, 7680], P(('dp', 'seq'), None, 'tp'), parts along dimension 0, may hold values from -10 to 10
- key_weight: bfloat16 [7680, 1024], P('tp'), may hold values from -0.0625 to 0.0625
- value_weight: bfloat16 [7680, 1024], P('tp'), may hold values from -0.0625 to 0.0625
- image_lists: int32 [128, 2], P(('dp', 'seq')), parts along dimension 0, may hold values from 0 to 15, all different within a row; in each aligned block of 4 rows (0 to 3, 4 to 7, ...) at most 2 rows name the same one
- owner: int32 [32], P('dp'), parts along dimension 0, may hold values from 0 to 15, each once
Outputs:
- attended: bfloat16 [8192, 8192], P(('dp', 'seq'), 'tp'), parts along dimension 0
- d_queries: bfloat16 [8192, 8192], P(('dp', 'seq'), 'tp'), parts along dimension 0
- d_projection: bfloat16 [4096, 7680], P(('dp', 'seq'), 'tp'), parts along dimension 0
The draws below stay inside these ranges and needn't reach their ends.
There are 2 independent parts, one for each index of `dp`. The reference program is written for one: setup_inputs(seed, part) draws one part's arguments, and reference() takes and returns one part's arrays. A program takes and returns all parts, laid end to end along the dimension named above; an argument that names none is the same for every part. Nothing has to cross between parts.
Inputs may be any that keep to these rules, and one draw needn't show every extreme that they name: `image_lists`: each row lists 2 different images; within the blocks of one index of seq no image is listed by more than 2 blocks, a bound that some block reaches. `owner`: each position once.
All inputs are finite; a program needn't handle non-finite values.
Results may differ from the reference program's by a relative error of at most 0.027.
The reference program's roundings to bfloat16 on the way count: a program that leaves them out, or rounds other values in their place, can miss the bound.
Values may be sent and summed in bfloat16 or wider, within the bound.
No kernel may reach another device: no remote copies, remote signals or barrier semaphores. Data moves between devices by JAX's collectives and lax.ppermute only.
A program may use at most 128 MiB of HBM per device.

```python
import math
import jax
import jax.numpy as jnp
import numpy as np
from jax import lax

QHEADS = 64
KVHEADS = 8
HEAD_DIM = 128
VISION = 7680
BLOCK = 64
LISTED = 2
BLOCKS_DEV = 4
IMAGE_TOK = 896
TOKENS = 4096
BLOCKS = 64
IMAGES = 16
CAPACITY = 2


def draw_queries(key, part):
    key = jax.random.fold_in(key, 11)
    base_key, scale_key = jax.random.split(key, 2)
    shape = (TOKENS, QHEADS * HEAD_DIM)
    row_scale = jnp.exp(jax.random.uniform(scale_key, (TOKENS, 1), jnp.float32, math.log(0.3), math.log(3.0)))
    values = jnp.clip(jax.random.normal(base_key, shape, jnp.float32), -4.0, 4.0) * row_scale
    return values.astype(jnp.bfloat16)


def draw_image_feats(key, part):
    key = jax.random.fold_in(key, 23)
    base_key, scale_key = jax.random.split(key, 2)
    shape = (IMAGES, IMAGE_TOK, VISION)
    row_scale = jnp.exp(jax.random.uniform(scale_key, (IMAGES, IMAGE_TOK, 1), jnp.float32, math.log(0.5), math.log(2.0)))
    values = jnp.clip(jax.random.normal(base_key, shape, jnp.float32), -4.0, 4.0) * row_scale
    return values.astype(jnp.bfloat16)


def steps_of(stream_key, dims, cuts, smallest, largest):
    def one(position, shards_of):
        steps = jax.random.uniform(jax.random.fold_in(jax.random.fold_in(stream_key, 6), position), (shards_of,), jnp.float32, smallest / len(cuts), largest / len(cuts))
        return jnp.repeat(jnp.exp(steps), dims[position] // shards_of).reshape((-1,) + (1,) * (len(dims) - position - 1))

    factor_of = one(*cuts[0])
    for cut in cuts[1:]:
        factor_of = factor_of * one(*cut)
    return factor_of


def shared_out(stream_key, own, number, rows, count, top, reach, lean):
    order = jax.random.permutation(stream_key, count)
    packed, usual = shares(count, rows * top, reach, lean, True), shares(count, rows * top, reach, lean, False)
    places = jnp.arange(count)

    def named(tallies, turn):
        used = int((tallies > 0).sum())
        fixed = max(1, used // 4)
        passed = fixed + (places - fixed + turn * (used - fixed)) % max(1, count - fixed)
        return jnp.zeros((count,), jnp.int32).at[order[jnp.where(places < fixed, places, passed)]].set(jnp.asarray(tallies, jnp.int32))

    tallies = jnp.where(number % 4 == 0, named(packed, number // 4), named(usual, number - number // 4 - 1))
    mixed = jax.random.permutation(jax.random.fold_in(own, 3), count)
    source_of, receiver = mixed[0:count // 2 * 2:2], mixed[1:count // 2 * 2:2]
    room = jnp.minimum(tallies[source_of] - 1, reach - tallies[receiver]) // 2
    room = jnp.where((source_of == order[0]) | (receiver == order[0]) | (tallies[receiver] == 0), 0, jnp.maximum(room, 0))
    passed = jax.random.randint(jax.random.fold_in(own, 4), (count // 2,), 0, 1 << 20) % (room + 1)
    tallies = tallies.at[source_of].add(-passed).at[receiver].add(passed)
    labels = jnp.searchsorted(jnp.cumsum(tallies), jnp.arange(rows * top), side="right").astype(jnp.int32)
    table = labels.reshape(top, rows).T
    table = table[jax.random.permutation(jax.random.fold_in(own, 1), rows)]
    turn = jax.random.randint(jax.random.fold_in(own, 2), (rows, 1), 0, top)
    return jnp.take_along_axis(table, (jnp.arange(top)[None, :] + turn) % top, axis=1)


def shares(amount, total, most, slope, full):
    weights = [(1 << 20) // math.isqrt(rank ** slope) + 1 for rank in range(1, amount + 1)]
    largest = most if full else min(most, max(-(-total // amount), total * weights[0] // sum(weights)))
    least = 1 if total - largest >= amount - 1 else 0
    given, spare = [largest] + [least] * (amount - 1), total - largest - least * (amount - 1)
    while spare > 0:
        free = [i for i in range(1, amount) if given[i] < largest] or [i for i in range(1, amount) if given[i] < most]
        pool, remaining = sum([weights[i] for i in free]), spare
        for i in free:
            addition = min(most - given[i], max(1, remaining * weights[i] // pool), spare)
            given[i] = given[i] + addition
            spare = spare - addition
    return np.array(given)


def noise(stream_key, shape, scale, reach, shards=(), held_as=jnp.bfloat16):
    array = jax.random.normal(stream_key, shape, jnp.float32) * scale
    if len(shards) > 0:
        array = steps_of(stream_key, shape, shards, -0.22, 0.18) * array
    return jnp.clip(array, min=-reach, max=reach).astype(held_as)


def setup_inputs(seed: int = 0, part: int = 0) -> dict:
    arg_keys = jax.random.split(jax.random.key(seed), 8)
    part_keys = jax.random.split(jax.random.fold_in(arg_keys[7], part), 8)
    queries = draw_queries(jax.random.fold_in(jax.random.fold_in(arg_keys[7], part), 71), part)
    d_out = noise(part_keys[1], (TOKENS, QHEADS * HEAD_DIM), 1.0, 6.0, ((0, 16), (1, 8)))
    image_feats = draw_image_feats(jax.random.fold_in(jax.random.fold_in(arg_keys[7], part), 71), part)
    key_weight = noise(arg_keys[3], (VISION, KVHEADS * HEAD_DIM), VISION ** -0.5, 0.0625, ((0, 8),))
    value_weight = noise(arg_keys[4], (VISION, KVHEADS * HEAD_DIM), VISION ** -0.5, 0.0625, ((0, 8),))
    image_lists_keys = jax.random.split(jax.random.fold_in(part_keys[5], 1), BLOCKS // BLOCKS_DEV)
    image_lists_turns = jax.random.permutation(jax.random.fold_in(part_keys[5], 3), BLOCKS // BLOCKS_DEV)
    image_lists = jax.vmap(lambda own, number: shared_out(jax.random.fold_in(part_keys[5], 2), own, number, BLOCKS_DEV, IMAGES, LISTED, CAPACITY, 2))(image_lists_keys, image_lists_turns).reshape((BLOCKS, LISTED))
    owner = jax.random.permutation(part_keys[6], IMAGES).astype(jnp.int32)
    return {"queries": queries, "d_out": d_out, "image_feats": image_feats, "key_weight": key_weight, "value_weight": value_weight, "image_lists": image_lists, "owner": owner}


def rounded(values):
    return lax.optimization_barrier(values.astype(jnp.bfloat16)).astype(jnp.float32)


def attend(query_rows, image_pair):
    score_scale = HEAD_DIM ** -0.5
    key_rows = image_pair[..., :HEAD_DIM]
    value_rows = image_pair[..., HEAD_DIM:]
    scores = jnp.einsum("rkgd,ktd->kgrt", query_rows, key_rows) * score_scale
    row_max = jnp.max(scores, axis=-1)
    weights = jnp.exp(scores - row_max[..., None])
    row_total = jnp.sum(weights, axis=-1)
    partial_out = rounded(jnp.einsum("kgrt,ktd->rkgd", rounded(weights), value_rows))
    return partial_out, row_max.transpose(2, 0, 1), row_total.transpose(2, 0, 1)


def grad_tile(query_rows, grad_rows, log_total, row_inner, image_pair):
    score_scale = HEAD_DIM ** -0.5
    key_rows = image_pair[..., :HEAD_DIM]
    value_rows = image_pair[..., HEAD_DIM:]
    scores = jnp.einsum("rkgd,ktd->kgrt", query_rows, key_rows) * score_scale
    probabilities = jnp.exp(scores - log_total.transpose(1, 2, 0)[..., None])
    value_grad = jnp.einsum("kgrt,rkgd->ktd", rounded(probabilities), grad_rows)
    prob_grad = jnp.einsum("rkgd,ktd->kgrt", grad_rows, value_rows)
    score_grad = rounded(probabilities * (prob_grad - row_inner.transpose(1, 2, 0)[..., None]))
    key_grad = jnp.einsum("kgrt,rkgd->ktd", score_grad, query_rows) * score_scale
    query_grad = rounded(jnp.einsum("kgrt,ktd->rkgd", score_grad, key_rows) * score_scale)
    return query_grad, jnp.concatenate([key_grad, value_grad], axis=-1)


def reference(queries, d_out, image_feats, key_weight, value_weight, image_lists, owner):
    group_size = QHEADS // KVHEADS
    feats_flat = image_feats.reshape(IMAGES * IMAGE_TOK, VISION)
    key_flat = rounded(jnp.dot(feats_flat, key_weight, preferred_element_type=jnp.float32))
    value_flat = rounded(jnp.dot(feats_flat, value_weight, preferred_element_type=jnp.float32))
    key_flat = key_flat.reshape(IMAGES, IMAGE_TOK, KVHEADS, HEAD_DIM)
    value_flat = value_flat.reshape(IMAGES, IMAGE_TOK, KVHEADS, HEAD_DIM)
    pair_all = jnp.concatenate([key_flat, value_flat], axis=-1).transpose(0, 2, 1, 3)
    places = owner[image_lists].astype(jnp.int32)
    query_blocks = queries.reshape(BLOCKS, BLOCK, KVHEADS, group_size, HEAD_DIM).astype(jnp.float32)
    grad_blocks = d_out.reshape(BLOCKS, BLOCK, KVHEADS, group_size, HEAD_DIM).astype(jnp.float32)

    def step(accum, inputs):
        query_one, grad_one, place_one = inputs
        results = [attend(query_one, pair_all[place_one[entry]]) for entry in range(LISTED)]
        partials = jnp.stack([item[0] for item in results])
        maxima = jnp.stack([item[1] for item in results])
        totals = jnp.stack([item[2] for item in results])
        list_max = jnp.max(maxima, axis=0)
        factor = jnp.exp(maxima - list_max[None])
        denominator = jnp.sum(factor * totals, axis=0)
        numerator = jnp.sum(factor[..., None] * partials, axis=0)
        output = rounded(numerator / denominator[..., None])
        log_total = list_max + jnp.log(denominator)
        row_inner = jnp.sum(grad_one * output, axis=-1)
        query_sum = jnp.zeros(query_one.shape, jnp.float32)
        for entry in range(LISTED):
            query_grad, pair_grad = grad_tile(query_one, grad_one, log_total, row_inner, pair_all[place_one[entry]])
            query_sum = query_sum + query_grad
            accum = accum.at[place_one[entry]].add(pair_grad)
        return accum, (output.astype(jnp.bfloat16), query_sum.astype(jnp.bfloat16))

    start = jnp.zeros((IMAGES, KVHEADS, IMAGE_TOK, 2 * HEAD_DIM), jnp.float32)
    accum, (outputs, query_grads) = lax.scan(step, start, (query_blocks, grad_blocks, places))
    grads_rounded = rounded(accum).reshape(IMAGES, KVHEADS, IMAGE_TOK, 2, HEAD_DIM)
    grad_rows = grads_rounded.transpose(3, 1, 4, 0, 2).reshape(2 * KVHEADS * HEAD_DIM, IMAGES * IMAGE_TOK)
    d_projection = jnp.dot(grad_rows, feats_flat.astype(jnp.float32), preferred_element_type=jnp.float32)
    attended = outputs.reshape(TOKENS, QHEADS * HEAD_DIM)
    d_queries = query_grads.reshape(TOKENS, QHEADS * HEAD_DIM)
    return attended, d_queries, d_projection.astype(jnp.bfloat16)
```

```python
import functools
import math

import jax
import jax.numpy as jnp
from jax import lax
from jax.experimental import pallas as pl
from jax.experimental.pallas import tpu as pltpu
from jax.sharding import PartitionSpec as P

QHEADS = 64
KVHEADS = 8
GROUP = QHEADS // KVHEADS
HEAD_DIM = 128
BLOCK = 64
ROWS = BLOCK * GROUP
TILE = 128
SIDE = 4
SCALE = HEAD_DIM ** -0.5
LOG2E = math.log2(math.e)
LN2 = math.log(2.0)
BF16 = jnp.bfloat16
F32 = jnp.float32
NT = (((1,), (1,)), ((), ()))
VMEM_LIMIT = 56 * 1024 * 1024


def matmul(a, b):
    return jnp.dot(a, b, preferred_element_type=F32)


def matmul_nt(a, b):
    return lax.dot_general(a, b, NT, preferred_element_type=F32)


def project_kernel(feats_ref, key_ref, value_ref, out_ref):
    feats = feats_ref[...]
    for part, weight_ref in enumerate((key_ref, value_ref)):
        both = matmul(feats, weight_ref[...])
        lanes = slice(part * HEAD_DIM, (part + 1) * HEAD_DIM)
        out_ref[0, :, lanes] = both[:, :HEAD_DIM]
        out_ref[1, :, lanes] = both[:, HEAD_DIM:]


def project(feats, key_weight, value_weight):
    tokens, depth = feats.shape
    weight_spec = pl.BlockSpec((depth, 2 * HEAD_DIM), lambda i: (0, i))
    return pl.pallas_call(
        project_kernel,
        grid=(KVHEADS // 2,),
        in_specs=[pl.BlockSpec((tokens, depth), lambda i: (0, 0)), weight_spec, weight_spec],
        out_specs=pl.BlockSpec((2, tokens, 2 * HEAD_DIM), lambda i: (i, 0, 0)),
        out_shape=jax.ShapeDtypeStruct((KVHEADS, tokens, 2 * HEAD_DIM), F32),
        compiler_params=pltpu.CompilerParams(vmem_limit_bytes=VMEM_LIMIT),
        name="project",
    )(feats, key_weight, value_weight)


def attend_kernel(heads, places_ref, query_ref, grad_ref, pair0_ref, pair1_ref, out_ref, dq_ref, stat_ref):
    pairs = (pair0_ref, pair1_ref)
    rows = heads * BLOCK
    lane = lax.broadcasted_iota(jnp.int32, (rows, HEAD_DIM), 1)
    for first in range(0, GROUP, heads):
        cols = [slice((first + g) * HEAD_DIM, (first + g + 1) * HEAD_DIM) for g in range(heads)]
        query = jnp.concatenate([query_ref[:, c] for c in cols], axis=0)
        grad = jnp.concatenate([grad_ref[:, c] for c in cols], axis=0)
        weights, maxima, totals, partials = [], [], [], []
        for pair in pairs:
            scores = matmul_nt(query, pair[0, :, :HEAD_DIM]) * (SCALE * LOG2E)
            row_max = jnp.max(scores, axis=1, keepdims=True)
            weight = jnp.exp2(scores - row_max)
            weights.append(weight)
            maxima.append(row_max)
            totals.append(jnp.sum(weight, axis=1, keepdims=True))
            partials.append(matmul(weight.astype(BF16), pair[0, :, HEAD_DIM:]).astype(BF16))
        top = jnp.maximum(maxima[0], maxima[1])
        factors = [jnp.exp2(m - top) for m in maxima]
        denominator = factors[0] * totals[0] + factors[1] * totals[1]
        numerator = factors[0] * partials[0].astype(F32) + factors[1] * partials[1].astype(F32)
        output = (numerator / denominator).astype(BF16)
        lse = top + jnp.log2(denominator)
        delta = jnp.sum(grad.astype(F32) * output.astype(F32), axis=1, keepdims=True)
        dq = []
        for pair, weight, factor in zip(pairs, weights, factors):
            prob_grad = matmul_nt(grad, pair[0, :, HEAD_DIM:])
            score_grad = weight * (factor / denominator) * (prob_grad - delta)
            part = matmul(score_grad.astype(BF16), pair[0, :, :HEAD_DIM]) * SCALE
            dq.append(part.astype(BF16).astype(F32))
        total = (dq[0] + dq[1]).astype(BF16)
        for g, c in enumerate(cols):
            out_ref[:, c] = output[g * BLOCK : (g + 1) * BLOCK]
            dq_ref[:, c] = total[g * BLOCK : (g + 1) * BLOCK]
        stats = jnp.transpose(jnp.where(lane == 0, lse, delta))
        stat_ref[0, :, first * BLOCK : (first + heads) * BLOCK] = stats[:8]


def attend(places, queries, d_out, pairs, heads=2):
    blocks = places.shape[0]
    tokens = pairs.shape[1]
    text = pl.BlockSpec((BLOCK, GROUP * HEAD_DIM), lambda c, p: (c, 0))

    def pair_spec(entry):
        return pl.BlockSpec((1, tokens, 2 * HEAD_DIM), lambda c, p: (p[c, entry], 0, 0))

    return pl.pallas_call(
        functools.partial(attend_kernel, heads),
        grid_spec=pltpu.PrefetchScalarGridSpec(
            num_scalar_prefetch=1,
            grid=(blocks,),
            in_specs=[text, text, pair_spec(0), pair_spec(1)],
            out_specs=[text, text, pl.BlockSpec((1, 8, ROWS), lambda c, p: (c, 0, 0))],
        ),
        out_shape=[
            jax.ShapeDtypeStruct(queries.shape, BF16),
            jax.ShapeDtypeStruct(queries.shape, BF16),
            jax.ShapeDtypeStruct((blocks, 8, ROWS), F32),
        ],
        compiler_params=pltpu.CompilerParams(vmem_limit_bytes=VMEM_LIMIT),
        name="attend",
    )(places, queries, d_out, pairs, pairs)


def spread_kernel(places_ref, column_ref, text_ref, stat_ref, pair_ref, out_ref):
    column = column_ref[0]
    blocks = text_ref.shape[0]
    tiles = pair_ref.shape[0]
    half = HEAD_DIM // 2

    def clear(m, carry):
        out_ref[:, m] = jnp.zeros((4, half, TILE), F32)
        return carry

    lax.fori_loop(0, tiles, clear, 0)

    def one(step, carry):
        block = step // 2
        place = places_ref[block, step % 2]
        line, spot = place // SIDE, place % SIDE
        begin = (7 * spot - column + SIDE - 1) // SIDE
        end = (7 * spot + 7 - column + SIDE - 1) // SIDE
        count = end - begin
        tile = line * 7 + begin

        def work(width):
            query = text_ref[block, 0]
            grad = text_ref[block, 1]
            lse = stat_ref[block, 0:1, :]
            delta = stat_ref[block, 1:2, :]
            pair = pair_ref[pl.ds(tile, width), 0].reshape(width * TILE, 2 * HEAD_DIM)
            scores = matmul(pair[:, :HEAD_DIM], query) * (SCALE * LOG2E)
            prob = jnp.exp2(scores - lse)
            prob_grad = matmul(pair[:, HEAD_DIM:], grad)
            score_grad = prob * (prob_grad - delta)
            d_value = matmul_nt(grad, prob.astype(BF16))
            d_key = matmul_nt(query, score_grad.astype(BF16))
            for i in range(width):
                lanes = slice(i * TILE, (i + 1) * TILE)
                out_ref[0, tile + i] += d_key[:half, lanes]
                out_ref[1, tile + i] += d_key[half:, lanes]
                out_ref[2, tile + i] += d_value[:half, lanes]
                out_ref[3, tile + i] += d_value[half:, lanes]

        @pl.when(count == 2)
        def _():
            work(2)

        @pl.when(count != 2)
        def _():
            work(1)

        return carry

    lax.fori_loop(0, 2 * blocks, one, 0)

    def scale(m, carry):
        out_ref[0, m] = out_ref[0, m] * SCALE
        out_ref[1, m] = out_ref[1, m] * SCALE
        return carry

    lax.fori_loop(0, tiles, scale, 0)


def spread(places, column, text, stats, pairs):
    blocks = text.shape[0]
    tiles = pairs.shape[0]
    half = HEAD_DIM // 2
    return pl.pallas_call(
        spread_kernel,
        grid_spec=pltpu.PrefetchScalarGridSpec(
            num_scalar_prefetch=2,
            grid=(1,),
            in_specs=[
                pl.BlockSpec(text.shape, lambda i, p, c: (0, 0, 0, 0)),
                pl.BlockSpec(stats.shape, lambda i, p, c: (0, 0, 0)),
                pl.BlockSpec((tiles, 1, TILE, 2 * HEAD_DIM), lambda i, p, c: (0, c[0], 0, 0)),
            ],
            out_specs=pl.BlockSpec((4, tiles, half, TILE), lambda i, p, c: (0, 0, 0, 0)),
        ),
        out_shape=jax.ShapeDtypeStruct((4, tiles, half, TILE), F32),
        compiler_params=pltpu.CompilerParams(vmem_limit_bytes=VMEM_LIMIT),
        name="spread",
    )(places, column, text, stats, pairs)


def fold_kernel(line_ref, grads_ref, own_ref, up_ref, down_ref, far_a_ref, far_b_ref, out_ref):
    line = line_ref[0]
    span = own_ref.shape[0]
    first = far_a_ref.shape[0]
    pieces = (
        (own_ref, 0, 0),
        (up_ref, SIDE - 1, 0),
        (down_ref, 1, 0),
        (far_a_ref, 2, 0),
        (far_b_ref, 2, first),
    )
    width = own_ref.shape[1]
    half = HEAD_DIM // 2
    for start in range(0, width, 256):
        cols = slice(start, min(start + 256, width))
        total = None
        for ref, shift, skip in pieces:
            offset = lax.rem(line + shift, SIDE) * span + skip
            part = matmul(grads_ref[:, pl.ds(pl.multiple_of(offset, TILE), ref.shape[0])], ref[:, cols])
            total = part if total is None else total + part
        for head in range(KVHEADS):
            out_ref[head % SIDE, (head // SIDE) * half : (head // SIDE + 1) * half, cols] = total[
                head * half : (head + 1) * half
            ]


def fold(line, grads, pieces):
    whole = [pl.BlockSpec(p.shape, lambda i, l: (0, 0)) for p in (grads, *pieces)]
    shape = (SIDE, HEAD_DIM, pieces[0].shape[1])
    return pl.pallas_call(
        fold_kernel,
        grid_spec=pltpu.PrefetchScalarGridSpec(
            num_scalar_prefetch=1,
            grid=(1,),
            in_specs=whole,
            out_specs=pl.BlockSpec(shape, lambda i, l: (0, 0, 0)),
        ),
        out_shape=jax.ShapeDtypeStruct(shape, F32),
        compiler_params=pltpu.CompilerParams(vmem_limit_bytes=VMEM_LIMIT),
        name="fold",
    )(line, grads, *pieces)


def along_x(shift):
    return [(y * SIDE + x, y * SIDE + (x + shift) % SIDE) for y in range(SIDE) for x in range(SIDE)]


def along_y(shift):
    return [(y * SIDE + x, ((y + shift) % SIDE) * SIDE + x) for y in range(SIDE) for x in range(SIDE)]


X_GROUPS = [[y * SIDE + x for x in range(SIDE)] for y in range(SIDE)]
Y_GROUPS = [[y * SIDE + x for y in range(SIDE)] for x in range(SIDE)]


def move(array, perm):
    return lax.ppermute(array, "seq", perm)


def per_device(queries, d_out, image_feats, key_weight, value_weight, image_lists, owner):
    me = lax.axis_index("seq")
    line, column = me // SIDE, me % SIDE
    blocks = image_lists.shape[0]
    feats = image_feats[0]
    tokens, depth = feats.shape
    tiles = tokens // TILE

    image_ids = lax.broadcasted_iota(jnp.int32, (*image_lists.shape, owner.shape[0]), 2)
    places = jnp.sum(jnp.where(image_lists[..., None] == image_ids, owner[None, None, :], 0), axis=-1)

    part = project(feats, key_weight, value_weight)
    queries_late, d_out_late, feats_late, part = lax.optimization_barrier((queries, d_out, feats, part))
    own_pair = lax.psum_scatter(part, "tp", scatter_dimension=0, tiled=True).astype(BF16)

    def turned(array):
        return array.reshape(blocks, BLOCK, GROUP, HEAD_DIM).transpose(0, 3, 2, 1).reshape(blocks, HEAD_DIM, ROWS)

    text = jnp.stack([turned(queries_late), turned(d_out_late)], axis=1)
    text_left = move(text, along_x(1))
    text_right = move(text, along_x(-1))
    far_a = move(text_left[: blocks // 2], along_x(1))
    far_b = move(text_right[blocks // 2 :], along_x(-1))
    row_text = jnp.concatenate([text, text_left, text_right, far_a, far_b], axis=0)

    tiled = jnp.concatenate([feats_late.reshape(tiles, TILE, depth), jnp.zeros((1, TILE, depth), BF16)])
    buffer = jnp.zeros((tiles + 1, TILE, depth), BF16)
    for shift in range(SIDE):
        target = (column + shift) % SIDE
        first = (target + column) % SIDE
        slab = jnp.concatenate(
            [
                lax.dynamic_slice_in_dim(tiled, first, 1, 0),
                lax.dynamic_slice_in_dim(tiled, first + SIDE, 1, 0),
            ]
        )
        if shift:
            slab = move(slab, along_x(shift))
        source = (column - shift) % SIDE
        first = (column + source) % SIDE
        slot = (7 * source + first - column) // SIDE
        second = jnp.where(first + SIDE < tiles, slot + 1, tiles)
        buffer = lax.dynamic_update_slice_in_dim(buffer, slab[1:], second, 0)
        buffer = lax.dynamic_update_slice_in_dim(buffer, slab[:1], slot, 0)
    own_feats = buffer[:tiles].reshape(tokens, depth)
    feats_up = move(own_feats, along_y(1))
    feats_down = move(own_feats, along_y(-1))
    cut = (tiles + 1) // 2 * TILE
    feats_far_a = move(feats_up[:cut], along_y(1))
    feats_far_b = move(feats_down[cut:], along_y(-1))

    gathered = lax.all_gather(own_pair, "seq", axis=0, tiled=True)
    attended, d_queries, stats = attend(places, queries, d_out, gathered)

    place_rows = jnp.pad(places.astype(F32), ((0, 0), (0, ROWS - places.shape[1])))
    news = stats.at[:, 2, :].set(place_rows)
    row_news = jnp.concatenate(
        [
            news,
            move(news, along_x(1)),
            move(news, along_x(-1)),
            move(news, along_x(2)),
        ],
        axis=0,
    )
    row_places = row_news[:, 2, :2].astype(jnp.int32)
    split = gathered.reshape(-1, SIDE, TILE, 2 * HEAD_DIM)
    grads = spread(row_places, column[None], row_text, row_news, split)

    own = lax.psum_scatter(grads, "seq", scatter_dimension=0, axis_index_groups=Y_GROUPS, tiled=True)[0]
    own = own.astype(BF16).transpose(1, 0, 2).reshape(HEAD_DIM // 2, -1)
    all_heads = lax.all_gather(own, "tp", axis=0, tiled=True)
    quarter = fold(line[None], all_heads, (own_feats, feats_up, feats_down, feats_far_a, feats_far_b))
    rows = lax.psum_scatter(quarter, "seq", scatter_dimension=0, axis_index_groups=X_GROUPS, tiled=True)[0]
    halves = rows.astype(BF16).reshape(2, HEAD_DIM // 2, depth)
    side = line % 2
    swap = [(y * SIDE + x, (y ^ 1) * SIDE + x) for y in range(SIDE) for x in range(SIDE)]
    mine = jnp.where(side == 0, halves[0], halves[1])
    other = move(jnp.where(side == 0, halves[1], halves[0]), swap)
    d_projection = jnp.concatenate(
        [jnp.where(side == 0, mine, other), jnp.where(side == 0, other, mine)], axis=0
    )
    return attended, d_queries, d_projection


def solution(mesh):
    return jax.shard_map(
        per_device,
        mesh=mesh,
        in_specs=(
            P(("dp", "seq"), "tp"),
            P(("dp", "seq"), "tp"),
            P(("dp", "seq"), None, "tp"),
            P("tp", None),
            P("tp", None),
            P(("dp", "seq"), None),
            P("dp"),
        ),
        out_specs=(P(("dp", "seq"), "tp"), P(("dp", "seq"), "tp"), P(("dp", "seq"), "tp")),
        check_vma=False,
    )
```

```python
import functools
import math

import jax
import jax.numpy as jnp
from jax import lax
from jax.experimental import pallas as pl
from jax.experimental.pallas import tpu as pltpu
from jax.sharding import PartitionSpec as P

QHEADS = 64
KVHEADS = 8
GROUP = QHEADS // KVHEADS
HEAD_DIM = 128
BLOCK = 64
ROWS = BLOCK * GROUP
TILE = 128
SIDE = 4
SCALE = HEAD_DIM ** -0.5
LOG2E = math.log2(math.e)
LN2 = math.log(2.0)
BF16 = jnp.bfloat16
F32 = jnp.float32
NT = (((1,), (1,)), ((), ()))
VMEM_LIMIT = 56 * 1024 * 1024


def matmul(a, b):
    return jnp.dot(a, b, preferred_element_type=F32)


def matmul_nt(a, b):
    return lax.dot_general(a, b, NT, preferred_element_type=F32)


def project_kernel(feats_ref, key_ref, value_ref, out_ref, turned_ref):
    @pl.when(pl.program_id(0) == 0)
    def _():
        turned_ref[...] = jnp.transpose(feats_ref[...])

    feats = turned_ref[...]
    for part, weight_ref in enumerate((key_ref, value_ref)):
        both = matmul(feats, weight_ref[...])
        lanes = slice(part * HEAD_DIM, (part + 1) * HEAD_DIM)
        out_ref[0, :, lanes] = both[:, :HEAD_DIM]
        out_ref[1, :, lanes] = both[:, HEAD_DIM:]


def project(feats, key_weight, value_weight):
    depth, tokens = feats.shape
    weight_spec = pl.BlockSpec((depth, 2 * HEAD_DIM), lambda i: (0, i))
    return pl.pallas_call(
        project_kernel,
        grid=(KVHEADS // 2,),
        in_specs=[pl.BlockSpec((depth, tokens), lambda i: (0, 0)), weight_spec, weight_spec],
        out_specs=pl.BlockSpec((2, tokens, 2 * HEAD_DIM), lambda i: (i, 0, 0)),
        out_shape=jax.ShapeDtypeStruct((KVHEADS, tokens, 2 * HEAD_DIM), F32),
        scratch_shapes=[pltpu.VMEM((tokens, depth), BF16)],
        compiler_params=pltpu.CompilerParams(vmem_limit_bytes=VMEM_LIMIT),
        name="project",
    )(feats, key_weight, value_weight)


def attend_kernel(heads, places_ref, query_ref, grad_ref, pair0_ref, pair1_ref, out_ref, dq_ref, stat_ref):
    pairs = (pair0_ref, pair1_ref)
    rows = heads * BLOCK
    lane = lax.broadcasted_iota(jnp.int32, (rows, HEAD_DIM), 1)
    for first in range(0, GROUP, heads):
        cols = [slice((first + g) * HEAD_DIM, (first + g + 1) * HEAD_DIM) for g in range(heads)]
        query = jnp.concatenate([query_ref[:, c] for c in cols], axis=0)
        grad = jnp.concatenate([grad_ref[:, c] for c in cols], axis=0)
        weights, maxima, totals, partials = [], [], [], []
        for pair in pairs:
            scores = matmul_nt(query, pair[0, :, :HEAD_DIM]) * (SCALE * LOG2E)
            row_max = jnp.max(scores, axis=1, keepdims=True)
            weight = jnp.exp2(scores - row_max)
            weights.append(weight)
            maxima.append(row_max)
            totals.append(jnp.sum(weight, axis=1, keepdims=True))
            partials.append(matmul(weight.astype(BF16), pair[0, :, HEAD_DIM:]).astype(BF16))
        top = jnp.maximum(maxima[0], maxima[1])
        factors = [jnp.exp2(m - top) for m in maxima]
        denominator = factors[0] * totals[0] + factors[1] * totals[1]
        numerator = factors[0] * partials[0].astype(F32) + factors[1] * partials[1].astype(F32)
        output = (numerator / denominator).astype(BF16)
        lse = top + jnp.log2(denominator)
        delta = jnp.sum(grad.astype(F32) * output.astype(F32), axis=1, keepdims=True)
        dq = []
        for pair, weight, factor in zip(pairs, weights, factors):
            prob_grad = matmul_nt(grad, pair[0, :, HEAD_DIM:])
            score_grad = weight * (factor / denominator) * (prob_grad - delta)
            part = matmul(score_grad.astype(BF16), pair[0, :, :HEAD_DIM]) * SCALE
            dq.append(part.astype(BF16).astype(F32))
        total = (dq[0] + dq[1]).astype(BF16)
        for g, c in enumerate(cols):
            out_ref[:, c] = output[g * BLOCK : (g + 1) * BLOCK]
            dq_ref[:, c] = total[g * BLOCK : (g + 1) * BLOCK]
        stats = jnp.transpose(jnp.where(lane == 0, lse, delta))
        stat_ref[0, :, first * BLOCK : (first + heads) * BLOCK] = stats[:8]


def attend(places, queries, d_out, pairs, heads=2):
    blocks = places.shape[0]
    tokens = pairs.shape[1]
    text = pl.BlockSpec((BLOCK, GROUP * HEAD_DIM), lambda c, p: (c, 0))

    def pair_spec(entry):
        return pl.BlockSpec((1, tokens, 2 * HEAD_DIM), lambda c, p: (p[c, entry], 0, 0))

    return pl.pallas_call(
        functools.partial(attend_kernel, heads),
        grid_spec=pltpu.PrefetchScalarGridSpec(
            num_scalar_prefetch=1,
            grid=(blocks,),
            in_specs=[text, text, pair_spec(0), pair_spec(1)],
            out_specs=[text, text, pl.BlockSpec((1, 8, ROWS), lambda c, p: (c, 0, 0))],
        ),
        out_shape=[
            jax.ShapeDtypeStruct(queries.shape, BF16),
            jax.ShapeDtypeStruct(queries.shape, BF16),
            jax.ShapeDtypeStruct((blocks, 8, ROWS), F32),
        ],
        compiler_params=pltpu.CompilerParams(vmem_limit_bytes=VMEM_LIMIT),
        name="attend",
    )(places, queries, d_out, pairs, pairs)


def spread_kernel(places_ref, column_ref, text_ref, stat_ref, pair_ref, out_ref):
    column = column_ref[0]
    blocks = text_ref.shape[0]
    tiles = pair_ref.shape[0]
    half = HEAD_DIM // 2

    def clear(m, carry):
        out_ref[:, m] = jnp.zeros((4, half, TILE), F32)
        return carry

    lax.fori_loop(0, tiles, clear, 0)

    def one(step, carry):
        block = step // 2
        place = places_ref[block, step % 2]
        line, spot = place // SIDE, place % SIDE
        begin = (7 * spot - column + SIDE - 1) // SIDE
        end = (7 * spot + 7 - column + SIDE - 1) // SIDE
        count = end - begin
        tile = line * 7 + begin

        def work(width):
            query = text_ref[block, 0]
            grad = text_ref[block, 1]
            lse = stat_ref[block, 0:1, :]
            delta = stat_ref[block, 1:2, :]
            pair = pair_ref[pl.ds(tile, width), 0].reshape(width * TILE, 2 * HEAD_DIM)
            scores = matmul(pair[:, :HEAD_DIM], query) * (SCALE * LOG2E)
            prob = jnp.exp2(scores - lse)
            prob_grad = matmul(pair[:, HEAD_DIM:], grad)
            score_grad = prob * (prob_grad - delta)
            d_value = matmul_nt(grad, prob.astype(BF16))
            d_key = matmul_nt(query, score_grad.astype(BF16))
            for i in range(width):
                lanes = slice(i * TILE, (i + 1) * TILE)
                out_ref[0, tile + i] += d_key[:half, lanes]
                out_ref[1, tile + i] += d_key[half:, lanes]
                out_ref[2, tile + i] += d_value[:half, lanes]
                out_ref[3, tile + i] += d_value[half:, lanes]

        @pl.when(count == 2)
        def _():
            work(2)

        @pl.when(count != 2)
        def _():
            work(1)

        return carry

    lax.fori_loop(0, 2 * blocks, one, 0)

    def scale(m, carry):
        out_ref[0, m] = out_ref[0, m] * SCALE
        out_ref[1, m] = out_ref[1, m] * SCALE
        return carry

    lax.fori_loop(0, tiles, scale, 0)


def spread(places, column, text, stats, pairs):
    blocks = text.shape[0]
    tiles = pairs.shape[0]
    half = HEAD_DIM // 2
    return pl.pallas_call(
        spread_kernel,
        grid_spec=pltpu.PrefetchScalarGridSpec(
            num_scalar_prefetch=2,
            grid=(1,),
            in_specs=[
                pl.BlockSpec(text.shape, lambda i, p, c: (0, 0, 0, 0)),
                pl.BlockSpec(stats.shape, lambda i, p, c: (0, 0, 0)),
                pl.BlockSpec((tiles, 1, TILE, 2 * HEAD_DIM), lambda i, p, c: (0, c[0], 0, 0)),
            ],
            out_specs=pl.BlockSpec((4, tiles, half, TILE), lambda i, p, c: (0, 0, 0, 0)),
        ),
        out_shape=jax.ShapeDtypeStruct((4, tiles, half, TILE), F32),
        compiler_params=pltpu.CompilerParams(vmem_limit_bytes=VMEM_LIMIT),
        name="spread",
    )(places, column, text, stats, pairs)


def fold_kernel(line_ref, grads_ref, own_ref, up_ref, down_ref, far_a_ref, far_b_ref, out_ref):
    line = line_ref[0]
    span = own_ref.shape[0]
    first = far_a_ref.shape[0]
    pieces = (
        (own_ref, 0, 0),
        (up_ref, SIDE - 1, 0),
        (down_ref, 1, 0),
        (far_a_ref, 2, 0),
        (far_b_ref, 2, first),
    )
    depth = own_ref.shape[1]
    half = HEAD_DIM // 2
    order = [head for x in range(SIDE) for head in (x, x + SIDE)]
    total = None
    for ref, shift, skip in pieces:
        begin = lax.rem(line + shift, SIDE) * span + skip
        count = ref.shape[0]
        grads = jnp.concatenate(
            [
                jnp.concatenate([grads_ref[head, begin + k] for head in order], axis=0)
                for k in range(count)
            ],
            axis=1,
        )
        feats = jnp.concatenate([ref[k] for k in range(count)], axis=1)
        part = matmul_nt(feats, grads)
        total = part if total is None else total + part
    for x in range(SIDE):
        out_ref[x] = total[:, x * HEAD_DIM : (x + 1) * HEAD_DIM]


def fold(line, grads, pieces):
    whole = [
        pl.BlockSpec(p.shape, functools.partial(lambda rank, i, l: (0,) * rank, p.ndim))
        for p in (grads, *pieces)
    ]
    shape = (SIDE, pieces[0].shape[1], HEAD_DIM)
    return pl.pallas_call(
        fold_kernel,
        grid_spec=pltpu.PrefetchScalarGridSpec(
            num_scalar_prefetch=1,
            grid=(1,),
            in_specs=whole,
            out_specs=pl.BlockSpec(shape, lambda i, l: (0, 0, 0)),
        ),
        out_shape=jax.ShapeDtypeStruct(shape, F32),
        compiler_params=pltpu.CompilerParams(vmem_limit_bytes=VMEM_LIMIT),
        name="fold",
    )(line, grads, *pieces)


def along_x(shift):
    return [(y * SIDE + x, y * SIDE + (x + shift) % SIDE) for y in range(SIDE) for x in range(SIDE)]


def along_y(shift):
    return [(y * SIDE + x, ((y + shift) % SIDE) * SIDE + x) for y in range(SIDE) for x in range(SIDE)]


X_GROUPS = [[y * SIDE + x for x in range(SIDE)] for y in range(SIDE)]
Y_GROUPS = [[y * SIDE + x for y in range(SIDE)] for x in range(SIDE)]


def move(array, perm):
    return lax.ppermute(array, "seq", perm)


def per_device(queries, d_out, image_feats, key_weight, value_weight, image_lists, owner):
    me = lax.axis_index("seq")
    line, column = me // SIDE, me % SIDE
    blocks = image_lists.shape[0]
    feats = image_feats[0].T
    depth, tokens = feats.shape
    tiles = tokens // TILE

    image_ids = lax.broadcasted_iota(jnp.int32, (*image_lists.shape, owner.shape[0]), 2)
    places = jnp.sum(jnp.where(image_lists[..., None] == image_ids, owner[None, None, :], 0), axis=-1)

    part = project(feats, key_weight, value_weight)
    queries_late, d_out_late, feats_late, places, part = lax.optimization_barrier(
        (queries, d_out, feats, places, part)
    )
    summed = lax.psum_scatter(part, "tp", scatter_dimension=0, tiled=True)

    def turned(array):
        return array.reshape(blocks, BLOCK, GROUP, HEAD_DIM).transpose(0, 3, 2, 1).reshape(blocks, HEAD_DIM, ROWS)

    text = jnp.stack([turned(queries_late), turned(d_out_late)], axis=1)
    text_left = move(text, along_x(1))
    text_right = move(text, along_x(-1))
    far_a = move(text_left[: blocks // 2], along_x(1))
    far_b = move(text_right[blocks // 2 :], along_x(-1))
    row_text = jnp.concatenate([text, text_left, text_right, far_a, far_b], axis=0)
    row_places = jnp.concatenate([places] + [move(places, along_x(shift)) for shift in (1, -1, 2)], axis=0)

    tiled = jnp.concatenate([feats_late, jnp.zeros((depth, TILE), BF16)], axis=1)
    buffer = jnp.zeros((tiles + 1, depth, TILE), BF16)
    for shift in range(SIDE):
        target = (column + shift) % SIDE
        first = (target + column) % SIDE
        slab = jnp.stack(
            [
                lax.dynamic_slice_in_dim(tiled, first * TILE, TILE, 1),
                lax.dynamic_slice_in_dim(tiled, (first + SIDE) * TILE, TILE, 1),
            ]
        )
        if shift:
            slab = move(slab, along_x(shift))
        source = (column - shift) % SIDE
        first = (column + source) % SIDE
        slot = (7 * source + first - column) // SIDE
        second = jnp.where(first + SIDE < tiles, slot + 1, tiles)
        buffer = lax.dynamic_update_slice_in_dim(buffer, slab[1:], second, 0)
        buffer = lax.dynamic_update_slice_in_dim(buffer, slab[:1], slot, 0)
    own_feats = buffer[:tiles]
    feats_up = move(own_feats, along_y(1))
    feats_down = move(own_feats, along_y(-1))
    cut = (tiles + 1) // 2
    feats_far_a = move(feats_up[:cut], along_y(1))
    feats_far_b = move(feats_down[cut:], along_y(-1))

    summed, row_text, row_places, *spread_feats = lax.optimization_barrier(
        (summed, row_text, row_places, own_feats, feats_up, feats_down, feats_far_a, feats_far_b)
    )
    own_pair = summed.astype(BF16)

    gathered = lax.all_gather(own_pair, "seq", axis=0, tiled=True)
    attended, d_queries, stats = attend(places, queries, d_out, gathered)

    row_stats = jnp.concatenate(
        [stats] + [move(stats, along_x(shift)) for shift in (1, -1, 2)],
        axis=0,
    )
    split = gathered.reshape(-1, SIDE, TILE, 2 * HEAD_DIM)
    grads = spread(row_places, column[None], row_text, row_stats, split)

    own = lax.psum_scatter(grads, "seq", scatter_dimension=0, axis_index_groups=Y_GROUPS, tiled=True)
    all_heads = lax.all_gather(own.astype(BF16), "tp", axis=0, tiled=True)
    quarter = fold(line[None], all_heads, spread_feats)
    rows = lax.psum_scatter(quarter, "seq", scatter_dimension=0, axis_index_groups=X_GROUPS, tiled=True)[0]
    rows = rows.astype(BF16)
    half = HEAD_DIM // 2
    side = line % 2
    swap = [(y * SIDE + x, (y ^ 1) * SIDE + x) for y in range(SIDE) for x in range(SIDE)]
    low, high = rows[:, :half], rows[:, half:]
    mine = jnp.where(side == 0, low, high)
    other = move(jnp.where(side == 0, high, low), swap)
    d_projection = jnp.concatenate(
        [jnp.where(side == 0, mine, other), jnp.where(side == 0, other, mine)], axis=1
    ).T
    return attended, d_queries, d_projection


def solution(mesh):
    return jax.shard_map(
        per_device,
        mesh=mesh,
        in_specs=(
            P(("dp", "seq"), "tp"),
            P(("dp", "seq"), "tp"),
            P(("dp", "seq"), None, "tp"),
            P("tp", None),
            P("tp", None),
            P(("dp", "seq"), None),
            P("dp"),
        ),
        out_specs=(P(("dp", "seq"), "tp"), P(("dp", "seq"), "tp"), P(("dp", "seq"), "tp")),
        check_vma=False,
    )
```

```python
import functools
import math

import jax
import jax.numpy as jnp
from jax import lax
from jax.experimental import pallas as pl
from jax.experimental.pallas import tpu as pltpu
from jax.sharding import PartitionSpec as P

QHEADS = 64
KVHEADS = 8
GROUP = QHEADS // KVHEADS
HEAD_DIM = 128
BLOCK = 64
ROWS = BLOCK * GROUP
TILE = 128
SIDE = 4
SCALE = HEAD_DIM ** -0.5
LOG2E = math.log2(math.e)
LN2 = math.log(2.0)
BF16 = jnp.bfloat16
F32 = jnp.float32
NT = (((1,), (1,)), ((), ()))
VMEM_LIMIT = 56 * 1024 * 1024


def matmul(a, b):
    return jnp.dot(a, b, preferred_element_type=F32)


def matmul_nt(a, b):
    return lax.dot_general(a, b, NT, preferred_element_type=F32)


def project_kernel(feats_ref, key_ref, value_ref, out_ref, turned_ref):
    @pl.when(pl.program_id(0) == 0)
    def _():
        turned_ref[...] = jnp.transpose(feats_ref[...])

    feats = turned_ref[...]
    for part, weight_ref in enumerate((key_ref, value_ref)):
        both = matmul(feats, weight_ref[...])
        lanes = slice(part * HEAD_DIM, (part + 1) * HEAD_DIM)
        out_ref[0, :, lanes] = both[:, :HEAD_DIM]
        out_ref[1, :, lanes] = both[:, HEAD_DIM:]


def project(feats, key_weight, value_weight):
    depth, tokens = feats.shape
    weight_spec = pl.BlockSpec((depth, 2 * HEAD_DIM), lambda i: (0, i))
    return pl.pallas_call(
        project_kernel,
        grid=(KVHEADS // 2,),
        in_specs=[pl.BlockSpec((depth, tokens), lambda i: (0, 0)), weight_spec, weight_spec],
        out_specs=pl.BlockSpec((2, tokens, 2 * HEAD_DIM), lambda i: (i, 0, 0)),
        out_shape=jax.ShapeDtypeStruct((KVHEADS, tokens, 2 * HEAD_DIM), F32),
        scratch_shapes=[pltpu.VMEM((tokens, depth), BF16)],
        compiler_params=pltpu.CompilerParams(vmem_limit_bytes=VMEM_LIMIT),
        name="project",
    )(feats, key_weight, value_weight)


def attend_kernel(
    places_ref, query_ref, grad_ref, key0_ref, key1_ref, value0_ref, value1_ref, out_ref, dq_ref, stat_ref
):
    pairs = ((key0_ref, value0_ref), (key1_ref, value1_ref))
    lane = lax.broadcasted_iota(jnp.int32, (ROWS, HEAD_DIM), 1)
    cols = [slice(g * HEAD_DIM, (g + 1) * HEAD_DIM) for g in range(GROUP)]
    query = jnp.concatenate([query_ref[:, c] for c in cols], axis=0)
    grad = jnp.concatenate([grad_ref[:, c] for c in cols], axis=0)
    weights, maxima, totals, partials = [], [], [], []
    for key_ref, value_ref in pairs:
        scores = matmul_nt(query, key_ref[0]) * (SCALE * LOG2E)
        row_max = jnp.max(scores, axis=1, keepdims=True)
        weight = jnp.exp2(scores - row_max)
        weights.append(weight)
        maxima.append(row_max)
        totals.append(jnp.sum(weight, axis=1, keepdims=True))
        partials.append(matmul(weight.astype(BF16), value_ref[0]).astype(BF16))
    top = jnp.maximum(maxima[0], maxima[1])
    factors = [jnp.exp2(m - top) for m in maxima]
    denominator = factors[0] * totals[0] + factors[1] * totals[1]
    numerator = factors[0] * partials[0].astype(F32) + factors[1] * partials[1].astype(F32)
    output = (numerator / denominator).astype(BF16)
    lse = top + jnp.log2(denominator)
    delta = jnp.sum(grad.astype(F32) * output.astype(F32), axis=1, keepdims=True)
    dq = []
    for (key_ref, value_ref), weight, factor in zip(pairs, weights, factors):
        prob_grad = matmul_nt(grad, value_ref[0])
        score_grad = weight * (factor / denominator) * (prob_grad - delta)
        part = matmul(score_grad.astype(BF16), key_ref[0]) * SCALE
        dq.append(part.astype(BF16).astype(F32))
    total = (dq[0] + dq[1]).astype(BF16)
    for g, c in enumerate(cols):
        out_ref[:, c] = output[g * BLOCK : (g + 1) * BLOCK]
        dq_ref[:, c] = total[g * BLOCK : (g + 1) * BLOCK]
    stat_ref[0] = jnp.transpose(jnp.where(lane == 0, lse, delta))[:8]


def attend(places, queries, d_out, keys, values):
    blocks = places.shape[0]
    tokens = keys.shape[1]
    text = pl.BlockSpec((BLOCK, GROUP * HEAD_DIM), lambda c, p: (c, 0))

    def image(entry):
        return pl.BlockSpec((1, tokens, HEAD_DIM), lambda c, p: (p[c, entry], 0, 0))

    return pl.pallas_call(
        attend_kernel,
        grid_spec=pltpu.PrefetchScalarGridSpec(
            num_scalar_prefetch=1,
            grid=(blocks,),
            in_specs=[text, text, image(0), image(1), image(0), image(1)],
            out_specs=[text, text, pl.BlockSpec((1, 8, ROWS), lambda c, p: (c, 0, 0))],
        ),
        out_shape=[
            jax.ShapeDtypeStruct(queries.shape, BF16),
            jax.ShapeDtypeStruct(queries.shape, BF16),
            jax.ShapeDtypeStruct((blocks, 8, ROWS), F32),
        ],
        compiler_params=pltpu.CompilerParams(vmem_limit_bytes=VMEM_LIMIT),
        name="attend",
    )(places, queries, d_out, keys, keys, values, values)


def spread_kernel(unroll, places_ref, column_ref, text_ref, stat_ref, key_ref, value_ref, out_ref):
    column = column_ref[0]
    blocks = text_ref.shape[0]
    tiles = key_ref.shape[0]
    half = HEAD_DIM // 2

    def clear(m, carry):
        out_ref[:, m] = jnp.zeros((4, half, TILE), F32)
        return carry

    lax.fori_loop(0, tiles, clear, 0)

    def one(block):
        query = text_ref[block, 0]
        grad = text_ref[block, 1]
        lse = stat_ref[block, 0:1, :]
        delta = stat_ref[block, 1:2, :]
        for entry in range(2):
            place = places_ref[block, entry]
            line, spot = place // SIDE, place % SIDE
            begin = (7 * spot - column + SIDE - 1) // SIDE
            end = (7 * spot + 7 - column + SIDE - 1) // SIDE
            first = line * 7 + begin
            second = jnp.minimum(first + 1, tiles - 1)
            shut = jnp.where(end - begin == 2, 0.0, 1e30).astype(F32)
            keys = jnp.concatenate([key_ref[first, 0], key_ref[second, 0]], axis=0)
            values = jnp.concatenate([value_ref[first, 0], value_ref[second, 0]], axis=0)
            scores = matmul(keys, query) * (SCALE * LOG2E)
            prob = jnp.concatenate(
                [jnp.exp2(scores[:TILE] - lse), jnp.exp2(scores[TILE:] - (lse + shut))], axis=0
            )
            prob_grad = matmul(values, grad)
            score_grad = prob * (prob_grad - delta)
            d_value = matmul_nt(grad, prob.astype(BF16))
            d_key = matmul_nt(query, score_grad.astype(BF16))
            for i, tile in enumerate((first, second)):
                lanes = slice(i * TILE, (i + 1) * TILE)
                out_ref[0, tile] += d_key[:half, lanes]
                out_ref[1, tile] += d_key[half:, lanes]
                out_ref[2, tile] += d_value[:half, lanes]
                out_ref[3, tile] += d_value[half:, lanes]

    def several(step, carry):
        for u in range(unroll):
            one(step * unroll + u)
        return carry

    lax.fori_loop(0, blocks // unroll, several, 0)

    def scale(m, carry):
        out_ref[0, m] = out_ref[0, m] * SCALE
        out_ref[1, m] = out_ref[1, m] * SCALE
        return carry

    lax.fori_loop(0, tiles, scale, 0)


def spread(places, column, text, stats, keys, values):
    tiles = keys.shape[0]
    half = HEAD_DIM // 2
    image = pl.BlockSpec((tiles, 1, TILE, HEAD_DIM), lambda i, p, c: (0, c[0], 0, 0))
    return pl.pallas_call(
        functools.partial(spread_kernel, SIDE),
        grid_spec=pltpu.PrefetchScalarGridSpec(
            num_scalar_prefetch=2,
            grid=(1,),
            in_specs=[
                pl.BlockSpec(text.shape, lambda i, p, c: (0, 0, 0, 0)),
                pl.BlockSpec(stats.shape, lambda i, p, c: (0, 0, 0)),
                image,
                image,
            ],
            out_specs=pl.BlockSpec((4, tiles, half, TILE), lambda i, p, c: (0, 0, 0, 0)),
        ),
        out_shape=jax.ShapeDtypeStruct((4, tiles, half, TILE), F32),
        compiler_params=pltpu.CompilerParams(vmem_limit_bytes=VMEM_LIMIT),
        name="spread",
    )(places, column, text, stats, keys, values)


def fold_kernel(line_ref, grads_ref, own_ref, up_ref, down_ref, far_a_ref, far_b_ref, out_ref):
    line = line_ref[0]
    span = own_ref.shape[0]
    first = far_a_ref.shape[0]
    pieces = (
        (own_ref, 0, 0),
        (up_ref, SIDE - 1, 0),
        (down_ref, 1, 0),
        (far_a_ref, 2, 0),
        (far_b_ref, 2, first),
    )
    depth = own_ref.shape[1]
    half = HEAD_DIM // 2
    order = [head for x in range(SIDE) for head in (x, x + SIDE)]
    total = None
    for ref, shift, skip in pieces:
        begin = lax.rem(line + shift, SIDE) * span + skip
        count = ref.shape[0]
        grads = jnp.concatenate(
            [
                jnp.concatenate([grads_ref[head, begin + k] for head in order], axis=0)
                for k in range(count)
            ],
            axis=1,
        )
        feats = jnp.concatenate([ref[k] for k in range(count)], axis=1)
        part = matmul_nt(feats, grads)
        total = part if total is None else total + part
    for x in range(SIDE):
        out_ref[x] = total[:, x * HEAD_DIM : (x + 1) * HEAD_DIM]


def fold(line, grads, pieces):
    whole = [
        pl.BlockSpec(p.shape, functools.partial(lambda rank, i, l: (0,) * rank, p.ndim))
        for p in (grads, *pieces)
    ]
    shape = (SIDE, pieces[0].shape[1], HEAD_DIM)
    return pl.pallas_call(
        fold_kernel,
        grid_spec=pltpu.PrefetchScalarGridSpec(
            num_scalar_prefetch=1,
            grid=(1,),
            in_specs=whole,
            out_specs=pl.BlockSpec(shape, lambda i, l: (0, 0, 0)),
        ),
        out_shape=jax.ShapeDtypeStruct(shape, F32),
        compiler_params=pltpu.CompilerParams(vmem_limit_bytes=VMEM_LIMIT),
        name="fold",
    )(line, grads, *pieces)


def along_x(shift):
    return [(y * SIDE + x, y * SIDE + (x + shift) % SIDE) for y in range(SIDE) for x in range(SIDE)]


def along_y(shift):
    return [(y * SIDE + x, ((y + shift) % SIDE) * SIDE + x) for y in range(SIDE) for x in range(SIDE)]


X_GROUPS = [[y * SIDE + x for x in range(SIDE)] for y in range(SIDE)]
Y_GROUPS = [[y * SIDE + x for y in range(SIDE)] for x in range(SIDE)]


def move(array, perm):
    return lax.ppermute(array, "seq", perm)


def around(block, along):
    half = block.shape[0] // 2
    left, right = move(block, along(1)), move(block, along(-1))
    far_low, far_high = move(left[:half], along(1)), move(right[half:], along(-1))
    return ((0, 0, block), (-1, 0, left), (1, 0, right), (2, 0, far_low), (2, half, far_high))


def around_halves(block, along):
    half = block.shape[0] // 2
    low, high = block[:half], block[half:]
    left_low, right_high = move(low, along(1)), move(high, along(-1))
    left_high, right_low = move(high, along(1)), move(low, along(-1))
    far_low, far_high = move(left_low, along(1)), move(right_high, along(-1))
    return (
        (0, 0, block),
        (-1, 0, left_low),
        (1, half, right_high),
        (-1, half, left_high),
        (1, 0, right_low),
        (2, 0, far_low),
        (2, half, far_high),
    )


def per_device(queries, d_out, image_feats, key_weight, value_weight, image_lists, owner):
    me = lax.axis_index("seq")
    line, column = me // SIDE, me % SIDE
    blocks = image_lists.shape[0]
    feats = image_feats[0].T
    depth, tokens = feats.shape
    tiles = tokens // TILE

    image_ids = lax.broadcasted_iota(jnp.int32, (*image_lists.shape, owner.shape[0]), 2)
    places = jnp.sum(jnp.where(image_lists[..., None] == image_ids, owner[None, None, :], 0), axis=-1)

    row_places = jnp.concatenate([places] + [move(places, along_x(shift)) for shift in (1, -1, 2)], axis=0)
    part = project(feats, key_weight, value_weight)
    queries_late, d_out_late, feats_late, row_places, part = lax.optimization_barrier(
        (queries, d_out, feats, row_places, part)
    )
    summed = lax.psum_scatter(part, "tp", scatter_dimension=0, tiled=True)

    def turned(array):
        return array.reshape(blocks, BLOCK, GROUP, HEAD_DIM).transpose(0, 3, 2, 1).reshape(blocks, HEAD_DIM, ROWS)

    text = jnp.stack([turned(queries_late), turned(d_out_late)], axis=1)
    text_left = move(text, along_x(1))
    text_right = move(text, along_x(-1))
    far_a = move(text_left[: blocks // 2], along_x(1))
    far_b = move(text_right[blocks // 2 :], along_x(-1))
    row_text = jnp.concatenate([text, text_left, text_right, far_a, far_b], axis=0)

    tiled = jnp.concatenate([feats_late, jnp.zeros((depth, TILE), BF16)], axis=1)
    buffer = jnp.zeros((tiles + 1, depth, TILE), BF16)
    for shift in range(SIDE):
        target = (column + shift) % SIDE
        first = (target + column) % SIDE
        slab = jnp.stack(
            [
                lax.dynamic_slice_in_dim(tiled, first * TILE, TILE, 1),
                lax.dynamic_slice_in_dim(tiled, (first + SIDE) * TILE, TILE, 1),
            ]
        )
        if shift:
            slab = move(slab, along_x(shift))
        source = (column - shift) % SIDE
        first = (column + source) % SIDE
        slot = (7 * source + first - column) // SIDE
        second = jnp.where(first + SIDE < tiles, slot + 1, tiles)
        buffer = lax.dynamic_update_slice_in_dim(buffer, slab[1:], second, 0)
        buffer = lax.dynamic_update_slice_in_dim(buffer, slab[:1], slot, 0)
    own_feats = buffer[:tiles]
    feats_up = move(own_feats, along_y(1))
    feats_down = move(own_feats, along_y(-1))
    summed, row_text, own_feats, feats_up, feats_down = lax.optimization_barrier(
        (summed, row_text, own_feats, feats_up, feats_down)
    )
    pair = summed[0].astype(BF16)
    keys, values = pair[:, :HEAD_DIM], pair[:, HEAD_DIM:]

    key_row = jnp.zeros((SIDE, tokens, HEAD_DIM), BF16)
    for shift, offset, piece in around(keys, along_x):
        key_row = lax.dynamic_update_slice(key_row, piece[None], ((column + shift) % SIDE, offset, 0))
    value_line = jnp.zeros((SIDE, tokens, HEAD_DIM), BF16)
    for shift, offset, piece in around(values, along_y):
        value_line = lax.dynamic_update_slice(value_line, piece[None], ((line + shift) % SIDE, offset, 0))
    keys = jnp.zeros((SIDE, SIDE, tokens, HEAD_DIM), BF16)
    for shift, offset, piece in around_halves(key_row, along_y):
        keys = lax.dynamic_update_slice(keys, piece[None], ((line + shift) % SIDE, offset, 0, 0))
    values = jnp.zeros((SIDE, SIDE, tokens, HEAD_DIM), BF16)
    for shift, offset, piece in around_halves(value_line, along_x):
        values = lax.dynamic_update_slice(values, piece[:, None], (offset, (column + shift) % SIDE, 0, 0))
    cut = (tiles + 1) // 2
    keys, values, up_cut, down_cut = lax.optimization_barrier((keys, values, feats_up[:cut], feats_down[cut:]))
    feats_far_a = move(up_cut, along_y(1))
    feats_far_b = move(down_cut, along_y(-1))

    images = (SIDE * SIDE, tokens, HEAD_DIM)
    attended, d_queries, stats = attend(places, queries, d_out, keys.reshape(images), values.reshape(images))

    row_stats = jnp.concatenate(
        [stats] + [move(stats, along_x(shift)) for shift in (1, -1, 2)],
        axis=0,
    )
    split = (-1, SIDE, TILE, HEAD_DIM)
    grads = spread(row_places, column[None], row_text, row_stats, keys.reshape(split), values.reshape(split))
    grads, feats_far_a, feats_far_b = lax.optimization_barrier((grads, feats_far_a, feats_far_b))
    spread_feats = (own_feats, feats_up, feats_down, feats_far_a, feats_far_b)

    own = lax.psum_scatter(grads, "seq", scatter_dimension=0, axis_index_groups=Y_GROUPS, tiled=True)
    all_heads = lax.all_gather(own.astype(BF16), "tp", axis=0, tiled=True)
    quarter = fold(line[None], all_heads, spread_feats)
    rows = lax.psum_scatter(quarter, "seq", scatter_dimension=0, axis_index_groups=X_GROUPS, tiled=True)[0]
    rows = rows.astype(BF16)
    half = HEAD_DIM // 2
    side = line % 2
    swap = [(y * SIDE + x, (y ^ 1) * SIDE + x) for y in range(SIDE) for x in range(SIDE)]
    low, high = rows[:, :half], rows[:, half:]
    mine = jnp.where(side == 0, low, high)
    other = move(jnp.where(side == 0, high, low), swap)
    d_projection = jnp.concatenate(
        [jnp.where(side == 0, mine, other), jnp.where(side == 0, other, mine)], axis=1
    ).T
    return attended, d_queries, d_projection


def solution(mesh):
    return jax.shard_map(
        per_device,
        mesh=mesh,
        in_specs=(
            P(("dp", "seq"), "tp"),
            P(("dp", "seq"), "tp"),
            P(("dp", "seq"), None, "tp"),
            P("tp", None),
            P("tp", None),
            P(("dp", "seq"), None),
            P("dp"),
        ),
        out_specs=(P(("dp", "seq"), "tp"), P(("dp", "seq"), "tp"), P(("dp", "seq"), "tp")),
        check_vma=False,
    )
```

```python
import functools
import math

import jax
import jax.numpy as jnp
from jax import lax
from jax.experimental import pallas as pl
from jax.experimental.pallas import tpu as pltpu
from jax.sharding import PartitionSpec as P

QHEADS = 64
KVHEADS = 8
GROUP = QHEADS // KVHEADS
HEAD_DIM = 128
BLOCK = 64
ROWS = BLOCK * GROUP
TILE = 128
SIDE = 4
SCALE = HEAD_DIM ** -0.5
LOG2E = math.log2(math.e)
LN2 = math.log(2.0)
BF16 = jnp.bfloat16
F32 = jnp.float32
NT = (((1,), (1,)), ((), ()))
VMEM_LIMIT = 56 * 1024 * 1024


def matmul(a, b):
    return jnp.dot(a, b, preferred_element_type=F32)


def matmul_nt(a, b):
    return lax.dot_general(a, b, NT, preferred_element_type=F32)


def project_kernel(feats_ref, key_ref, value_ref, out_ref, turned_ref):
    @pl.when(pl.program_id(0) == 0)
    def _():
        turned_ref[...] = jnp.transpose(feats_ref[...])

    feats = turned_ref[...]
    for part, weight_ref in enumerate((key_ref, value_ref)):
        both = matmul(feats, weight_ref[...])
        lanes = slice(part * HEAD_DIM, (part + 1) * HEAD_DIM)
        out_ref[0, :, lanes] = both[:, :HEAD_DIM]
        out_ref[1, :, lanes] = both[:, HEAD_DIM:]


def project(feats, key_weight, value_weight):
    depth, tokens = feats.shape
    weight_spec = pl.BlockSpec((depth, 2 * HEAD_DIM), lambda i: (0, i))
    return pl.pallas_call(
        project_kernel,
        grid=(KVHEADS // 2,),
        in_specs=[pl.BlockSpec((depth, tokens), lambda i: (0, 0)), weight_spec, weight_spec],
        out_specs=pl.BlockSpec((2, tokens, 2 * HEAD_DIM), lambda i: (i, 0, 0)),
        out_shape=jax.ShapeDtypeStruct((KVHEADS, tokens, 2 * HEAD_DIM), F32),
        scratch_shapes=[pltpu.VMEM((tokens, depth), BF16)],
        compiler_params=pltpu.CompilerParams(vmem_limit_bytes=VMEM_LIMIT),
        name="project",
    )(feats, key_weight, value_weight)


def attend_kernel(
    places_ref, query_ref, grad_ref, key0_ref, key1_ref, value0_ref, value1_ref, out_ref, dq_ref, stat_ref
):
    pairs = ((key0_ref, value0_ref), (key1_ref, value1_ref))
    lane = lax.broadcasted_iota(jnp.int32, (ROWS, HEAD_DIM), 1)
    cols = [slice(g * HEAD_DIM, (g + 1) * HEAD_DIM) for g in range(GROUP)]
    query = jnp.concatenate([query_ref[:, c] for c in cols], axis=0)
    grad = jnp.concatenate([grad_ref[:, c] for c in cols], axis=0)
    weights, maxima, totals, partials = [], [], [], []
    for key_ref, value_ref in pairs:
        scores = matmul_nt(query, key_ref[0]) * (SCALE * LOG2E)
        row_max = jnp.max(scores, axis=1, keepdims=True)
        weight = jnp.exp2(scores - row_max)
        weights.append(weight)
        maxima.append(row_max)
        totals.append(jnp.sum(weight, axis=1, keepdims=True))
        partials.append(matmul(weight.astype(BF16), value_ref[0]).astype(BF16))
    top = jnp.maximum(maxima[0], maxima[1])
    factors = [jnp.exp2(m - top) for m in maxima]
    denominator = factors[0] * totals[0] + factors[1] * totals[1]
    numerator = factors[0] * partials[0].astype(F32) + factors[1] * partials[1].astype(F32)
    output = (numerator / denominator).astype(BF16)
    lse = top + jnp.log2(denominator)
    delta = jnp.sum(grad.astype(F32) * output.astype(F32), axis=1, keepdims=True)
    dq = []
    for (key_ref, value_ref), weight, factor in zip(pairs, weights, factors):
        prob_grad = matmul_nt(grad, value_ref[0])
        score_grad = weight * (factor / denominator) * (prob_grad - delta)
        part = matmul(score_grad.astype(BF16), key_ref[0]) * SCALE
        dq.append(part.astype(BF16).astype(F32))
    total = (dq[0] + dq[1]).astype(BF16)
    for g, c in enumerate(cols):
        out_ref[:, c] = output[g * BLOCK : (g + 1) * BLOCK]
        dq_ref[:, c] = total[g * BLOCK : (g + 1) * BLOCK]
    stat_ref[0, 0:2] = jnp.transpose(jnp.where(lane == 0, lse, delta))[:2]
    for entry in range(2):
        place = places_ref[pl.program_id(0), entry].astype(F32)
        stat_ref[0, 2 + entry : 3 + entry] = jnp.full((1, ROWS), place, F32)


def attend(places, queries, d_out, keys, values):
    blocks = places.shape[0]
    tokens = keys.shape[1]
    text = pl.BlockSpec((BLOCK, GROUP * HEAD_DIM), lambda c, p: (c, 0))

    def image(entry):
        return pl.BlockSpec((1, tokens, HEAD_DIM), lambda c, p: (p[c, entry], 0, 0))

    return pl.pallas_call(
        attend_kernel,
        grid_spec=pltpu.PrefetchScalarGridSpec(
            num_scalar_prefetch=1,
            grid=(blocks,),
            in_specs=[text, text, image(0), image(1), image(0), image(1)],
            out_specs=[text, text, pl.BlockSpec((1, 4, ROWS), lambda c, p: (c, 0, 0))],
        ),
        out_shape=[
            jax.ShapeDtypeStruct(queries.shape, BF16),
            jax.ShapeDtypeStruct(queries.shape, BF16),
            jax.ShapeDtypeStruct((blocks, 4, ROWS), F32),
        ],
        compiler_params=pltpu.CompilerParams(vmem_limit_bytes=VMEM_LIMIT),
        name="attend",
    )(places, queries, d_out, keys, keys, values, values)


def spread_kernel(unroll, places_ref, column_ref, text_ref, stat_ref, key_ref, value_ref, out_ref):
    column = column_ref[0]
    blocks = text_ref.shape[0]
    tiles = key_ref.shape[0]
    half = HEAD_DIM // 2

    def clear(m, carry):
        out_ref[:, m] = jnp.zeros((4, half, TILE), F32)
        return carry

    lax.fori_loop(0, tiles, clear, 0)

    def one(block):
        query = text_ref[block, 0]
        grad = text_ref[block, 1]
        lse = stat_ref[block, 0:1, :]
        delta = stat_ref[block, 1:2, :]
        for entry in range(2):
            place = places_ref[block, entry]
            line, spot = place // SIDE, place % SIDE
            begin = (7 * spot - column + SIDE - 1) // SIDE
            end = (7 * spot + 7 - column + SIDE - 1) // SIDE
            first = line * 7 + begin
            second = jnp.minimum(first + 1, tiles - 1)
            shut = jnp.where(end - begin == 2, 0.0, 1e30).astype(F32)
            keys = jnp.concatenate([key_ref[first, 0], key_ref[second, 0]], axis=0)
            values = jnp.concatenate([value_ref[first, 0], value_ref[second, 0]], axis=0)
            scores = matmul(keys, query) * (SCALE * LOG2E)
            prob = jnp.concatenate(
                [jnp.exp2(scores[:TILE] - lse), jnp.exp2(scores[TILE:] - (lse + shut))], axis=0
            )
            prob_grad = matmul(values, grad)
            score_grad = prob * (prob_grad - delta)
            d_value = matmul_nt(grad, prob.astype(BF16))
            d_key = matmul_nt(query, score_grad.astype(BF16))
            for i, tile in enumerate((first, second)):
                lanes = slice(i * TILE, (i + 1) * TILE)
                out_ref[0, tile] += d_key[:half, lanes]
                out_ref[1, tile] += d_key[half:, lanes]
                out_ref[2, tile] += d_value[:half, lanes]
                out_ref[3, tile] += d_value[half:, lanes]

    def several(step, carry):
        for u in range(unroll):
            one(step * unroll + u)
        return carry

    lax.fori_loop(0, blocks // unroll, several, 0)

    def scale(m, carry):
        out_ref[0, m] = out_ref[0, m] * SCALE
        out_ref[1, m] = out_ref[1, m] * SCALE
        return carry

    lax.fori_loop(0, tiles, scale, 0)


def spread(places, column, text, stats, keys, values):
    tiles = keys.shape[0]
    half = HEAD_DIM // 2
    image = pl.BlockSpec((tiles, 1, TILE, HEAD_DIM), lambda i, p, c: (0, c[0], 0, 0))
    return pl.pallas_call(
        functools.partial(spread_kernel, SIDE),
        grid_spec=pltpu.PrefetchScalarGridSpec(
            num_scalar_prefetch=2,
            grid=(1,),
            in_specs=[
                pl.BlockSpec(text.shape, lambda i, p, c: (0, 0, 0, 0)),
                pl.BlockSpec(stats.shape, lambda i, p, c: (0, 0, 0)),
                image,
                image,
            ],
            out_specs=pl.BlockSpec((4, tiles, half, TILE), lambda i, p, c: (0, 0, 0, 0)),
        ),
        out_shape=jax.ShapeDtypeStruct((4, tiles, half, TILE), F32),
        compiler_params=pltpu.CompilerParams(vmem_limit_bytes=VMEM_LIMIT),
        name="spread",
    )(places, column, text, stats, keys, values)


def fold_kernel(line_ref, grads_ref, own_ref, up_ref, down_ref, far_a_ref, far_b_ref, out_ref):
    line = line_ref[0]
    span = own_ref.shape[0]
    first = far_a_ref.shape[0]
    pieces = (
        (own_ref, 0, 0),
        (up_ref, SIDE - 1, 0),
        (down_ref, 1, 0),
        (far_a_ref, 2, 0),
        (far_b_ref, 2, first),
    )
    depth = own_ref.shape[1]
    half = HEAD_DIM // 2
    order = [head for x in range(SIDE) for head in (x, x + SIDE)]
    total = None
    for ref, shift, skip in pieces:
        begin = lax.rem(line + shift, SIDE) * span + skip
        count = ref.shape[0]
        grads = jnp.concatenate(
            [
                jnp.concatenate([grads_ref[head, begin + k] for head in order], axis=0)
                for k in range(count)
            ],
            axis=1,
        )
        feats = jnp.concatenate([ref[k] for k in range(count)], axis=1)
        part = matmul_nt(feats, grads)
        total = part if total is None else total + part
    for x in range(SIDE):
        out_ref[x] = total[:, x * HEAD_DIM : (x + 1) * HEAD_DIM]


def fold(line, grads, pieces):
    whole = [
        pl.BlockSpec(p.shape, functools.partial(lambda rank, i, l: (0,) * rank, p.ndim))
        for p in (grads, *pieces)
    ]
    shape = (SIDE, pieces[0].shape[1], HEAD_DIM)
    return pl.pallas_call(
        fold_kernel,
        grid_spec=pltpu.PrefetchScalarGridSpec(
            num_scalar_prefetch=1,
            grid=(1,),
            in_specs=whole,
            out_specs=pl.BlockSpec(shape, lambda i, l: (0, 0, 0)),
        ),
        out_shape=jax.ShapeDtypeStruct(shape, F32),
        compiler_params=pltpu.CompilerParams(vmem_limit_bytes=VMEM_LIMIT),
        name="fold",
    )(line, grads, *pieces)


def along_x(shift):
    return [(y * SIDE + x, y * SIDE + (x + shift) % SIDE) for y in range(SIDE) for x in range(SIDE)]


def along_y(shift):
    return [(y * SIDE + x, ((y + shift) % SIDE) * SIDE + x) for y in range(SIDE) for x in range(SIDE)]


X_GROUPS = [[y * SIDE + x for x in range(SIDE)] for y in range(SIDE)]
Y_GROUPS = [[y * SIDE + x for y in range(SIDE)] for x in range(SIDE)]


def move(array, perm):
    return lax.ppermute(array, "seq", perm)


def around(block, along):
    half = block.shape[0] // 2
    left, right = move(block, along(1)), move(block, along(-1))
    far_low, far_high = move(left[:half], along(1)), move(right[half:], along(-1))
    return ((0, 0, block), (-1, 0, left), (1, 0, right), (2, 0, far_low), (2, half, far_high))


def per_device(queries, d_out, image_feats, key_weight, value_weight, image_lists, owner):
    me = lax.axis_index("seq")
    line, column = me // SIDE, me % SIDE
    blocks = image_lists.shape[0]
    feats = image_feats[0].T
    depth, tokens = feats.shape
    tiles = tokens // TILE

    image_ids = lax.broadcasted_iota(jnp.int32, (*image_lists.shape, owner.shape[0]), 2)
    places = jnp.sum(jnp.where(image_lists[..., None] == image_ids, owner[None, None, :], 0), axis=-1)

    part = project(feats, key_weight, value_weight)
    queries_late, d_out_late, feats_late, part = lax.optimization_barrier((queries, d_out, feats, part))
    summed = lax.psum_scatter(part, "tp", scatter_dimension=0, tiled=True)

    def turned(array):
        return array.reshape(blocks, BLOCK, GROUP, HEAD_DIM).transpose(0, 3, 2, 1).reshape(blocks, HEAD_DIM, ROWS)

    text = jnp.stack([turned(queries_late), turned(d_out_late)], axis=1)
    text_left = move(text, along_x(1))
    text_right = move(text, along_x(-1))
    far_a = move(text_left[: blocks // 2], along_x(1))
    far_b = move(text_right[blocks // 2 :], along_x(-1))
    row_text = jnp.concatenate([text, text_left, text_right, far_a, far_b], axis=0)

    tiled = jnp.concatenate([feats_late, jnp.zeros((depth, TILE), BF16)], axis=1)
    buffer = jnp.zeros((tiles + 1, depth, TILE), BF16)
    for shift in range(SIDE):
        target = (column + shift) % SIDE
        first = (target + column) % SIDE
        slab = jnp.stack(
            [
                lax.dynamic_slice_in_dim(tiled, first * TILE, TILE, 1),
                lax.dynamic_slice_in_dim(tiled, (first + SIDE) * TILE, TILE, 1),
            ]
        )
        if shift:
            slab = move(slab, along_x(shift))
        source = (column - shift) % SIDE
        first = (column + source) % SIDE
        slot = (7 * source + first - column) // SIDE
        second = jnp.where(first + SIDE < tiles, slot + 1, tiles)
        buffer = lax.dynamic_update_slice_in_dim(buffer, slab[1:], second, 0)
        buffer = lax.dynamic_update_slice_in_dim(buffer, slab[:1], slot, 0)
    own_feats = buffer[:tiles]
    feats_up = move(own_feats, along_y(1))
    feats_down = move(own_feats, along_y(-1))
    summed, row_text, own_feats, feats_up, feats_down = lax.optimization_barrier(
        (summed, row_text, own_feats, feats_up, feats_down)
    )
    pair = summed[0].astype(BF16)
    keys, values = pair[:, :HEAD_DIM], pair[:, HEAD_DIM:]

    key_row = jnp.zeros((SIDE, tokens, HEAD_DIM), BF16)
    for shift, offset, piece in around(keys, along_x):
        key_row = lax.dynamic_update_slice(key_row, piece[None], ((column + shift) % SIDE, offset, 0))
    value_line = jnp.zeros((SIDE, tokens, HEAD_DIM), BF16)
    for shift, offset, piece in around(values, along_y):
        value_line = lax.dynamic_update_slice(value_line, piece[None], ((line + shift) % SIDE, offset, 0))
    keys = jnp.zeros((SIDE, SIDE, tokens, HEAD_DIM), BF16)
    for shift, offset, piece in around(key_row, along_y):
        keys = lax.dynamic_update_slice(keys, piece[None], ((line + shift) % SIDE, offset, 0, 0))
    values = jnp.zeros((SIDE, SIDE, tokens, HEAD_DIM), BF16)
    for shift, offset, piece in around(value_line, along_x):
        values = lax.dynamic_update_slice(values, piece[:, None], (offset, (column + shift) % SIDE, 0, 0))
    cut = (tiles + 1) // 2
    keys, values, up_cut, down_cut = lax.optimization_barrier((keys, values, feats_up[:cut], feats_down[cut:]))
    feats_far_a = move(up_cut, along_y(1))
    feats_far_b = move(down_cut, along_y(-1))

    images = (SIDE * SIDE, tokens, HEAD_DIM)
    attended, d_queries, stats = attend(places, queries, d_out, keys.reshape(images), values.reshape(images))

    row_stats = jnp.concatenate(
        [stats] + [move(stats, along_x(shift)) for shift in (1, -1, 2)],
        axis=0,
    )
    row_places = row_stats[:, 2:, 0].astype(jnp.int32)
    split = (-1, SIDE, TILE, HEAD_DIM)
    grads = spread(row_places, column[None], row_text, row_stats, keys.reshape(split), values.reshape(split))
    grads, feats_far_a, feats_far_b = lax.optimization_barrier((grads, feats_far_a, feats_far_b))
    spread_feats = (own_feats, feats_up, feats_down, feats_far_a, feats_far_b)

    own = lax.psum_scatter(grads, "seq", scatter_dimension=0, axis_index_groups=Y_GROUPS, tiled=True)
    all_heads = lax.all_gather(own.astype(BF16), "tp", axis=0, tiled=True)
    quarter = fold(line[None], all_heads, spread_feats)
    rows = lax.psum_scatter(quarter, "seq", scatter_dimension=0, axis_index_groups=X_GROUPS, tiled=True)[0]
    rows = rows.astype(BF16)
    half = HEAD_DIM // 2
    side = line % 2
    swap = [(y * SIDE + x, (y ^ 1) * SIDE + x) for y in range(SIDE) for x in range(SIDE)]
    low, high = rows[:, :half], rows[:, half:]
    mine = jnp.where(side == 0, low, high)
    other = move(jnp.where(side == 0, high, low), swap)
    d_projection = jnp.concatenate(
        [jnp.where(side == 0, mine, other), jnp.where(side == 0, other, mine)], axis=1
    ).T
    return attended, d_queries, d_projection


def solution(mesh):
    return jax.shard_map(
        per_device,
        mesh=mesh,
        in_specs=(
            P(("dp", "seq"), "tp"),
            P(("dp", "seq"), "tp"),
            P(("dp", "seq"), None, "tp"),
            P("tp", None),
            P("tp", None),
            P(("dp", "seq"), None),
            P("dp"),
        ),
        out_specs=(P(("dp", "seq"), "tp"), P(("dp", "seq"), "tp"), P(("dp", "seq"), "tp")),
        check_vma=False,
    )
```

```python
import functools
import math

import jax
import jax.numpy as jnp
from jax import lax
from jax.experimental import pallas as pl
from jax.experimental.pallas import tpu as pltpu
from jax.sharding import PartitionSpec as P

QHEADS = 64
KVHEADS = 8
GROUP = QHEADS // KVHEADS
HEAD_DIM = 128
BLOCK = 64
ROWS = BLOCK * GROUP
TILE = 128
SIDE = 4
SCALE = HEAD_DIM ** -0.5
LOG2E = math.log2(math.e)
LN2 = math.log(2.0)
BF16 = jnp.bfloat16
F32 = jnp.float32
NT = (((1,), (1,)), ((), ()))
VMEM_LIMIT = 56 * 1024 * 1024


def matmul(a, b):
    return jnp.dot(a, b, preferred_element_type=F32)


def matmul_nt(a, b):
    return lax.dot_general(a, b, NT, preferred_element_type=F32)


def project_kernel(feats_ref, key_ref, value_ref, out_ref, turned_ref):
    @pl.when(pl.program_id(0) == 0)
    def _():
        turned_ref[...] = jnp.transpose(feats_ref[...])

    feats = turned_ref[...]
    for part, weight_ref in enumerate((key_ref, value_ref)):
        both = matmul(feats, weight_ref[...])
        lanes = slice(part * HEAD_DIM, (part + 1) * HEAD_DIM)
        out_ref[0, :, lanes] = both[:, :HEAD_DIM]
        out_ref[1, :, lanes] = both[:, HEAD_DIM:]


def project(feats, key_weight, value_weight):
    depth, tokens = feats.shape
    weight_spec = pl.BlockSpec((depth, 2 * HEAD_DIM), lambda i: (0, i))
    return pl.pallas_call(
        project_kernel,
        grid=(KVHEADS // 2,),
        in_specs=[pl.BlockSpec((depth, tokens), lambda i: (0, 0)), weight_spec, weight_spec],
        out_specs=pl.BlockSpec((2, tokens, 2 * HEAD_DIM), lambda i: (i, 0, 0)),
        out_shape=jax.ShapeDtypeStruct((KVHEADS, tokens, 2 * HEAD_DIM), F32),
        scratch_shapes=[pltpu.VMEM((tokens, depth), BF16)],
        compiler_params=pltpu.CompilerParams(vmem_limit_bytes=VMEM_LIMIT),
        name="project",
    )(feats, key_weight, value_weight)


def attend_kernel(
    places_ref, query_ref, grad_ref, key0_ref, key1_ref, value0_ref, value1_ref, out_ref, dq_ref, stat_ref
):
    pairs = ((key0_ref, value0_ref), (key1_ref, value1_ref))
    lane = lax.broadcasted_iota(jnp.int32, (ROWS, HEAD_DIM), 1)
    cols = [slice(g * HEAD_DIM, (g + 1) * HEAD_DIM) for g in range(GROUP)]
    query = jnp.concatenate([query_ref[:, c] for c in cols], axis=0)
    grad = jnp.concatenate([grad_ref[:, c] for c in cols], axis=0)
    weights, maxima, totals, partials = [], [], [], []
    for key_ref, value_ref in pairs:
        scores = matmul_nt(query, key_ref[0]) * (SCALE * LOG2E)
        row_max = jnp.max(scores, axis=1, keepdims=True)
        weight = jnp.exp2(scores - row_max)
        weights.append(weight)
        maxima.append(row_max)
        totals.append(jnp.sum(weight, axis=1, keepdims=True))
        partials.append(matmul(weight.astype(BF16), value_ref[0]).astype(BF16))
    top = jnp.maximum(maxima[0], maxima[1])
    factors = [jnp.exp2(m - top) for m in maxima]
    denominator = factors[0] * totals[0] + factors[1] * totals[1]
    numerator = factors[0] * partials[0].astype(F32) + factors[1] * partials[1].astype(F32)
    output = (numerator / denominator).astype(BF16)
    lse = top + jnp.log2(denominator)
    delta = jnp.sum(grad.astype(F32) * output.astype(F32), axis=1, keepdims=True)
    dq = []
    for (key_ref, value_ref), weight, factor in zip(pairs, weights, factors):
        prob_grad = matmul_nt(grad, value_ref[0])
        score_grad = weight * (factor / denominator) * (prob_grad - delta)
        part = matmul(score_grad.astype(BF16), key_ref[0]) * SCALE
        dq.append(part.astype(BF16).astype(F32))
    total = (dq[0] + dq[1]).astype(BF16)
    for g, c in enumerate(cols):
        out_ref[:, c] = output[g * BLOCK : (g + 1) * BLOCK]
        dq_ref[:, c] = total[g * BLOCK : (g + 1) * BLOCK]
    stat_ref[0, 0:2] = jnp.transpose(jnp.where(lane == 0, lse, delta))[:2]
    for entry in range(2):
        place = places_ref[pl.program_id(0), entry].astype(F32)
        stat_ref[0, 2 + entry : 3 + entry] = jnp.full((1, ROWS), place, F32)


def attend(places, queries, d_out, keys, values):
    blocks = places.shape[0]
    tokens = keys.shape[1]
    text = pl.BlockSpec((BLOCK, GROUP * HEAD_DIM), lambda c, p: (c, 0))

    def image(entry):
        return pl.BlockSpec((1, tokens, HEAD_DIM), lambda c, p: (p[c, entry], 0, 0))

    return pl.pallas_call(
        attend_kernel,
        grid_spec=pltpu.PrefetchScalarGridSpec(
            num_scalar_prefetch=1,
            grid=(blocks,),
            in_specs=[text, text, image(0), image(1), image(0), image(1)],
            out_specs=[text, text, pl.BlockSpec((1, 4, ROWS), lambda c, p: (c, 0, 0))],
        ),
        out_shape=[
            jax.ShapeDtypeStruct(queries.shape, BF16),
            jax.ShapeDtypeStruct(queries.shape, BF16),
            jax.ShapeDtypeStruct((blocks, 4, ROWS), F32),
        ],
        compiler_params=pltpu.CompilerParams(vmem_limit_bytes=VMEM_LIMIT),
        name="attend",
    )(places, queries, d_out, keys, keys, values, values)


def spread_kernel(unroll, places_ref, column_ref, text_ref, stat_ref, key_ref, value_ref, out_ref):
    column = column_ref[0]
    blocks = text_ref.shape[0]
    tiles = key_ref.shape[0]
    half = HEAD_DIM // 2

    def clear(m, carry):
        out_ref[:, m] = jnp.zeros((4, half, TILE), F32)
        return carry

    lax.fori_loop(0, tiles, clear, 0)

    def one(block):
        query = text_ref[block, 0]
        grad = text_ref[block, 1]
        lse = stat_ref[block, 0:1, :]
        delta = stat_ref[block, 1:2, :]
        for entry in range(2):
            place = places_ref[block, entry]
            line, spot = place // SIDE, place % SIDE
            begin = (7 * spot - column + SIDE - 1) // SIDE
            end = (7 * spot + 7 - column + SIDE - 1) // SIDE
            first = line * 7 + begin
            second = jnp.minimum(first + 1, tiles - 1)
            shut = jnp.where(end - begin == 2, 0.0, 1e30).astype(F32)
            keys = jnp.concatenate([key_ref[first, 0], key_ref[second, 0]], axis=0)
            values = jnp.concatenate([value_ref[first, 0], value_ref[second, 0]], axis=0)
            scores = matmul(keys, query) * (SCALE * LOG2E)
            prob = jnp.concatenate(
                [jnp.exp2(scores[:TILE] - lse), jnp.exp2(scores[TILE:] - (lse + shut))], axis=0
            )
            prob_grad = matmul(values, grad)
            score_grad = prob * (prob_grad - delta)
            d_value = matmul_nt(grad, prob.astype(BF16))
            d_key = matmul_nt(query, score_grad.astype(BF16))
            for i, tile in enumerate((first, second)):
                lanes = slice(i * TILE, (i + 1) * TILE)
                out_ref[0, tile] += d_key[:half, lanes]
                out_ref[1, tile] += d_key[half:, lanes]
                out_ref[2, tile] += d_value[:half, lanes]
                out_ref[3, tile] += d_value[half:, lanes]

    def several(step, carry):
        for u in range(unroll):
            one(step * unroll + u)
        return carry

    lax.fori_loop(0, blocks // unroll, several, 0)

    def scale(m, carry):
        out_ref[0, m] = out_ref[0, m] * SCALE
        out_ref[1, m] = out_ref[1, m] * SCALE
        return carry

    lax.fori_loop(0, tiles, scale, 0)


def spread(places, column, text, stats, keys, values):
    tiles = keys.shape[0]
    half = HEAD_DIM // 2
    image = pl.BlockSpec((tiles, 1, TILE, HEAD_DIM), lambda i, p, c: (0, c[0], 0, 0))
    return pl.pallas_call(
        functools.partial(spread_kernel, SIDE),
        grid_spec=pltpu.PrefetchScalarGridSpec(
            num_scalar_prefetch=2,
            grid=(1,),
            in_specs=[
                pl.BlockSpec(text.shape, lambda i, p, c: (0, 0, 0, 0)),
                pl.BlockSpec(stats.shape, lambda i, p, c: (0, 0, 0)),
                image,
                image,
            ],
            out_specs=pl.BlockSpec((4, tiles, half, TILE), lambda i, p, c: (0, 0, 0, 0)),
        ),
        out_shape=jax.ShapeDtypeStruct((4, tiles, half, TILE), F32),
        compiler_params=pltpu.CompilerParams(vmem_limit_bytes=VMEM_LIMIT),
        name="spread",
    )(places, column, text, stats, keys, values)


def fold_kernel(line_ref, grads_ref, own_ref, up_ref, down_ref, far_a_ref, far_b_ref, out_ref):
    line = line_ref[0]
    span = own_ref.shape[0]
    first = far_a_ref.shape[0]
    pieces = (
        (own_ref, 0, 0),
        (up_ref, SIDE - 1, 0),
        (down_ref, 1, 0),
        (far_a_ref, 2, 0),
        (far_b_ref, 2, first),
    )
    depth = own_ref.shape[1]
    half = HEAD_DIM // 2
    order = [head for x in range(SIDE) for head in (x, x + SIDE)]
    total = None
    for ref, shift, skip in pieces:
        begin = lax.rem(line + shift, SIDE) * span + skip
        count = ref.shape[0]
        grads = jnp.concatenate(
            [
                jnp.concatenate([grads_ref[head, begin + k] for head in order], axis=0)
                for k in range(count)
            ],
            axis=1,
        )
        feats = jnp.concatenate([ref[k] for k in range(count)], axis=1)
        part = matmul_nt(feats, grads)
        total = part if total is None else total + part
    for x in range(SIDE):
        out_ref[x] = total[:, x * HEAD_DIM : (x + 1) * HEAD_DIM]


def fold(line, grads, pieces):
    whole = [
        pl.BlockSpec(p.shape, functools.partial(lambda rank, i, l: (0,) * rank, p.ndim))
        for p in (grads, *pieces)
    ]
    shape = (SIDE, pieces[0].shape[1], HEAD_DIM)
    return pl.pallas_call(
        fold_kernel,
        grid_spec=pltpu.PrefetchScalarGridSpec(
            num_scalar_prefetch=1,
            grid=(1,),
            in_specs=whole,
            out_specs=pl.BlockSpec(shape, lambda i, l: (0, 0, 0)),
        ),
        out_shape=jax.ShapeDtypeStruct(shape, F32),
        compiler_params=pltpu.CompilerParams(vmem_limit_bytes=VMEM_LIMIT),
        name="fold",
    )(line, grads, *pieces)


def along_x(shift):
    return [(y * SIDE + x, y * SIDE + (x + shift) % SIDE) for y in range(SIDE) for x in range(SIDE)]


def along_y(shift):
    return [(y * SIDE + x, ((y + shift) % SIDE) * SIDE + x) for y in range(SIDE) for x in range(SIDE)]


X_GROUPS = [[y * SIDE + x for x in range(SIDE)] for y in range(SIDE)]
Y_GROUPS = [[y * SIDE + x for y in range(SIDE)] for x in range(SIDE)]


def move(array, perm):
    return lax.ppermute(array, "seq", perm)


def around(block, along):
    half = block.shape[0] // 2
    left, right = move(block, along(1)), move(block, along(-1))
    far_low, far_high = move(left[:half], along(1)), move(right[half:], along(-1))
    return ((0, 0, block), (-1, 0, left), (1, 0, right), (2, 0, far_low), (2, half, far_high))


def ring_sum(parts, along, index):
    half = parts.shape[1] // 2

    def part(shift, high):
        start = (((index + shift) % SIDE, half * high) + (0,) * (parts.ndim - 2))
        return lax.dynamic_slice(parts, start, (1, half, *parts.shape[2:]))[0]

    far_low, far_high = move(part(2, 0), along(1)), move(part(2, 1), along(-1))
    left_high, right_low = move(part(1, 1), along(1)), move(part(-1, 0), along(-1))
    left_low = move(part(1, 0) + far_low, along(1))
    right_high = move(part(-1, 1) + far_high, along(-1))
    return part(0, 0) + right_low + left_low, part(0, 1) + left_high + right_high


def per_device(queries, d_out, image_feats, key_weight, value_weight, image_lists, owner):
    me = lax.axis_index("seq")
    line, column = me // SIDE, me % SIDE
    blocks = image_lists.shape[0]
    feats = image_feats[0].T
    depth, tokens = feats.shape
    tiles = tokens // TILE

    image_ids = lax.broadcasted_iota(jnp.int32, (*image_lists.shape, owner.shape[0]), 2)
    places = jnp.sum(jnp.where(image_lists[..., None] == image_ids, owner[None, None, :], 0), axis=-1)

    part = project(feats, key_weight, value_weight)
    queries_late, d_out_late, feats_late, part = lax.optimization_barrier((queries, d_out, feats, part))
    summed = lax.psum_scatter(part, "tp", scatter_dimension=0, tiled=True)

    def turned(array):
        return array.reshape(blocks, BLOCK, GROUP, HEAD_DIM).transpose(0, 3, 2, 1).reshape(blocks, HEAD_DIM, ROWS)

    text = jnp.stack([turned(queries_late), turned(d_out_late)], axis=1)
    text_left = move(text, along_x(1))
    text_right = move(text, along_x(-1))
    far_a = move(text_left[: blocks // 2], along_x(1))
    far_b = move(text_right[blocks // 2 :], along_x(-1))
    row_text = jnp.concatenate([text, text_left, text_right, far_a, far_b], axis=0)

    tiled = jnp.concatenate([feats_late, jnp.zeros((depth, TILE), BF16)], axis=1)
    buffer = jnp.zeros((tiles + 1, depth, TILE), BF16)
    for shift in range(SIDE):
        target = (column + shift) % SIDE
        first = (target + column) % SIDE
        slab = jnp.stack(
            [
                lax.dynamic_slice_in_dim(tiled, first * TILE, TILE, 1),
                lax.dynamic_slice_in_dim(tiled, (first + SIDE) * TILE, TILE, 1),
            ]
        )
        if shift:
            slab = move(slab, along_x(shift))
        source = (column - shift) % SIDE
        first = (column + source) % SIDE
        slot = (7 * source + first - column) // SIDE
        second = jnp.where(first + SIDE < tiles, slot + 1, tiles)
        buffer = lax.dynamic_update_slice_in_dim(buffer, slab[1:], second, 0)
        buffer = lax.dynamic_update_slice_in_dim(buffer, slab[:1], slot, 0)
    own_feats = buffer[:tiles]
    summed, row_text, own_feats = lax.optimization_barrier((summed, row_text, own_feats))
    pair = summed[0].astype(BF16)
    keys, values = pair[:, :HEAD_DIM], pair[:, HEAD_DIM:]

    key_row = jnp.zeros((SIDE, tokens, HEAD_DIM), BF16)
    for shift, offset, piece in around(keys, along_x):
        key_row = lax.dynamic_update_slice(key_row, piece[None], ((column + shift) % SIDE, offset, 0))
    value_line = jnp.zeros((SIDE, tokens, HEAD_DIM), BF16)
    for shift, offset, piece in around(values, along_y):
        value_line = lax.dynamic_update_slice(value_line, piece[None], ((line + shift) % SIDE, offset, 0))
    keys = jnp.zeros((SIDE, SIDE, tokens, HEAD_DIM), BF16)
    for shift, offset, piece in around(key_row, along_y):
        keys = lax.dynamic_update_slice(keys, piece[None], ((line + shift) % SIDE, offset, 0, 0))
    values = jnp.zeros((SIDE, SIDE, tokens, HEAD_DIM), BF16)
    for shift, offset, piece in around(value_line, along_x):
        values = lax.dynamic_update_slice(values, piece[:, None], (offset, (column + shift) % SIDE, 0, 0))
    keys, values, own_feats = lax.optimization_barrier((keys, values, own_feats))
    feats_up = move(own_feats, along_y(1))
    feats_down = move(own_feats, along_y(-1))

    images = (SIDE * SIDE, tokens, HEAD_DIM)
    attended, d_queries, stats = attend(places, queries, d_out, keys.reshape(images), values.reshape(images))

    row_stats = jnp.concatenate(
        [stats] + [move(stats, along_x(shift)) for shift in (1, -1, 2)],
        axis=0,
    )
    row_places = row_stats[:, 2:, 0].astype(jnp.int32)
    split = (-1, SIDE, TILE, HEAD_DIM)
    grads = spread(row_places, column[None], row_text, row_stats, keys.reshape(split), values.reshape(split))
    grads, feats_up, feats_down = lax.optimization_barrier((grads, feats_up, feats_down))

    own = jnp.concatenate([half.astype(BF16) for half in ring_sum(grads, along_y, line)])
    cut = (tiles + 1) // 2
    own, up_cut, down_cut = lax.optimization_barrier((own, feats_up[:cut], feats_down[cut:]))
    all_heads = lax.all_gather(own[None], "tp", axis=0, tiled=True)
    feats_far_a = move(up_cut, along_y(1))
    feats_far_b = move(down_cut, along_y(-1))
    quarter = fold(line[None], all_heads, (own_feats, feats_up, feats_down, feats_far_a, feats_far_b))
    rows = jnp.concatenate([half.astype(BF16) for half in ring_sum(quarter, along_x, column)])
    half = HEAD_DIM // 2
    side = line % 2
    swap = [(y * SIDE + x, (y ^ 1) * SIDE + x) for y in range(SIDE) for x in range(SIDE)]
    low, high = rows[:, :half], rows[:, half:]
    mine = jnp.where(side == 0, low, high)
    other = move(jnp.where(side == 0, high, low), swap)
    d_projection = jnp.concatenate(
        [jnp.where(side == 0, mine, other), jnp.where(side == 0, other, mine)], axis=1
    ).T
    return attended, d_queries, d_projection


def solution(mesh):
    return jax.shard_map(
        per_device,
        mesh=mesh,
        in_specs=(
            P(("dp", "seq"), "tp"),
            P(("dp", "seq"), "tp"),
            P(("dp", "seq"), None, "tp"),
            P("tp", None),
            P("tp", None),
            P(("dp", "seq"), None),
            P("dp"),
        ),
        out_specs=(P(("dp", "seq"), "tp"), P(("dp", "seq"), "tp"), P(("dp", "seq"), "tp")),
        check_vma=False,
    )
```

```python
import functools
import math

import jax
import jax.numpy as jnp
from jax import lax
from jax.experimental import pallas as pl
from jax.experimental.pallas import tpu as pltpu
from jax.sharding import PartitionSpec as P

QHEADS = 64
KVHEADS = 8
GROUP = QHEADS // KVHEADS
HEAD_DIM = 128
BLOCK = 64
ROWS = BLOCK * GROUP
TILE = 128
SIDE = 4
SCALE = HEAD_DIM ** -0.5
LOG2E = math.log2(math.e)
LN2 = math.log(2.0)
BF16 = jnp.bfloat16
F32 = jnp.float32
NT = (((1,), (1,)), ((), ()))
VMEM_LIMIT = 56 * 1024 * 1024


def matmul(a, b):
    return jnp.dot(a, b, preferred_element_type=F32)


def matmul_nt(a, b):
    return lax.dot_general(a, b, NT, preferred_element_type=F32)


def project_kernel(feats_ref, key_ref, value_ref, out_ref, turned_ref):
    @pl.when(pl.program_id(0) == 0)
    def _():
        turned_ref[...] = jnp.transpose(feats_ref[...])

    feats = turned_ref[...]
    for part, weight_ref in enumerate((key_ref, value_ref)):
        both = matmul(feats, weight_ref[...])
        lanes = slice(part * HEAD_DIM, (part + 1) * HEAD_DIM)
        out_ref[0, :, lanes] = both[:, :HEAD_DIM]
        out_ref[1, :, lanes] = both[:, HEAD_DIM:]


def project(feats, key_weight, value_weight):
    depth, tokens = feats.shape
    weight_spec = pl.BlockSpec((depth, 2 * HEAD_DIM), lambda i: (0, i))
    return pl.pallas_call(
        project_kernel,
        grid=(KVHEADS // 2,),
        in_specs=[pl.BlockSpec((depth, tokens), lambda i: (0, 0)), weight_spec, weight_spec],
        out_specs=pl.BlockSpec((2, tokens, 2 * HEAD_DIM), lambda i: (i, 0, 0)),
        out_shape=jax.ShapeDtypeStruct((KVHEADS, tokens, 2 * HEAD_DIM), F32),
        scratch_shapes=[pltpu.VMEM((tokens, depth), BF16)],
        compiler_params=pltpu.CompilerParams(vmem_limit_bytes=VMEM_LIMIT),
        name="project",
    )(feats, key_weight, value_weight)


def attend_kernel(
    places_ref, query_ref, grad_ref, key0_ref, key1_ref, value0_ref, value1_ref, out_ref, dq_ref, stat_ref
):
    pairs = ((key0_ref, value0_ref), (key1_ref, value1_ref))
    heads = GROUP // 2
    rows = heads * BLOCK
    lane = lax.broadcasted_iota(jnp.int32, (rows, HEAD_DIM), 1)
    chains = []
    for first in range(0, GROUP, heads):
        cols = [slice(g * HEAD_DIM, (g + 1) * HEAD_DIM) for g in range(first, first + heads)]
        query = jnp.concatenate([query_ref[:, c] for c in cols], axis=0)
        grad = jnp.concatenate([grad_ref[:, c] for c in cols], axis=0)
        scores = [matmul_nt(query, key[0]) * (SCALE * LOG2E) for key, _ in pairs]
        prob_grads = [matmul_nt(grad, value[0]) for _, value in pairs]
        chains.append((cols, grad, scores, prob_grads))
    for index, (cols, grad, scores, prob_grads) in enumerate(chains):
        maxima = [jnp.max(s, axis=1, keepdims=True) for s in scores]
        weights = [jnp.exp2(s - m) for s, m in zip(scores, maxima)]
        totals = [jnp.sum(w, axis=1, keepdims=True) for w in weights]
        partials = [
            matmul(w.astype(BF16), value[0]).astype(BF16).astype(F32) for w, (_, value) in zip(weights, pairs)
        ]
        top = jnp.maximum(maxima[0], maxima[1])
        factors = [jnp.exp2(m - top) for m in maxima]
        denominator = factors[0] * totals[0] + factors[1] * totals[1]
        numerator = factors[0] * partials[0] + factors[1] * partials[1]
        output = (numerator / denominator).astype(BF16)
        lse = top + jnp.log2(denominator)
        delta = jnp.sum(grad.astype(F32) * output.astype(F32), axis=1, keepdims=True)
        dq = []
        for (key, _), weight, factor, prob_grad in zip(pairs, weights, factors, prob_grads):
            score_grad = weight * (factor / denominator) * (prob_grad - delta)
            part = matmul(score_grad.astype(BF16), key[0]) * SCALE
            dq.append(part.astype(BF16).astype(F32))
        total = (dq[0] + dq[1]).astype(BF16)
        for g, c in enumerate(cols):
            out_ref[:, c] = output[g * BLOCK : (g + 1) * BLOCK]
            dq_ref[:, c] = total[g * BLOCK : (g + 1) * BLOCK]
        stats = jnp.transpose(jnp.where(lane == 0, lse, delta))
        stat_ref[0, 0:2, index * rows : (index + 1) * rows] = stats[:2]
    for entry in range(2):
        place = places_ref[pl.program_id(0), entry].astype(F32)
        stat_ref[0, 2 + entry : 3 + entry] = jnp.full((1, ROWS), place, F32)


def attend(places, queries, d_out, keys, values):
    blocks = places.shape[0]
    tokens = keys.shape[1]
    text = pl.BlockSpec((BLOCK, GROUP * HEAD_DIM), lambda c, p: (c, 0))

    def image(entry):
        return pl.BlockSpec((1, tokens, HEAD_DIM), lambda c, p: (p[c, entry], 0, 0))

    return pl.pallas_call(
        attend_kernel,
        grid_spec=pltpu.PrefetchScalarGridSpec(
            num_scalar_prefetch=1,
            grid=(blocks,),
            in_specs=[text, text, image(0), image(1), image(0), image(1)],
            out_specs=[text, text, pl.BlockSpec((1, 4, ROWS), lambda c, p: (c, 0, 0))],
        ),
        out_shape=[
            jax.ShapeDtypeStruct(queries.shape, BF16),
            jax.ShapeDtypeStruct(queries.shape, BF16),
            jax.ShapeDtypeStruct((blocks, 4, ROWS), F32),
        ],
        compiler_params=pltpu.CompilerParams(vmem_limit_bytes=VMEM_LIMIT),
        name="attend",
    )(places, queries, d_out, keys, keys, values, values)


def spread_kernel(unroll, places_ref, column_ref, text_ref, stat_ref, key_ref, value_ref, out_ref):
    column = column_ref[0]
    blocks = text_ref.shape[0]
    tiles = key_ref.shape[0]
    half = HEAD_DIM // 2

    def clear(m, carry):
        out_ref[:, m] = jnp.zeros((4, half, TILE), F32)
        return carry

    lax.fori_loop(0, tiles, clear, 0)

    def one(block):
        query = text_ref[block, 0]
        grad = text_ref[block, 1]
        lse = stat_ref[block, 0:1, :]
        delta = stat_ref[block, 1:2, :]
        for entry in range(2):
            place = places_ref[block, entry]
            line, spot = place // SIDE, place % SIDE
            begin = (7 * spot - column + SIDE - 1) // SIDE
            end = (7 * spot + 7 - column + SIDE - 1) // SIDE
            first = line * 7 + begin
            second = jnp.minimum(first + 1, tiles - 1)
            shut = jnp.where(end - begin == 2, 0.0, 1e30).astype(F32)
            keys = jnp.concatenate([key_ref[first, 0], key_ref[second, 0]], axis=0)
            values = jnp.concatenate([value_ref[first, 0], value_ref[second, 0]], axis=0)
            scores = matmul(keys, query) * (SCALE * LOG2E)
            prob = jnp.concatenate(
                [jnp.exp2(scores[:TILE] - lse), jnp.exp2(scores[TILE:] - (lse + shut))], axis=0
            )
            prob_grad = matmul(values, grad)
            score_grad = prob * (prob_grad - delta)
            d_value = matmul_nt(grad, prob.astype(BF16))
            d_key = matmul_nt(query, score_grad.astype(BF16))
            for i, tile in enumerate((first, second)):
                lanes = slice(i * TILE, (i + 1) * TILE)
                out_ref[0, tile] += d_key[:half, lanes]
                out_ref[1, tile] += d_key[half:, lanes]
                out_ref[2, tile] += d_value[:half, lanes]
                out_ref[3, tile] += d_value[half:, lanes]

    def several(step, carry):
        for u in range(unroll):
            one(step * unroll + u)
        return carry

    lax.fori_loop(0, blocks // unroll, several, 0)

    def scale(m, carry):
        out_ref[0, m] = out_ref[0, m] * SCALE
        out_ref[1, m] = out_ref[1, m] * SCALE
        return carry

    lax.fori_loop(0, tiles, scale, 0)


def spread(places, column, text, stats, keys, values):
    tiles = keys.shape[0]
    half = HEAD_DIM // 2
    image = pl.BlockSpec((tiles, 1, TILE, HEAD_DIM), lambda i, p, c: (0, c[0], 0, 0))
    return pl.pallas_call(
        functools.partial(spread_kernel, SIDE),
        grid_spec=pltpu.PrefetchScalarGridSpec(
            num_scalar_prefetch=2,
            grid=(1,),
            in_specs=[
                pl.BlockSpec(text.shape, lambda i, p, c: (0, 0, 0, 0)),
                pl.BlockSpec(stats.shape, lambda i, p, c: (0, 0, 0)),
                image,
                image,
            ],
            out_specs=pl.BlockSpec((4, tiles, half, TILE), lambda i, p, c: (0, 0, 0, 0)),
        ),
        out_shape=jax.ShapeDtypeStruct((4, tiles, half, TILE), F32),
        compiler_params=pltpu.CompilerParams(vmem_limit_bytes=VMEM_LIMIT),
        name="spread",
    )(places, column, text, stats, keys, values)


def fold_kernel(line_ref, grads_ref, own_ref, up_ref, down_ref, far_a_ref, far_b_ref, out_ref):
    line = line_ref[0]
    span = own_ref.shape[0]
    first = far_a_ref.shape[0]
    pieces = (
        (own_ref, 0, 0),
        (up_ref, SIDE - 1, 0),
        (down_ref, 1, 0),
        (far_a_ref, 2, 0),
        (far_b_ref, 2, first),
    )
    order = [head for x in range(SIDE) for head in (x, x + SIDE)]
    total = None
    for ref, shift, skip in pieces:
        begin = lax.rem(line + shift, SIDE) * span + skip
        count = ref.shape[0]
        grads = jnp.concatenate(
            [
                jnp.concatenate([grads_ref[head, begin + k] for head in order], axis=0)
                for k in range(count)
            ],
            axis=1,
        )
        feats = jnp.concatenate([ref[k] for k in range(count)], axis=1)
        part = matmul_nt(feats, grads)
        total = part if total is None else total + part
    for x in range(SIDE):
        out_ref[x] = total[:, x * HEAD_DIM : (x + 1) * HEAD_DIM]


def fold(line, grads, pieces, steps=3):
    depth = pieces[0].shape[1] // steps
    specs = [pl.BlockSpec((p.shape[0], depth, TILE), lambda i, l: (0, i, 0)) for p in pieces]
    return pl.pallas_call(
        fold_kernel,
        grid_spec=pltpu.PrefetchScalarGridSpec(
            num_scalar_prefetch=1,
            grid=(steps,),
            in_specs=[pl.BlockSpec(grads.shape, lambda i, l: (0, 0, 0, 0)), *specs],
            out_specs=pl.BlockSpec((SIDE, depth, HEAD_DIM), lambda i, l: (0, i, 0)),
        ),
        out_shape=jax.ShapeDtypeStruct((SIDE, depth * steps, HEAD_DIM), F32),
        compiler_params=pltpu.CompilerParams(vmem_limit_bytes=VMEM_LIMIT),
        name="fold",
    )(line, grads, *pieces)


def along_x(shift):
    return [(y * SIDE + x, y * SIDE + (x + shift) % SIDE) for y in range(SIDE) for x in range(SIDE)]


def along_y(shift):
    return [(y * SIDE + x, ((y + shift) % SIDE) * SIDE + x) for y in range(SIDE) for x in range(SIDE)]


X_GROUPS = [[y * SIDE + x for x in range(SIDE)] for y in range(SIDE)]
Y_GROUPS = [[y * SIDE + x for y in range(SIDE)] for x in range(SIDE)]


def move(array, perm):
    return lax.ppermute(array, "seq", perm)


def around(block, along):
    half = block.shape[0] // 2
    left, right = move(block, along(1)), move(block, along(-1))
    far_low, far_high = move(left[:half], along(1)), move(right[half:], along(-1))
    return ((0, 0, block), (-1, 0, left), (1, 0, right), (2, 0, far_low), (2, half, far_high))


def ring_sum(parts, along, index, sent):
    half = parts.shape[1] // 2

    def part(shift, high):
        start = (((index + shift) % SIDE, half * high) + (0,) * (parts.ndim - 2))
        return lax.dynamic_slice(parts, start, (1, half, *parts.shape[2:]))[0]

    def shifted(term, shift):
        return move(term.astype(sent), along(shift))

    far = shifted(part(2, 0), 1), shifted(part(2, 1), -1)
    left_high, right_low = shifted(part(1, 1), 1), shifted(part(-1, 0), -1)
    far_low, far_high = lax.optimization_barrier(far)
    left_low = shifted(part(1, 0) + far_low.astype(F32), 1)
    right_high = shifted(part(-1, 1) + far_high.astype(F32), -1)
    low = part(0, 0) + right_low.astype(F32) + left_low.astype(F32)
    high = part(0, 1) + left_high.astype(F32) + right_high.astype(F32)
    return jnp.concatenate([low.astype(BF16), high.astype(BF16)])


def per_device(queries, d_out, image_feats, key_weight, value_weight, image_lists, owner):
    me = lax.axis_index("seq")
    line, column = me // SIDE, me % SIDE
    blocks = image_lists.shape[0]
    feats = image_feats[0].T
    depth, tokens = feats.shape
    tiles = tokens // TILE

    image_ids = lax.broadcasted_iota(jnp.int32, (*image_lists.shape, owner.shape[0]), 2)
    places = jnp.sum(jnp.where(image_lists[..., None] == image_ids, owner[None, None, :], 0), axis=-1)

    part = project(feats, key_weight, value_weight)
    queries_late, d_out_late, feats_late, part = lax.optimization_barrier((queries, d_out, feats, part))
    summed = lax.psum_scatter(part, "tp", scatter_dimension=0, tiled=True)

    def turned(array):
        return array.reshape(blocks, BLOCK, GROUP, HEAD_DIM).transpose(0, 3, 2, 1).reshape(blocks, HEAD_DIM, ROWS)

    text = jnp.stack([turned(queries_late), turned(d_out_late)], axis=1)
    text_left = move(text, along_x(1))
    text_right = move(text, along_x(-1))
    far_a = move(text_left[: blocks // 2], along_x(1))
    far_b = move(text_right[blocks // 2 :], along_x(-1))
    row_text = jnp.concatenate([text, text_left, text_right, far_a, far_b], axis=0)

    tiled = jnp.concatenate([feats_late, jnp.zeros((depth, TILE), BF16)], axis=1)
    buffer = jnp.zeros((tiles + 1, depth, TILE), BF16)
    for shift in range(SIDE):
        target = (column + shift) % SIDE
        first = (target + column) % SIDE
        slab = jnp.stack(
            [
                lax.dynamic_slice_in_dim(tiled, first * TILE, TILE, 1),
                lax.dynamic_slice_in_dim(tiled, (first + SIDE) * TILE, TILE, 1),
            ]
        )
        if shift:
            slab = move(slab, along_x(shift))
        source = (column - shift) % SIDE
        first = (column + source) % SIDE
        slot = (7 * source + first - column) // SIDE
        second = jnp.where(first + SIDE < tiles, slot + 1, tiles)
        buffer = lax.dynamic_update_slice_in_dim(buffer, slab[1:], second, 0)
        buffer = lax.dynamic_update_slice_in_dim(buffer, slab[:1], slot, 0)
    own_feats = buffer[:tiles]
    summed, row_text, own_feats = lax.optimization_barrier((summed, row_text, own_feats))
    pair = summed[0].astype(BF16)
    keys, values = pair[:, :HEAD_DIM], pair[:, HEAD_DIM:]

    key_row = jnp.zeros((SIDE, tokens, HEAD_DIM), BF16)
    for shift, offset, piece in around(keys, along_x):
        key_row = lax.dynamic_update_slice(key_row, piece[None], ((column + shift) % SIDE, offset, 0))
    value_line = jnp.zeros((SIDE, tokens, HEAD_DIM), BF16)
    for shift, offset, piece in around(values, along_y):
        value_line = lax.dynamic_update_slice(value_line, piece[None], ((line + shift) % SIDE, offset, 0))
    keys = jnp.zeros((SIDE, SIDE, tokens, HEAD_DIM), BF16)
    for shift, offset, piece in around(key_row, along_y):
        keys = lax.dynamic_update_slice(keys, piece[None], ((line + shift) % SIDE, offset, 0, 0))
    values = jnp.zeros((SIDE, SIDE, tokens, HEAD_DIM), BF16)
    for shift, offset, piece in around(value_line, along_x):
        values = lax.dynamic_update_slice(values, piece[:, None], (offset, (column + shift) % SIDE, 0, 0))
    keys, values, own_feats = lax.optimization_barrier((keys, values, own_feats))
    feats_up = move(own_feats, along_y(1))
    feats_down = move(own_feats, along_y(-1))

    images = (SIDE * SIDE, tokens, HEAD_DIM)
    attended, d_queries, stats = attend(places, queries, d_out, keys.reshape(images), values.reshape(images))

    row_stats = jnp.concatenate(
        [stats] + [move(stats, along_x(shift)) for shift in (1, -1, 2)],
        axis=0,
    )
    row_places = row_stats[:, 2:, 0].astype(jnp.int32)
    split = (-1, SIDE, TILE, HEAD_DIM)
    grads = spread(row_places, column[None], row_text, row_stats, keys.reshape(split), values.reshape(split))
    grads, feats_up, feats_down = lax.optimization_barrier((grads, feats_up, feats_down))

    own = ring_sum(grads, along_y, line, BF16)
    cut = (tiles + 1) // 2
    own, up_cut, down_cut = lax.optimization_barrier((own, feats_up[:cut], feats_down[cut:]))
    all_heads = lax.all_gather(own[None], "tp", axis=0, tiled=True)
    feats_far_a = move(up_cut, along_y(1))
    feats_far_b = move(down_cut, along_y(-1))
    quarter = fold(line[None], all_heads, (own_feats, feats_up, feats_down, feats_far_a, feats_far_b))
    rows = ring_sum(quarter, along_x, column, F32)
    half = HEAD_DIM // 2
    side = line % 2
    swap = [(y * SIDE + x, (y ^ 1) * SIDE + x) for y in range(SIDE) for x in range(SIDE)]
    low, high = rows[:, :half], rows[:, half:]
    mine = jnp.where(side == 0, low, high)
    other = move(jnp.where(side == 0, high, low), swap)
    d_projection = jnp.concatenate(
        [jnp.where(side == 0, mine, other), jnp.where(side == 0, other, mine)], axis=1
    ).T
    return attended, d_queries, d_projection


def solution(mesh):
    return jax.shard_map(
        per_device,
        mesh=mesh,
        in_specs=(
            P(("dp", "seq"), "tp"),
            P(("dp", "seq"), "tp"),
            P(("dp", "seq"), None, "tp"),
            P("tp", None),
            P("tp", None),
            P(("dp", "seq"), None),
            P("dp"),
        ),
        out_specs=(P(("dp", "seq"), "tp"), P(("dp", "seq"), "tp"), P(("dp", "seq"), "tp")),
        check_vma=False,
    )
```

```python
import functools
import math

import jax
import jax.numpy as jnp
from jax import lax
from jax.experimental import pallas as pl
from jax.experimental.pallas import tpu as pltpu
from jax.sharding import PartitionSpec as P

QHEADS = 64
KVHEADS = 8
GROUP = QHEADS // KVHEADS
HEAD_DIM = 128
BLOCK = 64
ROWS = BLOCK * GROUP
TILE = 128
SIDE = 4
SCALE = HEAD_DIM ** -0.5
LOG2E = math.log2(math.e)
LN2 = math.log(2.0)
BF16 = jnp.bfloat16
F32 = jnp.float32
NT = (((1,), (1,)), ((), ()))
VMEM_LIMIT = 56 * 1024 * 1024


def matmul(a, b):
    return jnp.dot(a, b, preferred_element_type=F32)


def matmul_nt(a, b):
    return lax.dot_general(a, b, NT, preferred_element_type=F32)


def project_kernel(feats_ref, key_ref, value_ref, out_ref, turned_ref):
    @pl.when(pl.program_id(0) == 0)
    def _():
        turned_ref[...] = jnp.transpose(feats_ref[...])

    feats = turned_ref[...]
    for part, weight_ref in enumerate((key_ref, value_ref)):
        both = matmul(feats, weight_ref[...])
        lanes = slice(part * HEAD_DIM, (part + 1) * HEAD_DIM)
        out_ref[0, :, lanes] = both[:, :HEAD_DIM]
        out_ref[1, :, lanes] = both[:, HEAD_DIM:]


def project(feats, key_weight, value_weight):
    depth, tokens = feats.shape
    weight_spec = pl.BlockSpec((depth, 2 * HEAD_DIM), lambda i: (0, i))
    return pl.pallas_call(
        project_kernel,
        grid=(KVHEADS // 2,),
        in_specs=[pl.BlockSpec((depth, tokens), lambda i: (0, 0)), weight_spec, weight_spec],
        out_specs=pl.BlockSpec((2, tokens, 2 * HEAD_DIM), lambda i: (i, 0, 0)),
        out_shape=jax.ShapeDtypeStruct((KVHEADS, tokens, 2 * HEAD_DIM), F32),
        scratch_shapes=[pltpu.VMEM((tokens, depth), BF16)],
        compiler_params=pltpu.CompilerParams(vmem_limit_bytes=VMEM_LIMIT),
        name="project",
    )(feats, key_weight, value_weight)


def attend_kernel(
    places_ref, query_ref, grad_ref, key0_ref, key1_ref, value0_ref, value1_ref, out_ref, dq_ref, stat_ref
):
    pairs = ((key0_ref, value0_ref), (key1_ref, value1_ref))
    heads = GROUP
    rows = heads * BLOCK
    lane = lax.broadcasted_iota(jnp.int32, (rows, HEAD_DIM), 1)
    chains = []
    for first in range(0, GROUP, heads):
        cols = [slice(g * HEAD_DIM, (g + 1) * HEAD_DIM) for g in range(first, first + heads)]
        query = jnp.concatenate([query_ref[:, c] for c in cols], axis=0)
        grad = jnp.concatenate([grad_ref[:, c] for c in cols], axis=0)
        scores = [matmul_nt(query, key[0]) * (SCALE * LOG2E) for key, _ in pairs]
        prob_grads = [matmul_nt(grad, value[0]) for _, value in pairs]
        chains.append((cols, grad, scores, prob_grads))
    for index, (cols, grad, scores, prob_grads) in enumerate(chains):
        maxima = [jnp.max(s, axis=1, keepdims=True) for s in scores]
        weights = [jnp.exp2(s - m) for s, m in zip(scores, maxima)]
        totals = [jnp.sum(w, axis=1, keepdims=True) for w in weights]
        partials = [
            matmul(w.astype(BF16), value[0]).astype(BF16).astype(F32) for w, (_, value) in zip(weights, pairs)
        ]
        top = jnp.maximum(maxima[0], maxima[1])
        factors = [jnp.exp2(m - top) for m in maxima]
        denominator = factors[0] * totals[0] + factors[1] * totals[1]
        numerator = factors[0] * partials[0] + factors[1] * partials[1]
        output = (numerator / denominator).astype(BF16)
        lse = top + jnp.log2(denominator)
        delta = jnp.sum(grad.astype(F32) * output.astype(F32), axis=1, keepdims=True)
        dq = []
        for (key, _), weight, factor, prob_grad in zip(pairs, weights, factors, prob_grads):
            score_grad = weight * (factor / denominator) * (prob_grad - delta)
            part = matmul(score_grad.astype(BF16), key[0]) * SCALE
            dq.append(part.astype(BF16).astype(F32))
        total = (dq[0] + dq[1]).astype(BF16)
        for g, c in enumerate(cols):
            out_ref[:, c] = output[g * BLOCK : (g + 1) * BLOCK]
            dq_ref[:, c] = total[g * BLOCK : (g + 1) * BLOCK]
        stats = jnp.transpose(jnp.where(lane == 0, lse, delta))
        stat_ref[0, 0:2, index * rows : (index + 1) * rows] = stats[:2]
    for entry in range(2):
        place = places_ref[pl.program_id(0), entry].astype(F32)
        stat_ref[0, 2 + entry : 3 + entry] = jnp.full((1, ROWS), place, F32)


def attend(places, queries, d_out, keys, values):
    blocks = places.shape[0]
    tokens = keys.shape[1]
    text = pl.BlockSpec((BLOCK, GROUP * HEAD_DIM), lambda c, p: (c, 0))

    def image(entry):
        return pl.BlockSpec((1, tokens, HEAD_DIM), lambda c, p: (p[c, entry], 0, 0))

    return pl.pallas_call(
        attend_kernel,
        grid_spec=pltpu.PrefetchScalarGridSpec(
            num_scalar_prefetch=1,
            grid=(blocks,),
            in_specs=[text, text, image(0), image(1), image(0), image(1)],
            out_specs=[text, text, pl.BlockSpec((1, 4, ROWS), lambda c, p: (c, 0, 0))],
        ),
        out_shape=[
            jax.ShapeDtypeStruct(queries.shape, BF16),
            jax.ShapeDtypeStruct(queries.shape, BF16),
            jax.ShapeDtypeStruct((blocks, 4, ROWS), F32),
        ],
        compiler_params=pltpu.CompilerParams(vmem_limit_bytes=VMEM_LIMIT),
        name="attend",
    )(places, queries, d_out, keys, keys, values, values)


def spread_kernel(unroll, places_ref, column_ref, text_ref, stat_ref, key_ref, value_ref, out_ref):
    column = column_ref[0]
    blocks = text_ref.shape[0]
    tiles = key_ref.shape[0]
    half = HEAD_DIM // 2

    def clear(m, carry):
        out_ref[:, m] = jnp.zeros((4, half, TILE), F32)
        return carry

    lax.fori_loop(0, tiles, clear, 0)

    def one(block):
        query = text_ref[block, 0]
        grad = text_ref[block, 1]
        lse = stat_ref[block, 0:1, :]
        delta = stat_ref[block, 1:2, :]
        for entry in range(2):
            place = places_ref[block, entry]
            line, spot = place // SIDE, place % SIDE
            begin = (7 * spot - column + SIDE - 1) // SIDE
            end = (7 * spot + 7 - column + SIDE - 1) // SIDE
            first = line * 7 + begin
            second = jnp.minimum(first + 1, tiles - 1)
            shut = jnp.where(end - begin == 2, 0.0, 1e30).astype(F32)
            keys = jnp.concatenate([key_ref[first, 0], key_ref[second, 0]], axis=0)
            values = jnp.concatenate([value_ref[first, 0], value_ref[second, 0]], axis=0)
            scores = matmul(keys, query) * (SCALE * LOG2E)
            prob = jnp.concatenate(
                [jnp.exp2(scores[:TILE] - lse), jnp.exp2(scores[TILE:] - (lse + shut))], axis=0
            )
            prob_grad = matmul(values, grad)
            score_grad = prob * (prob_grad - delta)
            d_value = matmul_nt(grad, prob.astype(BF16))
            d_key = matmul_nt(query, score_grad.astype(BF16))
            for i, tile in enumerate((first, second)):
                lanes = slice(i * TILE, (i + 1) * TILE)
                out_ref[0, tile] += d_key[:half, lanes]
                out_ref[1, tile] += d_key[half:, lanes]
                out_ref[2, tile] += d_value[:half, lanes]
                out_ref[3, tile] += d_value[half:, lanes]

    def several(step, carry):
        for u in range(unroll):
            one(step * unroll + u)
        return carry

    lax.fori_loop(0, blocks // unroll, several, 0)

    def scale(m, carry):
        out_ref[0, m] = out_ref[0, m] * SCALE
        out_ref[1, m] = out_ref[1, m] * SCALE
        return carry

    lax.fori_loop(0, tiles, scale, 0)


def spread(places, column, text, stats, keys, values):
    tiles = keys.shape[0]
    half = HEAD_DIM // 2
    image = pl.BlockSpec((tiles, 1, TILE, HEAD_DIM), lambda i, p, c: (0, c[0], 0, 0))
    return pl.pallas_call(
        functools.partial(spread_kernel, SIDE),
        grid_spec=pltpu.PrefetchScalarGridSpec(
            num_scalar_prefetch=2,
            grid=(1,),
            in_specs=[
                pl.BlockSpec(text.shape, lambda i, p, c: (0, 0, 0, 0)),
                pl.BlockSpec(stats.shape, lambda i, p, c: (0, 0, 0)),
                image,
                image,
            ],
            out_specs=pl.BlockSpec((4, tiles, half, TILE), lambda i, p, c: (0, 0, 0, 0)),
        ),
        out_shape=jax.ShapeDtypeStruct((4, tiles, half, TILE), F32),
        compiler_params=pltpu.CompilerParams(vmem_limit_bytes=VMEM_LIMIT),
        name="spread",
    )(places, column, text, stats, keys, values)


def fold_kernel(
    shifts, place_ref, grads_ref, own_ref, up_ref, down_ref, far_a_ref, far_b_ref, *out_refs
):
    line, column = place_ref[0], place_ref[1]
    span = own_ref.shape[0]
    first = far_a_ref.shape[0]
    pieces = (
        (own_ref, 0, 0),
        (up_ref, SIDE - 1, 0),
        (down_ref, 1, 0),
        (far_a_ref, 2, 0),
        (far_b_ref, 2, first),
    )
    targets = [lax.rem(column + SIDE + shift, SIDE) for shift in shifts]
    order = [head for target in targets for head in (target, target + SIDE)]
    total = None
    for ref, shift, skip in pieces:
        begin = lax.rem(line + shift, SIDE) * span + skip
        count = ref.shape[0]
        grads = jnp.concatenate(
            [
                jnp.concatenate([grads_ref[head, begin + k] for head in order], axis=0)
                for k in range(count)
            ],
            axis=1,
        )
        feats = jnp.concatenate([ref[k] for k in range(count)], axis=1)
        part = matmul_nt(feats, grads)
        total = part if total is None else total + part
    for index, out_ref in enumerate(out_refs):
        out_ref[...] = total[:, index * HEAD_DIM : (index + 1) * HEAD_DIM]


def fold(shifts, place, grads, pieces, steps=3):
    depth = pieces[0].shape[1]
    specs = [pl.BlockSpec((p.shape[0], depth // steps, TILE), lambda i, l: (0, i, 0)) for p in pieces]
    out = pl.BlockSpec((depth // steps, HEAD_DIM), lambda i, l: (i, 0))
    return pl.pallas_call(
        functools.partial(fold_kernel, shifts),
        grid_spec=pltpu.PrefetchScalarGridSpec(
            num_scalar_prefetch=1,
            grid=(steps,),
            in_specs=[pl.BlockSpec(grads.shape, lambda i, l: (0, 0, 0, 0)), *specs],
            out_specs=[out for _ in shifts],
        ),
        out_shape=[jax.ShapeDtypeStruct((depth, HEAD_DIM), F32) for _ in shifts],
        compiler_params=pltpu.CompilerParams(vmem_limit_bytes=VMEM_LIMIT),
        name="fold",
    )(place, grads, *pieces)


def along_x(shift):
    return [(y * SIDE + x, y * SIDE + (x + shift) % SIDE) for y in range(SIDE) for x in range(SIDE)]


def along_y(shift):
    return [(y * SIDE + x, ((y + shift) % SIDE) * SIDE + x) for y in range(SIDE) for x in range(SIDE)]


X_GROUPS = [[y * SIDE + x for x in range(SIDE)] for y in range(SIDE)]
Y_GROUPS = [[y * SIDE + x for y in range(SIDE)] for x in range(SIDE)]


def move(array, perm):
    return lax.ppermute(array, "seq", perm)


def around(block, along):
    half = block.shape[0] // 2
    left, right = move(block, along(1)), move(block, along(-1))
    far_low, far_high = move(left[:half], along(1)), move(right[half:], along(-1))
    return ((0, 0, block), (-1, 0, left), (1, 0, right), (2, 0, far_low), (2, half, far_high))


def ring_sum(parts, along, sent):
    half = parts[0].shape[0] // 2
    lows = {shift: part[:half] for shift, part in parts.items()}
    highs = {shift: part[half:] for shift, part in parts.items()}

    def shifted(term, shift):
        return move(term.astype(sent), along(shift))

    far = shifted(lows[2], 1), shifted(highs[2], -1)
    left_high, right_low = shifted(highs[1], 1), shifted(lows[-1], -1)
    far_low, far_high = lax.optimization_barrier(far)
    near = (lows[1] + far_low.astype(F32)).astype(sent), (highs[-1] + far_high.astype(F32)).astype(sent)
    near_low, near_high = lax.optimization_barrier(near)
    left_low, right_high = shifted(near_low, 1), shifted(near_high, -1)
    low = lows[0] + right_low.astype(F32) + left_low.astype(F32)
    high = highs[0] + left_high.astype(F32) + right_high.astype(F32)
    return low.astype(BF16), high.astype(BF16)


def per_device(queries, d_out, image_feats, key_weight, value_weight, image_lists, owner):
    me = lax.axis_index("seq")
    line, column = me // SIDE, me % SIDE
    blocks = image_lists.shape[0]
    feats = image_feats[0].T
    depth, tokens = feats.shape
    tiles = tokens // TILE

    image_ids = lax.broadcasted_iota(jnp.int32, (*image_lists.shape, owner.shape[0]), 2)
    places = jnp.sum(jnp.where(image_lists[..., None] == image_ids, owner[None, None, :], 0), axis=-1)

    part = project(feats, key_weight, value_weight)
    queries_late, d_out_late, feats_late, part = lax.optimization_barrier((queries, d_out, feats, part))
    summed = lax.psum_scatter(part, "tp", scatter_dimension=0, tiled=True)

    def turned(array):
        return array.reshape(blocks, BLOCK, GROUP, HEAD_DIM).transpose(0, 3, 2, 1).reshape(blocks, HEAD_DIM, ROWS)

    text = jnp.stack([turned(queries_late), turned(d_out_late)], axis=1)
    text_left = move(text, along_x(1))
    text_right = move(text, along_x(-1))
    far_a = move(text_left[: blocks // 2], along_x(1))
    far_b = move(text_right[blocks // 2 :], along_x(-1))
    row_text = jnp.concatenate([text, text_left, text_right, far_a, far_b], axis=0)

    tiled = jnp.concatenate([feats_late, jnp.zeros((depth, TILE), BF16)], axis=1)
    buffer = jnp.zeros((tiles + 1, depth, TILE), BF16)
    for shift in range(SIDE):
        target = (column + shift) % SIDE
        first = (target + column) % SIDE
        slab = jnp.stack(
            [
                lax.dynamic_slice_in_dim(tiled, first * TILE, TILE, 1),
                lax.dynamic_slice_in_dim(tiled, (first + SIDE) * TILE, TILE, 1),
            ]
        )
        if shift:
            slab = move(slab, along_x(shift))
        source = (column - shift) % SIDE
        first = (column + source) % SIDE
        slot = (7 * source + first - column) // SIDE
        second = jnp.where(first + SIDE < tiles, slot + 1, tiles)
        buffer = lax.dynamic_update_slice_in_dim(buffer, slab[1:], second, 0)
        buffer = lax.dynamic_update_slice_in_dim(buffer, slab[:1], slot, 0)
    own_feats = buffer[:tiles]
    summed, row_text, own_feats = lax.optimization_barrier((summed, row_text, own_feats))
    pair = summed[0].astype(BF16)
    keys, values = pair[:, :HEAD_DIM], pair[:, HEAD_DIM:]

    key_row = jnp.zeros((SIDE, tokens, HEAD_DIM), BF16)
    for shift, offset, piece in around(keys, along_x):
        key_row = lax.dynamic_update_slice(key_row, piece[None], ((column + shift) % SIDE, offset, 0))
    value_line = jnp.zeros((SIDE, tokens, HEAD_DIM), BF16)
    for shift, offset, piece in around(values, along_y):
        value_line = lax.dynamic_update_slice(value_line, piece[None], ((line + shift) % SIDE, offset, 0))
    keys = jnp.zeros((SIDE, SIDE, tokens, HEAD_DIM), BF16)
    for shift, offset, piece in around(key_row, along_y):
        keys = lax.dynamic_update_slice(keys, piece[None], ((line + shift) % SIDE, offset, 0, 0))
    values = jnp.zeros((SIDE, SIDE, tokens, HEAD_DIM), BF16)
    for shift, offset, piece in around(value_line, along_x):
        values = lax.dynamic_update_slice(values, piece[:, None], (offset, (column + shift) % SIDE, 0, 0))
    keys, values, own_feats = lax.optimization_barrier((keys, values, own_feats))
    feats_up = move(own_feats, along_y(1))
    feats_down = move(own_feats, along_y(-1))

    images = (SIDE * SIDE, tokens, HEAD_DIM)
    attended, d_queries, stats = attend(places, queries, d_out, keys.reshape(images), values.reshape(images))

    row_stats = jnp.concatenate(
        [stats] + [move(stats, along_x(shift)) for shift in (1, -1, 2)],
        axis=0,
    )
    row_places = row_stats[:, 2:, 0].astype(jnp.int32)
    split = (-1, SIDE, TILE, HEAD_DIM)
    grads = spread(row_places, column[None], row_text, row_stats, keys.reshape(split), values.reshape(split))
    grads, feats_up, feats_down = lax.optimization_barrier((grads, feats_up, feats_down))

    parts = {
        shift: lax.dynamic_index_in_dim(grads, (line + shift) % SIDE, 0, False) for shift in (2, 1, -1, 0)
    }
    own = jnp.concatenate(ring_sum(parts, along_y, BF16))
    cut = (tiles + 1) // 2
    own, up_cut, down_cut = lax.optimization_barrier((own, feats_up[:cut], feats_down[cut:]))
    all_heads = lax.all_gather(own[None], "tp", axis=0, tiled=True)
    feats_far_a = move(up_cut, along_y(1))
    feats_far_b = move(down_cut, along_y(-1))
    pieces = (own_feats, feats_up, feats_down, feats_far_a, feats_far_b)
    place = jnp.stack([line, column])
    parts = {}
    for shifts in ((2, 1), (-1, 0)):
        parts.update(zip(shifts, fold(shifts, place, all_heads, pieces)))
    rows = ring_sum(parts, along_x, F32)

    half = HEAD_DIM // 2
    side = line % 2
    swap = [(y * SIDE + x, (y ^ 1) * SIDE + x) for y in range(SIDE) for x in range(SIDE)]
    given = [jnp.where(side == 0, r[:, half:], r[:, :half]) for r in rows]
    taken = move(jnp.concatenate(given, axis=1), swap)
    taken = taken[:, :half], taken[:, half:]
    kept = [jnp.where(side == 0, r[:, :half], r[:, half:]) for r in rows]
    d_projection = jnp.concatenate(
        [
            jnp.concatenate([jnp.where(side == 0, k, t), jnp.where(side == 0, t, k)], axis=1)
            for k, t in zip(kept, taken)
        ]
    ).T
    return attended, d_queries, d_projection


def solution(mesh):
    return jax.shard_map(
        per_device,
        mesh=mesh,
        in_specs=(
            P(("dp", "seq"), "tp"),
            P(("dp", "seq"), "tp"),
            P(("dp", "seq"), None, "tp"),
            P("tp", None),
            P("tp", None),
            P(("dp", "seq"), None),
            P("dp"),
        ),
        out_specs=(P(("dp", "seq"), "tp"), P(("dp", "seq"), "tp"), P(("dp", "seq"), "tp")),
        check_vma=False,
    )
```

```python
import functools
import math

import jax
import jax.numpy as jnp
from jax import lax
from jax.experimental import pallas as pl
from jax.experimental.pallas import tpu as pltpu
from jax.sharding import PartitionSpec as P

QHEADS = 64
KVHEADS = 8
GROUP = QHEADS // KVHEADS
HEAD_DIM = 128
BLOCK = 64
ROWS = BLOCK * GROUP
TILE = 128
SIDE = 4
SCALE = HEAD_DIM ** -0.5
LOG2E = math.log2(math.e)
LN2 = math.log(2.0)
BF16 = jnp.bfloat16
F32 = jnp.float32
NT = (((1,), (1,)), ((), ()))
VMEM_LIMIT = 28 * 1024 * 1024
VMEM_WHOLE = 60 * 1024 * 1024


def matmul(a, b):
    return jnp.dot(a, b, preferred_element_type=F32)


def matmul_nt(a, b):
    return lax.dot_general(a, b, NT, preferred_element_type=F32)


def project_kernel(feats_ref, key_ref, value_ref, out_ref, turned_ref):
    @pl.when(pl.program_id(0) == 0)
    def _():
        turned_ref[...] = jnp.transpose(feats_ref[...])

    feats = turned_ref[...]
    for part, weight_ref in enumerate((key_ref, value_ref)):
        both = matmul(feats, weight_ref[...])
        lanes = slice(part * HEAD_DIM, (part + 1) * HEAD_DIM)
        out_ref[0, :, lanes] = both[:, :HEAD_DIM]
        out_ref[1, :, lanes] = both[:, HEAD_DIM:]


def project(feats, key_weight, value_weight):
    depth, tokens = feats.shape
    weight_spec = pl.BlockSpec((depth, 2 * HEAD_DIM), lambda i: (0, i))
    return pl.pallas_call(
        project_kernel,
        grid=(KVHEADS // 2,),
        in_specs=[pl.BlockSpec((depth, tokens), lambda i: (0, 0)), weight_spec, weight_spec],
        out_specs=pl.BlockSpec((2, tokens, 2 * HEAD_DIM), lambda i: (i, 0, 0)),
        out_shape=jax.ShapeDtypeStruct((KVHEADS, tokens, 2 * HEAD_DIM), F32),
        scratch_shapes=[pltpu.VMEM((tokens, depth), BF16)],
        compiler_params=pltpu.CompilerParams(vmem_limit_bytes=VMEM_WHOLE),
        name="project",
    )(feats, key_weight, value_weight)


def attend_kernel(places_ref, query_ref, grad_ref, key_ref, value_ref, out_ref, dq_ref, stat_ref):
    listed = [places_ref[pl.program_id(0), entry] for entry in range(2)]
    pairs = [(key_ref.at[place], value_ref.at[place]) for place in listed]
    heads = GROUP
    rows = heads * BLOCK
    lane = lax.broadcasted_iota(jnp.int32, (rows, HEAD_DIM), 1)
    chains = []
    for first in range(0, GROUP, heads):
        cols = [slice(g * HEAD_DIM, (g + 1) * HEAD_DIM) for g in range(first, first + heads)]
        query = jnp.concatenate([query_ref[:, c] for c in cols], axis=0)
        grad = jnp.concatenate([grad_ref[:, c] for c in cols], axis=0)
        scores = [matmul_nt(query, key[...]) * (SCALE * LOG2E) for key, _ in pairs]
        prob_grads = [matmul_nt(grad, value[...]) for _, value in pairs]
        chains.append((cols, grad, scores, prob_grads))
    for index, (cols, grad, scores, prob_grads) in enumerate(chains):
        maxima = [jnp.max(s, axis=1, keepdims=True) for s in scores]
        weights = [jnp.exp2(s - m) for s, m in zip(scores, maxima)]
        totals = [jnp.sum(w, axis=1, keepdims=True) for w in weights]
        partials = [
            matmul(w.astype(BF16), value[...]).astype(BF16).astype(F32) for w, (_, value) in zip(weights, pairs)
        ]
        top = jnp.maximum(maxima[0], maxima[1])
        factors = [jnp.exp2(m - top) for m in maxima]
        denominator = factors[0] * totals[0] + factors[1] * totals[1]
        numerator = factors[0] * partials[0] + factors[1] * partials[1]
        output = (numerator / denominator).astype(BF16)
        lse = top + jnp.log2(denominator)
        delta = jnp.sum(grad.astype(F32) * output.astype(F32), axis=1, keepdims=True)
        dq = []
        for (key, _), weight, factor, prob_grad in zip(pairs, weights, factors, prob_grads):
            score_grad = weight * (factor / denominator) * (prob_grad - delta)
            part = matmul(score_grad.astype(BF16), key[...]) * SCALE
            dq.append(part.astype(BF16).astype(F32))
        total = (dq[0] + dq[1]).astype(BF16)
        for g, c in enumerate(cols):
            out_ref[:, c] = output[g * BLOCK : (g + 1) * BLOCK]
            dq_ref[:, c] = total[g * BLOCK : (g + 1) * BLOCK]
        stats = jnp.transpose(jnp.where(lane == 0, lse, delta))
        stat_ref[0, 0:2, index * rows : (index + 1) * rows] = stats[:2]
    for entry, place in enumerate(listed):
        stat_ref[0, 2 + entry : 3 + entry] = jnp.full((1, ROWS), place.astype(F32), F32)


def attend(places, queries, d_out, keys, values):
    blocks = places.shape[0]
    text = pl.BlockSpec((BLOCK, GROUP * HEAD_DIM), lambda c, p: (c, 0))
    held = pl.BlockSpec(memory_space=pltpu.VMEM)
    return pl.pallas_call(
        attend_kernel,
        grid_spec=pltpu.PrefetchScalarGridSpec(
            num_scalar_prefetch=1,
            grid=(blocks,),
            in_specs=[text, text, held, held],
            out_specs=[text, text, pl.BlockSpec((1, 4, ROWS), lambda c, p: (c, 0, 0))],
        ),
        out_shape=[
            jax.ShapeDtypeStruct(queries.shape, BF16),
            jax.ShapeDtypeStruct(queries.shape, BF16),
            jax.ShapeDtypeStruct((blocks, 4, ROWS), F32),
        ],
        compiler_params=pltpu.CompilerParams(vmem_limit_bytes=VMEM_LIMIT),
        name="attend",
    )(places, queries, d_out, keys, values)


def spread_kernel(unroll, places_ref, column_ref, text_ref, stat_ref, key_ref, value_ref, out_ref):
    column = column_ref[0]
    blocks = text_ref.shape[0]
    tiles = key_ref.shape[0]
    half = HEAD_DIM // 2

    def clear(m, carry):
        out_ref[:, m] = jnp.zeros((4, half, TILE), F32)
        return carry

    lax.fori_loop(0, tiles, clear, 0)

    def one(block):
        query = text_ref[block, 0]
        grad = text_ref[block, 1]
        lse = stat_ref[block, 0:1, :]
        delta = stat_ref[block, 1:2, :]
        for entry in range(2):
            place = places_ref[block, entry]
            line, spot = place // SIDE, place % SIDE
            begin = (7 * spot - column + SIDE - 1) // SIDE
            end = (7 * spot + 7 - column + SIDE - 1) // SIDE
            first = line * 7 + begin
            second = jnp.minimum(first + 1, tiles - 1)
            shut = jnp.where(end - begin == 2, 0.0, 1e30).astype(F32)
            keys = jnp.concatenate([key_ref[first, column], key_ref[second, column]], axis=0)
            values = jnp.concatenate([value_ref[first, column], value_ref[second, column]], axis=0)
            scores = matmul(keys, query) * (SCALE * LOG2E)
            prob = jnp.concatenate(
                [jnp.exp2(scores[:TILE] - lse), jnp.exp2(scores[TILE:] - (lse + shut))], axis=0
            )
            prob_grad = matmul(values, grad)
            score_grad = prob * (prob_grad - delta)
            d_value = matmul_nt(grad, prob.astype(BF16))
            d_key = matmul_nt(query, score_grad.astype(BF16))
            for i, tile in enumerate((first, second)):
                lanes = slice(i * TILE, (i + 1) * TILE)
                out_ref[0, tile] += d_key[:half, lanes]
                out_ref[1, tile] += d_key[half:, lanes]
                out_ref[2, tile] += d_value[:half, lanes]
                out_ref[3, tile] += d_value[half:, lanes]

    def several(step, carry):
        for u in range(unroll):
            one(step * unroll + u)
        return carry

    lax.fori_loop(0, blocks // unroll, several, 0)

    def scale(m, carry):
        out_ref[0, m] = out_ref[0, m] * SCALE
        out_ref[1, m] = out_ref[1, m] * SCALE
        return carry

    lax.fori_loop(0, tiles, scale, 0)


def spread(places, column, text, stats, keys, values):
    tiles = keys.shape[0]
    half = HEAD_DIM // 2
    held = pl.BlockSpec(memory_space=pltpu.VMEM)
    return pl.pallas_call(
        functools.partial(spread_kernel, SIDE),
        grid_spec=pltpu.PrefetchScalarGridSpec(
            num_scalar_prefetch=2,
            grid=(1,),
            in_specs=[held, held, held, held],
            out_specs=held,
        ),
        out_shape=jax.ShapeDtypeStruct((4, tiles, half, TILE), F32),
        compiler_params=pltpu.CompilerParams(vmem_limit_bytes=VMEM_LIMIT),
        name="spread",
    )(places, column, text, stats, keys, values)


def fold_kernel(
    shifts, place_ref, grads_ref, own_ref, up_ref, down_ref, far_a_ref, far_b_ref, *out_refs
):
    line, column = place_ref[0], place_ref[1]
    span = own_ref.shape[0]
    first = far_a_ref.shape[0]
    pieces = (
        (own_ref, 0, 0),
        (up_ref, SIDE - 1, 0),
        (down_ref, 1, 0),
        (far_a_ref, 2, 0),
        (far_b_ref, 2, first),
    )
    targets = [lax.rem(column + SIDE + shift, SIDE) for shift in shifts]
    order = [head for target in targets for head in (target, target + SIDE)]
    total = None
    for ref, shift, skip in pieces:
        begin = lax.rem(line + shift, SIDE) * span + skip
        count = ref.shape[0]
        grads = jnp.concatenate(
            [
                jnp.concatenate([grads_ref[head, begin + k] for head in order], axis=0)
                for k in range(count)
            ],
            axis=1,
        )
        feats = jnp.concatenate([ref[k] for k in range(count)], axis=1)
        part = matmul_nt(feats, grads)
        total = part if total is None else total + part
    for index, out_ref in enumerate(out_refs):
        out_ref[...] = total[:, index * HEAD_DIM : (index + 1) * HEAD_DIM]


def fold(shifts, place, grads, pieces):
    depth = pieces[0].shape[1]
    held = pl.BlockSpec(memory_space=pltpu.VMEM)
    return pl.pallas_call(
        functools.partial(fold_kernel, shifts),
        in_specs=[pl.BlockSpec(memory_space=pltpu.SMEM), held, *[held for _ in pieces]],
        out_specs=[held for _ in shifts],
        out_shape=[jax.ShapeDtypeStruct((depth, HEAD_DIM), F32) for _ in shifts],
        compiler_params=pltpu.CompilerParams(vmem_limit_bytes=VMEM_LIMIT),
        name="fold",
    )(place, grads, *pieces)


def along_x(shift):
    return [(y * SIDE + x, y * SIDE + (x + shift) % SIDE) for y in range(SIDE) for x in range(SIDE)]


def along_y(shift):
    return [(y * SIDE + x, ((y + shift) % SIDE) * SIDE + x) for y in range(SIDE) for x in range(SIDE)]


X_GROUPS = [[y * SIDE + x for x in range(SIDE)] for y in range(SIDE)]
Y_GROUPS = [[y * SIDE + x for y in range(SIDE)] for x in range(SIDE)]


def move(array, perm):
    return lax.ppermute(array, "seq", perm)


def around(block, along):
    half = block.shape[0] // 2
    left, right = move(block, along(1)), move(block, along(-1))
    far_low, far_high = move(left[:half], along(1)), move(right[half:], along(-1))
    return ((0, 0, block), (-1, 0, left), (1, 0, right), (2, 0, far_low), (2, half, far_high))


def ring_sum(parts, along, sent):
    half = parts[0].shape[0] // 2
    lows = {shift: part[:half] for shift, part in parts.items()}
    highs = {shift: part[half:] for shift, part in parts.items()}

    def shifted(term, shift):
        return move(term.astype(sent), along(shift))

    far = shifted(lows[2], 1), shifted(highs[2], -1)
    left_high, right_low = shifted(highs[1], 1), shifted(lows[-1], -1)
    far_low, far_high = lax.optimization_barrier(far)
    near = (lows[1] + far_low.astype(F32)).astype(sent), (highs[-1] + far_high.astype(F32)).astype(sent)
    near_low, near_high = lax.optimization_barrier(near)
    left_low, right_high = shifted(near_low, 1), shifted(near_high, -1)
    low = lows[0] + right_low.astype(F32) + left_low.astype(F32)
    high = highs[0] + left_high.astype(F32) + right_high.astype(F32)
    return low.astype(BF16), high.astype(BF16)


def per_device(queries, d_out, image_feats, key_weight, value_weight, image_lists, owner):
    me = lax.axis_index("seq")
    line, column = me // SIDE, me % SIDE
    blocks = image_lists.shape[0]
    feats = image_feats[0].T
    depth, tokens = feats.shape
    tiles = tokens // TILE

    image_ids = lax.broadcasted_iota(jnp.int32, (*image_lists.shape, owner.shape[0]), 2)
    places = jnp.sum(jnp.where(image_lists[..., None] == image_ids, owner[None, None, :], 0), axis=-1)

    part = project(feats, key_weight, value_weight)
    queries_late, d_out_late, feats_late, part = lax.optimization_barrier((queries, d_out, feats, part))
    summed = lax.psum_scatter(part, "tp", scatter_dimension=0, tiled=True)

    def turned(array):
        return array.reshape(blocks, BLOCK, GROUP, HEAD_DIM).transpose(0, 3, 2, 1).reshape(blocks, HEAD_DIM, ROWS)

    text = jnp.stack([turned(queries_late), turned(d_out_late)], axis=1)
    text_left = move(text, along_x(1))
    text_right = move(text, along_x(-1))
    far_a = move(text_left[: blocks // 2], along_x(1))
    far_b = move(text_right[blocks // 2 :], along_x(-1))
    row_text = jnp.concatenate([text, text_left, text_right, far_a, far_b], axis=0)

    tiled = jnp.concatenate([feats_late, jnp.zeros((depth, TILE), BF16)], axis=1)
    buffer = jnp.zeros((tiles + 1, depth, TILE), BF16)
    for shift in range(SIDE):
        target = (column + shift) % SIDE
        first = (target + column) % SIDE
        slab = jnp.stack(
            [
                lax.dynamic_slice_in_dim(tiled, first * TILE, TILE, 1),
                lax.dynamic_slice_in_dim(tiled, (first + SIDE) * TILE, TILE, 1),
            ]
        )
        if shift:
            slab = move(slab, along_x(shift))
        source = (column - shift) % SIDE
        first = (column + source) % SIDE
        slot = (7 * source + first - column) // SIDE
        second = jnp.where(first + SIDE < tiles, slot + 1, tiles)
        buffer = lax.dynamic_update_slice_in_dim(buffer, slab[1:], second, 0)
        buffer = lax.dynamic_update_slice_in_dim(buffer, slab[:1], slot, 0)
    own_feats = buffer[:tiles]
    summed, row_text, own_feats = lax.optimization_barrier((summed, row_text, own_feats))
    pair = summed[0].astype(BF16)
    keys, values = pair[:, :HEAD_DIM], pair[:, HEAD_DIM:]

    key_row = jnp.zeros((SIDE, tokens, HEAD_DIM), BF16)
    for shift, offset, piece in around(keys, along_x):
        key_row = lax.dynamic_update_slice(key_row, piece[None], ((column + shift) % SIDE, offset, 0))
    value_line = jnp.zeros((SIDE, tokens, HEAD_DIM), BF16)
    for shift, offset, piece in around(values, along_y):
        value_line = lax.dynamic_update_slice(value_line, piece[None], ((line + shift) % SIDE, offset, 0))
    keys = jnp.zeros((SIDE, SIDE, tokens, HEAD_DIM), BF16)
    for shift, offset, piece in around(key_row, along_y):
        keys = lax.dynamic_update_slice(keys, piece[None], ((line + shift) % SIDE, offset, 0, 0))
    values = jnp.zeros((SIDE, SIDE, tokens, HEAD_DIM), BF16)
    for shift, offset, piece in around(value_line, along_x):
        values = lax.dynamic_update_slice(values, piece[:, None], (offset, (column + shift) % SIDE, 0, 0))
    keys, values, own_feats = lax.optimization_barrier((keys, values, own_feats))
    feats_up = move(own_feats, along_y(1))
    feats_down = move(own_feats, along_y(-1))

    images = (SIDE * SIDE, tokens, HEAD_DIM)
    attended, d_queries, stats = attend(places, queries, d_out, keys.reshape(images), values.reshape(images))

    row_stats = jnp.concatenate(
        [stats] + [move(stats, along_x(shift)) for shift in (1, -1, 2)],
        axis=0,
    )
    row_places = row_stats[:, 2:, 0].astype(jnp.int32)
    split = (-1, SIDE, TILE, HEAD_DIM)
    grads = spread(row_places, column[None], row_text, row_stats, keys.reshape(split), values.reshape(split))
    grads, feats_up, feats_down = lax.optimization_barrier((grads, feats_up, feats_down))

    parts = {
        shift: lax.dynamic_index_in_dim(grads, (line + shift) % SIDE, 0, False) for shift in (2, 1, -1, 0)
    }
    own = jnp.concatenate(ring_sum(parts, along_y, BF16))
    cut = (tiles + 1) // 2
    own, up_cut, down_cut = lax.optimization_barrier((own, feats_up[:cut], feats_down[cut:]))
    all_heads = lax.all_gather(own[None], "tp", axis=0, tiled=True)
    feats_far_a = move(up_cut, along_y(1))
    feats_far_b = move(down_cut, along_y(-1))
    pieces = (own_feats, feats_up, feats_down, feats_far_a, feats_far_b)
    place = jnp.stack([line, column])
    parts = {}
    for shifts in ((2, 1), (-1, 0)):
        parts.update(zip(shifts, fold(shifts, place, all_heads, pieces)))
    rows = ring_sum(parts, along_x, F32)

    half = HEAD_DIM // 2
    side = line % 2
    swap = [(y * SIDE + x, (y ^ 1) * SIDE + x) for y in range(SIDE) for x in range(SIDE)]
    given = [jnp.where(side == 0, r[:, half:], r[:, :half]) for r in rows]
    taken = move(jnp.concatenate(given, axis=1), swap)
    taken = taken[:, :half], taken[:, half:]
    kept = [jnp.where(side == 0, r[:, :half], r[:, half:]) for r in rows]
    d_projection = jnp.concatenate(
        [
            jnp.concatenate([jnp.where(side == 0, k, t), jnp.where(side == 0, t, k)], axis=1)
            for k, t in zip(kept, taken)
        ]
    ).T
    return attended, d_queries, d_projection


def solution(mesh):
    return jax.shard_map(
        per_device,
        mesh=mesh,
        in_specs=(
            P(("dp", "seq"), "tp"),
            P(("dp", "seq"), "tp"),
            P(("dp", "seq"), None, "tp"),
            P("tp", None),
            P("tp", None),
            P(("dp", "seq"), None),
            P("dp"),
        ),
        out_specs=(P(("dp", "seq"), "tp"), P(("dp", "seq"), "tp"), P(("dp", "seq"), "tp")),
        check_vma=False,
    )
```

```python
import functools
import math

import jax
import jax.numpy as jnp
from jax import lax
from jax.experimental import pallas as pl
from jax.experimental.pallas import tpu as pltpu
from jax.sharding import PartitionSpec as P

QHEADS = 64
KVHEADS = 8
GROUP = QHEADS // KVHEADS
HEAD_DIM = 128
BLOCK = 64
ROWS = BLOCK * GROUP
TILE = 128
SIDE = 4
SCALE = HEAD_DIM ** -0.5
LOG2E = math.log2(math.e)
LN2 = math.log(2.0)
BF16 = jnp.bfloat16
F32 = jnp.float32
NT = (((1,), (1,)), ((), ()))
VMEM_LIMIT = 56 * 1024 * 1024
VMEM_HALF = 28 * 1024 * 1024


def matmul(a, b):
    return jnp.dot(a, b, preferred_element_type=F32)


def matmul_nt(a, b):
    return lax.dot_general(a, b, NT, preferred_element_type=F32)


def project_kernel(feats_ref, key_ref, value_ref, out_ref, turned_ref):
    @pl.when(pl.program_id(0) == 0)
    def _():
        turned_ref[...] = jnp.transpose(feats_ref[...])

    feats = turned_ref[...]
    for part, weight_ref in enumerate((key_ref, value_ref)):
        both = matmul(feats, weight_ref[...])
        lanes = slice(part * HEAD_DIM, (part + 1) * HEAD_DIM)
        out_ref[0, :, lanes] = both[:, :HEAD_DIM]
        out_ref[1, :, lanes] = both[:, HEAD_DIM:]


def project(feats, key_weight, value_weight):
    depth, tokens = feats.shape
    weight_spec = pl.BlockSpec((depth, 2 * HEAD_DIM), lambda i: (0, i))
    return pl.pallas_call(
        project_kernel,
        grid=(KVHEADS // 2,),
        in_specs=[pl.BlockSpec((depth, tokens), lambda i: (0, 0)), weight_spec, weight_spec],
        out_specs=pl.BlockSpec((2, tokens, 2 * HEAD_DIM), lambda i: (i, 0, 0)),
        out_shape=jax.ShapeDtypeStruct((KVHEADS, tokens, 2 * HEAD_DIM), F32),
        scratch_shapes=[pltpu.VMEM((tokens, depth), BF16)],
        compiler_params=pltpu.CompilerParams(vmem_limit_bytes=VMEM_LIMIT),
        name="project",
    )(feats, key_weight, value_weight)


def attend_kernel(
    places_ref, query_ref, grad_ref, key0_ref, key1_ref, value0_ref, value1_ref, out_ref, dq_ref, stat_ref
):
    pairs = ((key0_ref, value0_ref), (key1_ref, value1_ref))
    heads = GROUP
    rows = heads * BLOCK
    lane = lax.broadcasted_iota(jnp.int32, (rows, HEAD_DIM), 1)
    chains = []
    for first in range(0, GROUP, heads):
        cols = [slice(g * HEAD_DIM, (g + 1) * HEAD_DIM) for g in range(first, first + heads)]
        query = jnp.concatenate([query_ref[:, c] for c in cols], axis=0)
        grad = jnp.concatenate([grad_ref[:, c] for c in cols], axis=0)
        scores = [matmul_nt(query, key[0]) * (SCALE * LOG2E) for key, _ in pairs]
        prob_grads = [matmul_nt(grad, value[0]) for _, value in pairs]
        chains.append((cols, grad, scores, prob_grads))
    for index, (cols, grad, scores, prob_grads) in enumerate(chains):
        maxima = [jnp.max(s, axis=1, keepdims=True) for s in scores]
        weights = [jnp.exp2(s - m) for s, m in zip(scores, maxima)]
        totals = [jnp.sum(w, axis=1, keepdims=True) for w in weights]
        partials = [
            matmul(w.astype(BF16), value[0]).astype(BF16).astype(F32) for w, (_, value) in zip(weights, pairs)
        ]
        top = jnp.maximum(maxima[0], maxima[1])
        factors = [jnp.exp2(m - top) for m in maxima]
        denominator = factors[0] * totals[0] + factors[1] * totals[1]
        numerator = factors[0] * partials[0] + factors[1] * partials[1]
        output = (numerator / denominator).astype(BF16)
        lse = top + jnp.log2(denominator)
        delta = jnp.sum(grad.astype(F32) * output.astype(F32), axis=1, keepdims=True)
        dq = []
        for (key, _), weight, factor, prob_grad in zip(pairs, weights, factors, prob_grads):
            score_grad = weight * (factor / denominator) * (prob_grad - delta)
            part = matmul(score_grad.astype(BF16), key[0]) * SCALE
            dq.append(part.astype(BF16).astype(F32))
        total = (dq[0] + dq[1]).astype(BF16)
        for g, c in enumerate(cols):
            out_ref[:, c] = output[g * BLOCK : (g + 1) * BLOCK]
            dq_ref[:, c] = total[g * BLOCK : (g + 1) * BLOCK]
        stats = jnp.transpose(jnp.where(lane == 0, lse, delta))
        stat_ref[0, 0:2, index * rows : (index + 1) * rows] = stats[:2]
    for entry in range(2):
        place = places_ref[pl.program_id(0), entry].astype(F32)
        stat_ref[0, 2 + entry : 3 + entry] = jnp.full((1, ROWS), place, F32)


def attend(places, queries, d_out, keys, values):
    blocks = places.shape[0]
    tokens = keys.shape[1]
    text = pl.BlockSpec((BLOCK, GROUP * HEAD_DIM), lambda c, p: (c, 0))

    def image(entry):
        return pl.BlockSpec((1, tokens, HEAD_DIM), lambda c, p: (p[c, entry], 0, 0))

    return pl.pallas_call(
        attend_kernel,
        grid_spec=pltpu.PrefetchScalarGridSpec(
            num_scalar_prefetch=1,
            grid=(blocks,),
            in_specs=[text, text, image(0), image(1), image(0), image(1)],
            out_specs=[text, text, pl.BlockSpec((1, 4, ROWS), lambda c, p: (c, 0, 0))],
        ),
        out_shape=[
            jax.ShapeDtypeStruct(queries.shape, BF16),
            jax.ShapeDtypeStruct(queries.shape, BF16),
            jax.ShapeDtypeStruct((blocks, 4, ROWS), F32),
        ],
        compiler_params=pltpu.CompilerParams(vmem_limit_bytes=VMEM_LIMIT),
        name="attend",
    )(places, queries, d_out, keys, keys, values, values)


def spread_kernel(unroll, places_ref, column_ref, text_ref, stat_ref, key_ref, value_ref, out_ref):
    column = column_ref[0]
    blocks = text_ref.shape[0]
    tiles = key_ref.shape[0]
    half = HEAD_DIM // 2

    def clear(m, carry):
        out_ref[:, m] = jnp.zeros((4, half, TILE), F32)
        return carry

    lax.fori_loop(0, tiles, clear, 0)

    def one(block):
        query = text_ref[block, 0]
        grad = text_ref[block, 1]
        lse = stat_ref[block, 0:1, :]
        delta = stat_ref[block, 1:2, :]
        for entry in range(2):
            place = places_ref[block, entry]
            line, spot = place // SIDE, place % SIDE
            begin = (7 * spot - column + SIDE - 1) // SIDE
            end = (7 * spot + 7 - column + SIDE - 1) // SIDE
            first = line * 7 + begin
            second = jnp.minimum(first + 1, tiles - 1)
            shut = jnp.where(end - begin == 2, 0.0, 1e30).astype(F32)
            keys = jnp.concatenate([key_ref[first, 0], key_ref[second, 0]], axis=0)
            values = jnp.concatenate([value_ref[first, 0], value_ref[second, 0]], axis=0)
            scores = matmul(keys, query) * (SCALE * LOG2E)
            prob = jnp.concatenate(
                [jnp.exp2(scores[:TILE] - lse), jnp.exp2(scores[TILE:] - (lse + shut))], axis=0
            )
            prob_grad = matmul(values, grad)
            score_grad = prob * (prob_grad - delta)
            d_value = matmul_nt(grad, prob.astype(BF16))
            d_key = matmul_nt(query, score_grad.astype(BF16))
            for i, tile in enumerate((first, second)):
                lanes = slice(i * TILE, (i + 1) * TILE)
                out_ref[0, tile] += d_key[:half, lanes]
                out_ref[1, tile] += d_key[half:, lanes]
                out_ref[2, tile] += d_value[:half, lanes]
                out_ref[3, tile] += d_value[half:, lanes]

    def several(step, carry):
        for u in range(unroll):
            one(step * unroll + u)
        return carry

    lax.fori_loop(0, blocks // unroll, several, 0)

    def scale(m, carry):
        out_ref[0, m] = out_ref[0, m] * SCALE
        out_ref[1, m] = out_ref[1, m] * SCALE
        return carry

    lax.fori_loop(0, tiles, scale, 0)


def spread(places, column, text, stats, keys, values):
    tiles = keys.shape[0]
    half = HEAD_DIM // 2
    image = pl.BlockSpec((tiles, 1, TILE, HEAD_DIM), lambda i, p, c: (0, c[0], 0, 0))
    return pl.pallas_call(
        functools.partial(spread_kernel, SIDE),
        grid_spec=pltpu.PrefetchScalarGridSpec(
            num_scalar_prefetch=2,
            grid=(1,),
            in_specs=[
                pl.BlockSpec(text.shape, lambda i, p, c: (0, 0, 0, 0)),
                pl.BlockSpec(stats.shape, lambda i, p, c: (0, 0, 0)),
                image,
                image,
            ],
            out_specs=pl.BlockSpec((4, tiles, half, TILE), lambda i, p, c: (0, 0, 0, 0)),
        ),
        out_shape=jax.ShapeDtypeStruct((4, tiles, half, TILE), F32),
        compiler_params=pltpu.CompilerParams(vmem_limit_bytes=VMEM_LIMIT),
        name="spread",
    )(places, column, text, stats, keys, values)


def fold_kernel(
    shifts, place_ref, grads_ref, own_ref, up_ref, down_ref, far_a_ref, far_b_ref, *out_refs
):
    line, column = place_ref[0], place_ref[1]
    span = own_ref.shape[0]
    first = far_a_ref.shape[0]
    pieces = (
        (own_ref, 0, 0),
        (up_ref, SIDE - 1, 0),
        (down_ref, 1, 0),
        (far_a_ref, 2, 0),
        (far_b_ref, 2, first),
    )
    targets = [lax.rem(column + SIDE + shift, SIDE) for shift in shifts]
    order = [head for target in targets for head in (target, target + SIDE)]
    total = None
    for ref, shift, skip in pieces:
        begin = lax.rem(line + shift, SIDE) * span + skip
        count = ref.shape[0]
        grads = jnp.concatenate(
            [
                jnp.concatenate([grads_ref[head, begin + k] for head in order], axis=0)
                for k in range(count)
            ],
            axis=1,
        )
        feats = jnp.concatenate([ref[k] for k in range(count)], axis=1)
        part = matmul_nt(feats, grads)
        total = part if total is None else total + part
    for index, out_ref in enumerate(out_refs):
        out_ref[...] = total[:, index * HEAD_DIM : (index + 1) * HEAD_DIM]


def fold(shifts, place, grads, pieces):
    depth = pieces[0].shape[1]
    held = pl.BlockSpec(memory_space=pltpu.VMEM)
    far = [pl.BlockSpec(p.shape, lambda i, l: (0, 0, 0)) for p in pieces[3:]]
    return pl.pallas_call(
        functools.partial(fold_kernel, shifts),
        grid_spec=pltpu.PrefetchScalarGridSpec(
            num_scalar_prefetch=1,
            grid=(1,),
            in_specs=[pl.BlockSpec(grads.shape, lambda i, l: (0, 0, 0, 0)), held, held, held, *far],
            out_specs=[held for _ in shifts],
        ),
        out_shape=[jax.ShapeDtypeStruct((depth, HEAD_DIM), F32) for _ in shifts],
        compiler_params=pltpu.CompilerParams(vmem_limit_bytes=VMEM_HALF),
        name="fold",
    )(place, grads, *pieces)


def along_x(shift):
    return [(y * SIDE + x, y * SIDE + (x + shift) % SIDE) for y in range(SIDE) for x in range(SIDE)]


def along_y(shift):
    return [(y * SIDE + x, ((y + shift) % SIDE) * SIDE + x) for y in range(SIDE) for x in range(SIDE)]


X_GROUPS = [[y * SIDE + x for x in range(SIDE)] for y in range(SIDE)]
Y_GROUPS = [[y * SIDE + x for y in range(SIDE)] for x in range(SIDE)]


def move(array, perm):
    return lax.ppermute(array, "seq", perm)


def around(block, along):
    half = block.shape[0] // 2
    left, right = move(block, along(1)), move(block, along(-1))
    far_low, far_high = move(left[:half], along(1)), move(right[half:], along(-1))
    return ((0, 0, block), (-1, 0, left), (1, 0, right), (2, 0, far_low), (2, half, far_high))


def ring_sum(parts, along, sent):
    half = parts[0].shape[0] // 2
    lows = {shift: part[:half] for shift, part in parts.items()}
    highs = {shift: part[half:] for shift, part in parts.items()}

    def shifted(term, shift):
        return move(term.astype(sent), along(shift))

    far = shifted(lows[2], 1), shifted(highs[2], -1)
    left_high, right_low = shifted(highs[1], 1), shifted(lows[-1], -1)
    far_low, far_high = lax.optimization_barrier(far)
    near = (lows[1] + far_low.astype(F32)).astype(sent), (highs[-1] + far_high.astype(F32)).astype(sent)
    near_low, near_high = lax.optimization_barrier(near)
    left_low, right_high = shifted(near_low, 1), shifted(near_high, -1)
    low = lows[0] + right_low.astype(F32) + left_low.astype(F32)
    high = highs[0] + left_high.astype(F32) + right_high.astype(F32)
    return low.astype(BF16), high.astype(BF16)


def per_device(queries, d_out, image_feats, key_weight, value_weight, image_lists, owner):
    me = lax.axis_index("seq")
    line, column = me // SIDE, me % SIDE
    blocks = image_lists.shape[0]
    feats = image_feats[0].T
    depth, tokens = feats.shape
    tiles = tokens // TILE

    image_ids = lax.broadcasted_iota(jnp.int32, (*image_lists.shape, owner.shape[0]), 2)
    places = jnp.sum(jnp.where(image_lists[..., None] == image_ids, owner[None, None, :], 0), axis=-1)

    part = project(feats, key_weight, value_weight)
    queries_late, d_out_late, feats_late, part = lax.optimization_barrier((queries, d_out, feats, part))
    summed = lax.psum_scatter(part, "tp", scatter_dimension=0, tiled=True)

    def turned(array):
        return array.reshape(blocks, BLOCK, GROUP, HEAD_DIM).transpose(0, 3, 2, 1).reshape(blocks, HEAD_DIM, ROWS)

    text = jnp.stack([turned(queries_late), turned(d_out_late)], axis=1)
    text_left = move(text, along_x(1))
    text_right = move(text, along_x(-1))
    far_a = move(text_left[: blocks // 2], along_x(1))
    far_b = move(text_right[blocks // 2 :], along_x(-1))
    row_text = jnp.concatenate([text, text_left, text_right, far_a, far_b], axis=0)

    tiled = jnp.concatenate([feats_late, jnp.zeros((depth, TILE), BF16)], axis=1)
    buffer = jnp.zeros((tiles + 1, depth, TILE), BF16)
    for shift in range(SIDE):
        target = (column + shift) % SIDE
        first = (target + column) % SIDE
        slab = jnp.stack(
            [
                lax.dynamic_slice_in_dim(tiled, first * TILE, TILE, 1),
                lax.dynamic_slice_in_dim(tiled, (first + SIDE) * TILE, TILE, 1),
            ]
        )
        if shift:
            slab = move(slab, along_x(shift))
        source = (column - shift) % SIDE
        first = (column + source) % SIDE
        slot = (7 * source + first - column) // SIDE
        second = jnp.where(first + SIDE < tiles, slot + 1, tiles)
        buffer = lax.dynamic_update_slice_in_dim(buffer, slab[1:], second, 0)
        buffer = lax.dynamic_update_slice_in_dim(buffer, slab[:1], slot, 0)
    own_feats = buffer[:tiles]
    summed, row_text, own_feats = lax.optimization_barrier((summed, row_text, own_feats))
    pair = summed[0].astype(BF16)
    keys, values = pair[:, :HEAD_DIM], pair[:, HEAD_DIM:]

    key_row = jnp.zeros((SIDE, tokens, HEAD_DIM), BF16)
    for shift, offset, piece in around(keys, along_x):
        key_row = lax.dynamic_update_slice(key_row, piece[None], ((column + shift) % SIDE, offset, 0))
    value_line = jnp.zeros((SIDE, tokens, HEAD_DIM), BF16)
    for shift, offset, piece in around(values, along_y):
        value_line = lax.dynamic_update_slice(value_line, piece[None], ((line + shift) % SIDE, offset, 0))
    keys = jnp.zeros((SIDE, SIDE, tokens, HEAD_DIM), BF16)
    for shift, offset, piece in around(key_row, along_y):
        keys = lax.dynamic_update_slice(keys, piece[None], ((line + shift) % SIDE, offset, 0, 0))
    values = jnp.zeros((SIDE, SIDE, tokens, HEAD_DIM), BF16)
    for shift, offset, piece in around(value_line, along_x):
        values = lax.dynamic_update_slice(values, piece[:, None], (offset, (column + shift) % SIDE, 0, 0))
    keys, values, own_feats = lax.optimization_barrier((keys, values, own_feats))
    feats_up = move(own_feats, along_y(1))
    feats_down = move(own_feats, along_y(-1))

    images = (SIDE * SIDE, tokens, HEAD_DIM)
    attended, d_queries, stats = attend(places, queries, d_out, keys.reshape(images), values.reshape(images))

    row_stats = jnp.concatenate(
        [stats] + [move(stats, along_x(shift)) for shift in (1, -1, 2)],
        axis=0,
    )
    row_places = row_stats[:, 2:, 0].astype(jnp.int32)
    split = (-1, SIDE, TILE, HEAD_DIM)
    grads = spread(row_places, column[None], row_text, row_stats, keys.reshape(split), values.reshape(split))
    grads, feats_up, feats_down = lax.optimization_barrier((grads, feats_up, feats_down))

    parts = {
        shift: lax.dynamic_index_in_dim(grads, (line + shift) % SIDE, 0, False) for shift in (2, 1, -1, 0)
    }
    own = jnp.concatenate(ring_sum(parts, along_y, BF16))
    cut = (tiles + 1) // 2
    own, up_cut, down_cut = lax.optimization_barrier((own, feats_up[:cut], feats_down[cut:]))
    all_heads = lax.all_gather(own[None], "tp", axis=0, tiled=True)
    feats_far_a = move(up_cut, along_y(1))
    feats_far_b = move(down_cut, along_y(-1))
    pieces = (own_feats, feats_up, feats_down, feats_far_a, feats_far_b)
    place = jnp.stack([line, column])
    parts = {}
    for shifts in ((2, 1), (-1, 0)):
        parts.update(zip(shifts, fold(shifts, place, all_heads, pieces)))
    rows = ring_sum(parts, along_x, F32)

    half = HEAD_DIM // 2
    side = line % 2
    swap = [(y * SIDE + x, (y ^ 1) * SIDE + x) for y in range(SIDE) for x in range(SIDE)]
    given = [jnp.where(side == 0, r[:, half:], r[:, :half]) for r in rows]
    taken = move(jnp.concatenate(given, axis=1), swap)
    taken = taken[:, :half], taken[:, half:]
    kept = [jnp.where(side == 0, r[:, :half], r[:, half:]) for r in rows]
    d_projection = jnp.concatenate(
        [
            jnp.concatenate([jnp.where(side == 0, k, t), jnp.where(side == 0, t, k)], axis=1)
            for k, t in zip(kept, taken)
        ]
    ).T
    return attended, d_queries, d_projection


def solution(mesh):
    return jax.shard_map(
        per_device,
        mesh=mesh,
        in_specs=(
            P(("dp", "seq"), "tp"),
            P(("dp", "seq"), "tp"),
            P(("dp", "seq"), None, "tp"),
            P("tp", None),
            P("tp", None),
            P(("dp", "seq"), None),
            P("dp"),
        ),
        out_specs=(P(("dp", "seq"), "tp"), P(("dp", "seq"), "tp"), P(("dp", "seq"), "tp")),
        check_vma=False,
    )
```

```python
import functools
import math

import jax
import jax.numpy as jnp
from jax import lax
from jax.experimental import pallas as pl
from jax.experimental.pallas import tpu as pltpu
from jax.sharding import PartitionSpec as P

QHEADS = 64
KVHEADS = 8
GROUP = QHEADS // KVHEADS
HEAD_DIM = 128
BLOCK = 64
ROWS = BLOCK * GROUP
TILE = 128
SIDE = 4
SCALE = HEAD_DIM ** -0.5
LOG2E = math.log2(math.e)
LN2 = math.log(2.0)
BF16 = jnp.bfloat16
F32 = jnp.float32
NT = (((1,), (1,)), ((), ()))
VMEM_LIMIT = 56 * 1024 * 1024
VMEM_HALF = 28 * 1024 * 1024


def matmul(a, b):
    return jnp.dot(a, b, preferred_element_type=F32)


def matmul_nt(a, b):
    return lax.dot_general(a, b, NT, preferred_element_type=F32)


def project_kernel(feats_ref, key_ref, value_ref, out_ref, side_ref, turned_ref):
    @pl.when(pl.program_id(0) == 0)
    def _():
        turned_ref[...] = jnp.transpose(feats_ref[...])

    feats = turned_ref[...]
    for part, weight_ref in enumerate((key_ref, value_ref)):
        both = matmul(feats, weight_ref[...])
        lanes = slice(part * HEAD_DIM, (part + 1) * HEAD_DIM)
        cut = out_ref.shape[1]
        for head in range(2):
            one = both[:, head * HEAD_DIM : (head + 1) * HEAD_DIM]
            out_ref[head, :, lanes] = one[:cut]
            side_ref[head, :, lanes] = one[cut:]


def project(feats, key_weight, value_weight):
    depth, tokens = feats.shape
    aside = tokens // SIDE
    weight_spec = pl.BlockSpec((depth, 2 * HEAD_DIM), lambda i: (0, i))
    return pl.pallas_call(
        project_kernel,
        grid=(KVHEADS // 2,),
        in_specs=[pl.BlockSpec((depth, tokens), lambda i: (0, 0)), weight_spec, weight_spec],
        out_specs=[pl.BlockSpec((2, rows, 2 * HEAD_DIM), lambda i: (i, 0, 0)) for rows in (tokens - aside, aside)],
        out_shape=[
            jax.ShapeDtypeStruct((KVHEADS, rows, 2 * HEAD_DIM), F32) for rows in (tokens - aside, aside)
        ],
        scratch_shapes=[pltpu.VMEM((tokens, depth), BF16)],
        compiler_params=pltpu.CompilerParams(vmem_limit_bytes=VMEM_LIMIT),
        name="project",
    )(feats, key_weight, value_weight)


def attend_kernel(
    places_ref, query_ref, grad_ref, key0_ref, key1_ref, value0_ref, value1_ref, out_ref, dq_ref, stat_ref
):
    pairs = ((key0_ref, value0_ref), (key1_ref, value1_ref))
    heads = GROUP
    rows = heads * BLOCK
    lane = lax.broadcasted_iota(jnp.int32, (rows, HEAD_DIM), 1)
    chains = []
    for first in range(0, GROUP, heads):
        cols = [slice(g * HEAD_DIM, (g + 1) * HEAD_DIM) for g in range(first, first + heads)]
        query = jnp.concatenate([query_ref[:, c] for c in cols], axis=0)
        grad = jnp.concatenate([grad_ref[:, c] for c in cols], axis=0)
        scores = [matmul_nt(query, key[0]) * (SCALE * LOG2E) for key, _ in pairs]
        prob_grads = [matmul_nt(grad, value[0]) for _, value in pairs]
        chains.append((cols, grad, scores, prob_grads))
    for index, (cols, grad, scores, prob_grads) in enumerate(chains):
        maxima = [jnp.max(s, axis=1, keepdims=True) for s in scores]
        weights = [jnp.exp2(s - m) for s, m in zip(scores, maxima)]
        totals = [jnp.sum(w, axis=1, keepdims=True) for w in weights]
        partials = [
            matmul(w.astype(BF16), value[0]).astype(BF16).astype(F32) for w, (_, value) in zip(weights, pairs)
        ]
        top = jnp.maximum(maxima[0], maxima[1])
        factors = [jnp.exp2(m - top) for m in maxima]
        denominator = factors[0] * totals[0] + factors[1] * totals[1]
        numerator = factors[0] * partials[0] + factors[1] * partials[1]
        output = (numerator / denominator).astype(BF16)
        lse = top + jnp.log2(denominator)
        delta = jnp.sum(grad.astype(F32) * output.astype(F32), axis=1, keepdims=True)
        dq = []
        for (key, _), weight, factor, prob_grad in zip(pairs, weights, factors, prob_grads):
            score_grad = weight * (factor / denominator) * (prob_grad - delta)
            part = matmul(score_grad.astype(BF16), key[0]) * SCALE
            dq.append(part.astype(BF16).astype(F32))
        total = (dq[0] + dq[1]).astype(BF16)
        for g, c in enumerate(cols):
            out_ref[:, c] = output[g * BLOCK : (g + 1) * BLOCK]
            dq_ref[:, c] = total[g * BLOCK : (g + 1) * BLOCK]
        stats = jnp.transpose(jnp.where(lane == 0, lse, delta))
        stat_ref[0, 0:2, index * rows : (index + 1) * rows] = stats[:2]
    for entry in range(2):
        place = places_ref[pl.program_id(0), entry].astype(F32)
        stat_ref[0, 2 + entry : 3 + entry] = jnp.full((1, ROWS), place, F32)


def attend(places, queries, d_out, keys, values):
    blocks = places.shape[0]
    tokens = keys.shape[1]
    text = pl.BlockSpec((BLOCK, GROUP * HEAD_DIM), lambda c, p: (c, 0))

    def image(entry):
        return pl.BlockSpec((1, tokens, HEAD_DIM), lambda c, p: (p[c, entry], 0, 0))

    return pl.pallas_call(
        attend_kernel,
        grid_spec=pltpu.PrefetchScalarGridSpec(
            num_scalar_prefetch=1,
            grid=(blocks,),
            in_specs=[text, text, image(0), image(1), image(0), image(1)],
            out_specs=[text, text, pl.BlockSpec((1, 4, ROWS), lambda c, p: (c, 0, 0))],
        ),
        out_shape=[
            jax.ShapeDtypeStruct(queries.shape, BF16),
            jax.ShapeDtypeStruct(queries.shape, BF16),
            jax.ShapeDtypeStruct((blocks, 4, ROWS), F32),
        ],
        compiler_params=pltpu.CompilerParams(vmem_limit_bytes=VMEM_LIMIT),
        name="attend",
    )(places, queries, d_out, keys, keys, values, values)


def spread_kernel(unroll, places_ref, column_ref, text_ref, stat_ref, key_ref, value_ref, out_ref):
    column = column_ref[0]
    blocks = text_ref.shape[0]
    tiles = key_ref.shape[0]
    half = HEAD_DIM // 2

    def clear(m, carry):
        out_ref[:, m] = jnp.zeros((4, half, TILE), F32)
        return carry

    lax.fori_loop(0, tiles, clear, 0)

    def one(block):
        query = text_ref[block, 0]
        grad = text_ref[block, 1]
        lse = stat_ref[block, 0:1, :]
        delta = stat_ref[block, 1:2, :]
        for entry in range(2):
            place = places_ref[block, entry]
            line, spot = place // SIDE, place % SIDE
            begin = (7 * spot - column + SIDE - 1) // SIDE
            end = (7 * spot + 7 - column + SIDE - 1) // SIDE
            first = line * 7 + begin
            second = jnp.minimum(first + 1, tiles - 1)
            shut = jnp.where(end - begin == 2, 0.0, 1e30).astype(F32)
            keys = jnp.concatenate([key_ref[first, 0], key_ref[second, 0]], axis=0)
            values = jnp.concatenate([value_ref[first, 0], value_ref[second, 0]], axis=0)
            scores = matmul(keys, query) * (SCALE * LOG2E)
            prob = jnp.concatenate(
                [jnp.exp2(scores[:TILE] - lse), jnp.exp2(scores[TILE:] - (lse + shut))], axis=0
            )
            prob_grad = matmul(values, grad)
            score_grad = prob * (prob_grad - delta)
            d_value = matmul_nt(grad, prob.astype(BF16))
            d_key = matmul_nt(query, score_grad.astype(BF16))
            for i, tile in enumerate((first, second)):
                lanes = slice(i * TILE, (i + 1) * TILE)
                out_ref[0, tile] += d_key[:half, lanes]
                out_ref[1, tile] += d_key[half:, lanes]
                out_ref[2, tile] += d_value[:half, lanes]
                out_ref[3, tile] += d_value[half:, lanes]

    def several(step, carry):
        for u in range(unroll):
            one(step * unroll + u)
        return carry

    lax.fori_loop(0, blocks // unroll, several, 0)

    def scale(m, carry):
        out_ref[0, m] = out_ref[0, m] * SCALE
        out_ref[1, m] = out_ref[1, m] * SCALE
        return carry

    lax.fori_loop(0, tiles, scale, 0)


def spread(places, column, text, stats, keys, values):
    tiles = keys.shape[0]
    half = HEAD_DIM // 2
    image = pl.BlockSpec((tiles, 1, TILE, HEAD_DIM), lambda i, p, c: (0, c[0], 0, 0))
    return pl.pallas_call(
        functools.partial(spread_kernel, SIDE),
        grid_spec=pltpu.PrefetchScalarGridSpec(
            num_scalar_prefetch=2,
            grid=(1,),
            in_specs=[
                pl.BlockSpec(text.shape, lambda i, p, c: (0, 0, 0, 0)),
                pl.BlockSpec(stats.shape, lambda i, p, c: (0, 0, 0)),
                image,
                image,
            ],
            out_specs=pl.BlockSpec((4, tiles, half, TILE), lambda i, p, c: (0, 0, 0, 0)),
        ),
        out_shape=jax.ShapeDtypeStruct((4, tiles, half, TILE), F32),
        compiler_params=pltpu.CompilerParams(vmem_limit_bytes=VMEM_LIMIT),
        name="spread",
    )(places, column, text, stats, keys, values)


def fold_kernel(
    shifts, place_ref, grads_ref, own_ref, up_ref, down_ref, far_a_ref, far_b_ref, *rest
):
    out_refs, (heads_ref, near_a_ref, near_b_ref, sems) = rest[: len(shifts)], rest[len(shifts) :]
    line, column = place_ref[0], place_ref[1]
    span = own_ref.shape[0]
    first = far_a_ref.shape[0]
    targets = [lax.rem(column + SIDE + shift, SIDE) for shift in shifts]
    order = [head for target in targets for head in (target, target + SIDE)]
    copies = [
        pltpu.make_async_copy(grads_ref.at[head], heads_ref.at[i], sems.at[i]) for i, head in enumerate(order)
    ]
    far_copies = [
        pltpu.make_async_copy(far_a_ref, near_a_ref, sems.at[len(order)]),
        pltpu.make_async_copy(far_b_ref, near_b_ref, sems.at[len(order) + 1]),
    ]
    for copy in copies + far_copies:
        copy.start()
    for copy in copies:
        copy.wait()

    def terms(ref, shift, skip):
        begin = lax.rem(line + shift, SIDE) * span + skip
        count = ref.shape[0]
        grads = jnp.concatenate(
            [
                jnp.concatenate([heads_ref[i, begin + k] for i in range(len(order))], axis=0)
                for k in range(count)
            ],
            axis=1,
        )
        return matmul_nt(jnp.concatenate([ref[k] for k in range(count)], axis=1), grads)

    total = terms(own_ref, 0, 0) + terms(up_ref, SIDE - 1, 0) + terms(down_ref, 1, 0)
    for copy in far_copies:
        copy.wait()
    total = total + terms(near_a_ref, 2, 0) + terms(near_b_ref, 2, first)
    for index, out_ref in enumerate(out_refs):
        out_ref[...] = total[:, index * HEAD_DIM : (index + 1) * HEAD_DIM]


def fold(shifts, place, grads, pieces):
    depth = pieces[0].shape[1]
    held = pl.BlockSpec(memory_space=pltpu.VMEM)
    away = pl.BlockSpec(memory_space=pl.ANY)
    heads = 2 * len(shifts)
    return pl.pallas_call(
        functools.partial(fold_kernel, shifts),
        grid_spec=pltpu.PrefetchScalarGridSpec(
            num_scalar_prefetch=1,
            grid=(1,),
            in_specs=[away, held, held, held, away, away],
            out_specs=[held for _ in shifts],
            scratch_shapes=[
                pltpu.VMEM((heads, *grads.shape[1:]), BF16),
                *[pltpu.VMEM(p.shape, BF16) for p in pieces[3:]],
                pltpu.SemaphoreType.DMA((heads + 2,)),
            ],
        ),
        out_shape=[jax.ShapeDtypeStruct((depth, HEAD_DIM), F32) for _ in shifts],
        compiler_params=pltpu.CompilerParams(vmem_limit_bytes=VMEM_HALF),
        name="fold",
    )(place, grads, *pieces)


def along_x(shift):
    return [(y * SIDE + x, y * SIDE + (x + shift) % SIDE) for y in range(SIDE) for x in range(SIDE)]


def along_y(shift):
    return [(y * SIDE + x, ((y + shift) % SIDE) * SIDE + x) for y in range(SIDE) for x in range(SIDE)]


X_GROUPS = [[y * SIDE + x for x in range(SIDE)] for y in range(SIDE)]
Y_GROUPS = [[y * SIDE + x for y in range(SIDE)] for x in range(SIDE)]


def move(array, perm):
    return lax.ppermute(array, "seq", perm)


def around(block, along):
    half = block.shape[0] // 2
    left, right = move(block, along(1)), move(block, along(-1))
    far_low, far_high = move(left[:half], along(1)), move(right[half:], along(-1))
    return ((0, 0, block), (-1, 0, left), (1, 0, right), (2, 0, far_low), (2, half, far_high))


def ring_sum(parts, along, sent):
    half = parts[0].shape[0] // 2
    lows = {shift: part[:half] for shift, part in parts.items()}
    highs = {shift: part[half:] for shift, part in parts.items()}

    def shifted(term, shift):
        return move(term.astype(sent), along(shift))

    far = shifted(lows[2], 1), shifted(highs[2], -1)
    left_high, right_low = shifted(highs[1], 1), shifted(lows[-1], -1)
    far_low, far_high = lax.optimization_barrier(far)
    near = (lows[1] + far_low.astype(F32)).astype(sent), (highs[-1] + far_high.astype(F32)).astype(sent)
    near_low, near_high = lax.optimization_barrier(near)
    left_low, right_high = shifted(near_low, 1), shifted(near_high, -1)
    low = lows[0] + right_low.astype(F32) + left_low.astype(F32)
    high = highs[0] + left_high.astype(F32) + right_high.astype(F32)
    return low.astype(BF16), high.astype(BF16)


def per_device(queries, d_out, image_feats, key_weight, value_weight, image_lists, owner):
    me = lax.axis_index("seq")
    line, column = me // SIDE, me % SIDE
    blocks = image_lists.shape[0]
    feats = image_feats[0].T
    depth, tokens = feats.shape
    tiles = tokens // TILE

    image_ids = lax.broadcasted_iota(jnp.int32, (*image_lists.shape, owner.shape[0]), 2)
    places = jnp.sum(jnp.where(image_lists[..., None] == image_ids, owner[None, None, :], 0), axis=-1)

    part, aside = project(feats, key_weight, value_weight)
    queries_late, d_out_late, feats_late, part, aside = lax.optimization_barrier(
        (queries, d_out, feats, part, aside)
    )
    summed = lax.psum_scatter(part, "tp", scatter_dimension=0, tiled=True)

    def turned(array):
        return array.reshape(blocks, BLOCK, GROUP, HEAD_DIM).transpose(0, 3, 2, 1).reshape(blocks, HEAD_DIM, ROWS)

    text = jnp.stack([turned(queries_late), turned(d_out_late)], axis=1)
    text_left = move(text, along_x(1))
    text_right = move(text, along_x(-1))

    plane, planes = lax.axis_index("tp"), lax.axis_size("tp")
    middle = aside.shape[1] // 2

    def mine(shift):
        return lax.dynamic_index_in_dim(aside, (plane + shift) % planes, 0, False)

    def along_z(array, shift):
        return lax.ppermute(array, "tp", [(z, (z + shift) % planes) for z in range(planes)])

    opposite = mine(planes // 2)
    ahead, behind = along_z(opposite[:middle], 1), along_z(opposite[middle:], -1)
    for distance in range(planes // 2 - 1, 0, -1):
        right, left = mine(distance), mine(-distance)
        if distance == planes // 2 - 1:
            right = jnp.concatenate([right[:middle] + ahead, right[middle:]])
            left = jnp.concatenate([left[:middle], left[middle:] + behind])
        else:
            right, left = right + ahead, left + behind
        ahead, behind = along_z(right, 1), along_z(left, -1)
        if distance == planes // 2 - 1:
            ahead, behind, text_left, text_right = lax.optimization_barrier(
                (ahead, behind, text_left, text_right)
            )
        if distance == planes // 2 - 2:
            ahead, behind, feats_late = lax.optimization_barrier((ahead, behind, feats_late))
    aside = mine(0) + ahead + behind

    far_a = move(text_left[: blocks // 2], along_x(1))
    far_b = move(text_right[blocks // 2 :], along_x(-1))
    row_text = jnp.concatenate([text, text_left, text_right, far_a, far_b], axis=0)

    tiled = jnp.concatenate([feats_late, jnp.zeros((depth, TILE), BF16)], axis=1)
    slabs = []
    for shift in range(SIDE):
        first = (column + shift + column) % SIDE
        slab = jnp.stack(
            [
                lax.dynamic_slice_in_dim(tiled, first * TILE, TILE, 1),
                lax.dynamic_slice_in_dim(tiled, (first + SIDE) * TILE, TILE, 1),
            ]
        )
        slabs.append(move(slab, along_x(shift)) if shift else slab)

    summed, aside, row_text, *slabs = lax.optimization_barrier((summed, aside, row_text, *slabs))
    pair = jnp.concatenate([summed[0].astype(BF16), aside.astype(BF16)])
    keys, values = pair[:, :HEAD_DIM], pair[:, HEAD_DIM:]

    buffer = jnp.zeros((tiles + 1, depth, TILE), BF16)
    for shift, slab in enumerate(slabs):
        source = (column - shift) % SIDE
        first = (column + source) % SIDE
        slot = (7 * source + first - column) // SIDE
        second = jnp.where(first + SIDE < tiles, slot + 1, tiles)
        buffer = lax.dynamic_update_slice_in_dim(buffer, slab[1:], second, 0)
        buffer = lax.dynamic_update_slice_in_dim(buffer, slab[:1], slot, 0)
    own_feats = buffer[:tiles]

    key_row = jnp.zeros((SIDE, tokens, HEAD_DIM), BF16)
    for shift, offset, piece in around(keys, along_x):
        key_row = lax.dynamic_update_slice(key_row, piece[None], ((column + shift) % SIDE, offset, 0))
    value_line = jnp.zeros((SIDE, tokens, HEAD_DIM), BF16)
    for shift, offset, piece in around(values, along_y):
        value_line = lax.dynamic_update_slice(value_line, piece[None], ((line + shift) % SIDE, offset, 0))
    keys = jnp.zeros((SIDE, SIDE, tokens, HEAD_DIM), BF16)
    for shift, offset, piece in around(key_row, along_y):
        keys = lax.dynamic_update_slice(keys, piece[None], ((line + shift) % SIDE, offset, 0, 0))
    values = jnp.zeros((SIDE, SIDE, tokens, HEAD_DIM), BF16)
    for shift, offset, piece in around(value_line, along_x):
        values = lax.dynamic_update_slice(values, piece[:, None], (offset, (column + shift) % SIDE, 0, 0))
    keys, values, own_feats = lax.optimization_barrier((keys, values, own_feats))
    feats_up = move(own_feats, along_y(1))
    feats_down = move(own_feats, along_y(-1))

    images = (SIDE * SIDE, tokens, HEAD_DIM)
    attended, d_queries, stats = attend(places, queries, d_out, keys.reshape(images), values.reshape(images))

    row_stats = jnp.concatenate(
        [stats] + [move(stats, along_x(shift)) for shift in (1, -1, 2)],
        axis=0,
    )
    row_places = row_stats[:, 2:, 0].astype(jnp.int32)
    split = (-1, SIDE, TILE, HEAD_DIM)
    grads = spread(row_places, column[None], row_text, row_stats, keys.reshape(split), values.reshape(split))
    grads, feats_up, feats_down = lax.optimization_barrier((grads, feats_up, feats_down))

    parts = {
        shift: lax.dynamic_index_in_dim(grads, (line + shift) % SIDE, 0, False) for shift in (2, 1, -1, 0)
    }
    own = jnp.concatenate(ring_sum(parts, along_y, BF16))
    cut = (tiles + 1) // 2
    own, up_cut, down_cut = lax.optimization_barrier((own, feats_up[:cut], feats_down[cut:]))
    all_heads = lax.all_gather(own[None], "tp", axis=0, tiled=True)
    feats_far_a = move(up_cut, along_y(1))
    feats_far_b = move(down_cut, along_y(-1))
    pieces = (own_feats, feats_up, feats_down, feats_far_a, feats_far_b)
    place = jnp.stack([line, column])
    parts = {}
    for shifts in ((2, 1), (-1, 0)):
        parts.update(zip(shifts, fold(shifts, place, all_heads, pieces)))
    rows = ring_sum(parts, along_x, F32)

    half = HEAD_DIM // 2
    side = line % 2
    swap = [(y * SIDE + x, (y ^ 1) * SIDE + x) for y in range(SIDE) for x in range(SIDE)]
    given = [jnp.where(side == 0, r[:, half:], r[:, :half]) for r in rows]
    taken = move(jnp.concatenate(given, axis=1), swap)
    taken = taken[:, :half], taken[:, half:]
    kept = [jnp.where(side == 0, r[:, :half], r[:, half:]) for r in rows]
    d_projection = jnp.concatenate(
        [
            jnp.concatenate([jnp.where(side == 0, k, t), jnp.where(side == 0, t, k)], axis=1)
            for k, t in zip(kept, taken)
        ]
    ).T
    return attended, d_queries, d_projection


def solution(mesh):
    return jax.shard_map(
        per_device,
        mesh=mesh,
        in_specs=(
            P(("dp", "seq"), "tp"),
            P(("dp", "seq"), "tp"),
            P(("dp", "seq"), None, "tp"),
            P("tp", None),
            P("tp", None),
            P(("dp", "seq"), None),
            P("dp"),
        ),
        out_specs=(P(("dp", "seq"), "tp"), P(("dp", "seq"), "tp"), P(("dp", "seq"), "tp")),
        check_vma=False,
    )
```

```python
import functools
import math

import jax
import jax.numpy as jnp
from jax import lax
from jax.experimental import pallas as pl
from jax.experimental.pallas import tpu as pltpu
from jax.sharding import PartitionSpec as P

QHEADS = 64
KVHEADS = 8
GROUP = QHEADS // KVHEADS
HEAD_DIM = 128
BLOCK = 64
ROWS = BLOCK * GROUP
TILE = 128
SIDE = 4
SCALE = HEAD_DIM ** -0.5
LOG2E = math.log2(math.e)
LN2 = math.log(2.0)
BF16 = jnp.bfloat16
F32 = jnp.float32
FIRST_STEP = ((2, 0), (2, 1), (1, 1), (-1, 0))
NT = (((1,), (1,)), ((), ()))
VMEM_LIMIT = 56 * 1024 * 1024
VMEM_HALF = 28 * 1024 * 1024


def matmul(a, b):
    return jnp.dot(a, b, preferred_element_type=F32)


def matmul_nt(a, b):
    return lax.dot_general(a, b, NT, preferred_element_type=F32)


def project_kernel(feats_ref, key_ref, value_ref, out_ref, turned_ref):
    @pl.when(pl.program_id(0) == 0)
    def _():
        turned_ref[...] = jnp.transpose(feats_ref[...])

    feats = turned_ref[...]
    for part, weight_ref in enumerate((key_ref, value_ref)):
        both = matmul(feats, weight_ref[...])
        lanes = slice(part * HEAD_DIM, (part + 1) * HEAD_DIM)
        out_ref[0, :, lanes] = both[:, :HEAD_DIM]
        out_ref[1, :, lanes] = both[:, HEAD_DIM:]


def project(feats, key_weight, value_weight):
    depth, tokens = feats.shape
    weight_spec = pl.BlockSpec((depth, 2 * HEAD_DIM), lambda i: (0, i))
    return pl.pallas_call(
        project_kernel,
        grid=(KVHEADS // 2,),
        in_specs=[pl.BlockSpec((depth, tokens), lambda i: (0, 0)), weight_spec, weight_spec],
        out_specs=pl.BlockSpec((2, tokens, 2 * HEAD_DIM), lambda i: (i, 0, 0)),
        out_shape=jax.ShapeDtypeStruct((KVHEADS, tokens, 2 * HEAD_DIM), F32),
        scratch_shapes=[pltpu.VMEM((tokens, depth), BF16)],
        compiler_params=pltpu.CompilerParams(vmem_limit_bytes=VMEM_LIMIT),
        name="project",
    )(feats, key_weight, value_weight)


def attend_kernel(
    places_ref, query_ref, grad_ref, key0_ref, key1_ref, value0_ref, value1_ref, out_ref, dq_ref, stat_ref
):
    pairs = ((key0_ref, value0_ref), (key1_ref, value1_ref))
    heads = GROUP
    rows = heads * BLOCK
    lane = lax.broadcasted_iota(jnp.int32, (rows, HEAD_DIM), 1)
    chains = []
    for first in range(0, GROUP, heads):
        cols = [slice(g * HEAD_DIM, (g + 1) * HEAD_DIM) for g in range(first, first + heads)]
        query = jnp.concatenate([query_ref[:, c] for c in cols], axis=0)
        grad = jnp.concatenate([grad_ref[:, c] for c in cols], axis=0)
        scores = [matmul_nt(query, key[0]) * (SCALE * LOG2E) for key, _ in pairs]
        prob_grads = [matmul_nt(grad, value[0]) for _, value in pairs]
        chains.append((cols, grad, scores, prob_grads))
    for index, (cols, grad, scores, prob_grads) in enumerate(chains):
        maxima = [jnp.max(s, axis=1, keepdims=True) for s in scores]
        weights = [jnp.exp2(s - m) for s, m in zip(scores, maxima)]
        totals = [jnp.sum(w, axis=1, keepdims=True) for w in weights]
        partials = [
            matmul(w.astype(BF16), value[0]).astype(BF16).astype(F32) for w, (_, value) in zip(weights, pairs)
        ]
        top = jnp.maximum(maxima[0], maxima[1])
        factors = [jnp.exp2(m - top) for m in maxima]
        denominator = factors[0] * totals[0] + factors[1] * totals[1]
        numerator = factors[0] * partials[0] + factors[1] * partials[1]
        output = (numerator / denominator).astype(BF16)
        lse = top + jnp.log2(denominator)
        delta = jnp.sum(grad.astype(F32) * output.astype(F32), axis=1, keepdims=True)
        dq = []
        for (key, _), weight, factor, prob_grad in zip(pairs, weights, factors, prob_grads):
            score_grad = weight * (factor / denominator) * (prob_grad - delta)
            part = matmul(score_grad.astype(BF16), key[0]) * SCALE
            dq.append(part.astype(BF16).astype(F32))
        total = (dq[0] + dq[1]).astype(BF16)
        for g, c in enumerate(cols):
            out_ref[:, c] = output[g * BLOCK : (g + 1) * BLOCK]
            dq_ref[:, c] = total[g * BLOCK : (g + 1) * BLOCK]
        stats = jnp.transpose(jnp.where(lane == 0, lse, delta))
        stat_ref[0, 0:2, index * rows : (index + 1) * rows] = stats[:2]
    for entry in range(2):
        place = places_ref[pl.program_id(0), entry].astype(F32)
        stat_ref[0, 2 + entry : 3 + entry] = jnp.full((1, ROWS), place, F32)


def attend(places, queries, d_out, keys, values):
    blocks = places.shape[0]
    tokens = keys.shape[1]
    text = pl.BlockSpec((BLOCK, GROUP * HEAD_DIM), lambda c, p: (c, 0))

    def image(entry):
        return pl.BlockSpec((1, tokens, HEAD_DIM), lambda c, p: (p[c, entry], 0, 0))

    return pl.pallas_call(
        attend_kernel,
        grid_spec=pltpu.PrefetchScalarGridSpec(
            num_scalar_prefetch=1,
            grid=(blocks,),
            in_specs=[text, text, image(0), image(1), image(0), image(1)],
            out_specs=[text, text, pl.BlockSpec((1, 4, ROWS), lambda c, p: (c, 0, 0))],
        ),
        out_shape=[
            jax.ShapeDtypeStruct(queries.shape, BF16),
            jax.ShapeDtypeStruct(queries.shape, BF16),
            jax.ShapeDtypeStruct((blocks, 4, ROWS), F32),
        ],
        compiler_params=pltpu.CompilerParams(vmem_limit_bytes=VMEM_LIMIT),
        name="attend",
    )(places, queries, d_out, keys, keys, values, values)


def spread_kernel(unroll, places_ref, place_ref, text_ref, stat_ref, key_ref, value_ref, out_ref, *sent_refs):
    line, column = place_ref[0], place_ref[1]
    blocks = text_ref.shape[0]
    tiles = key_ref.shape[0]
    half = HEAD_DIM // 2

    def clear(m, carry):
        out_ref[:, m] = jnp.zeros((4, half, TILE), F32)
        return carry

    lax.fori_loop(0, tiles, clear, 0)

    def one(block):
        query = text_ref[block, 0]
        grad = text_ref[block, 1]
        lse = stat_ref[block, 0:1, :]
        delta = stat_ref[block, 1:2, :]
        for entry in range(2):
            place = places_ref[block, entry]
            row, spot = place // SIDE, place % SIDE
            begin = (7 * spot - column + SIDE - 1) // SIDE
            end = (7 * spot + 7 - column + SIDE - 1) // SIDE
            first = row * 7 + begin
            second = jnp.minimum(first + 1, tiles - 1)
            shut = jnp.where(end - begin == 2, 0.0, 1e30).astype(F32)
            keys = jnp.concatenate([key_ref[first, 0], key_ref[second, 0]], axis=0)
            values = jnp.concatenate([value_ref[first, 0], value_ref[second, 0]], axis=0)
            scores = matmul(keys, query) * (SCALE * LOG2E)
            prob = jnp.concatenate(
                [jnp.exp2(scores[:TILE] - lse), jnp.exp2(scores[TILE:] - (lse + shut))], axis=0
            )
            prob_grad = matmul(values, grad)
            score_grad = prob * (prob_grad - delta)
            d_value = matmul_nt(grad, prob.astype(BF16))
            d_key = matmul_nt(query, score_grad.astype(BF16))
            for i, tile in enumerate((first, second)):
                lanes = slice(i * TILE, (i + 1) * TILE)
                out_ref[0, tile] += d_key[:half, lanes]
                out_ref[1, tile] += d_key[half:, lanes]
                out_ref[2, tile] += d_value[:half, lanes]
                out_ref[3, tile] += d_value[half:, lanes]

    def several(step, carry):
        for u in range(unroll):
            one(step * unroll + u)
        return carry

    lax.fori_loop(0, blocks // unroll, several, 0)

    def scale(m, carry):
        out_ref[0, m] = out_ref[0, m] * SCALE
        out_ref[1, m] = out_ref[1, m] * SCALE
        return carry

    lax.fori_loop(0, tiles, scale, 0)

    part = tiles // 2
    for sent_ref, (shift, high) in zip(sent_refs, FIRST_STEP):
        target = lax.rem(line + SIDE + shift, SIDE)

        def send(m, carry):
            sent_ref[m] = out_ref[target, high * part + m].astype(BF16)
            return carry

        lax.fori_loop(0, part, send, 0)


def spread(places, place, text, stats, keys, values):
    tiles = keys.shape[0]
    half = HEAD_DIM // 2
    image = pl.BlockSpec((tiles, 1, TILE, HEAD_DIM), lambda i, p, c: (0, c[1], 0, 0))
    return pl.pallas_call(
        functools.partial(spread_kernel, SIDE),
        grid_spec=pltpu.PrefetchScalarGridSpec(
            num_scalar_prefetch=2,
            grid=(1,),
            in_specs=[
                pl.BlockSpec(text.shape, lambda i, p, c: (0, 0, 0, 0)),
                pl.BlockSpec(stats.shape, lambda i, p, c: (0, 0, 0)),
                image,
                image,
            ],
            out_specs=[
                pl.BlockSpec((4, tiles, half, TILE), lambda i, p, c: (0, 0, 0, 0)),
                *[pl.BlockSpec((tiles // 2, half, TILE), lambda i, p, c: (0, 0, 0)) for _ in FIRST_STEP],
            ],
        ),
        out_shape=[
            jax.ShapeDtypeStruct((4, tiles, half, TILE), F32),
            *[jax.ShapeDtypeStruct((tiles // 2, half, TILE), BF16) for _ in FIRST_STEP],
        ],
        compiler_params=pltpu.CompilerParams(vmem_limit_bytes=VMEM_LIMIT),
        name="spread",
    )(places, place, text, stats, keys, values)


def fold_kernel(
    shifts, place_ref, grads_ref, own_ref, up_ref, down_ref, far_a_ref, far_b_ref, *out_refs
):
    line, column = place_ref[0], place_ref[1]
    span = own_ref.shape[0]
    first = far_a_ref.shape[0]
    pieces = (
        (own_ref, 0, 0),
        (up_ref, SIDE - 1, 0),
        (down_ref, 1, 0),
        (far_a_ref, 2, 0),
        (far_b_ref, 2, first),
    )
    targets = [lax.rem(column + SIDE + shift, SIDE) for shift in shifts]
    order = [head for target in targets for head in (target, target + SIDE)]
    total = None
    for ref, shift, skip in pieces:
        begin = lax.rem(line + shift, SIDE) * span + skip
        count = ref.shape[0]
        grads = jnp.concatenate(
            [
                jnp.concatenate([grads_ref[head, begin + k] for head in order], axis=0)
                for k in range(count)
            ],
            axis=1,
        )
        feats = jnp.concatenate([ref[k] for k in range(count)], axis=1)
        part = matmul_nt(feats, grads)
        total = part if total is None else total + part
    for index, out_ref in enumerate(out_refs):
        out_ref[...] = total[:, index * HEAD_DIM : (index + 1) * HEAD_DIM]


def fold(shifts, place, grads, pieces):
    depth = pieces[0].shape[1]
    held = pl.BlockSpec(memory_space=pltpu.VMEM)
    far = [pl.BlockSpec(p.shape, lambda i, l: (0, 0, 0)) for p in pieces[3:]]
    return pl.pallas_call(
        functools.partial(fold_kernel, shifts),
        grid_spec=pltpu.PrefetchScalarGridSpec(
            num_scalar_prefetch=1,
            grid=(1,),
            in_specs=[pl.BlockSpec(grads.shape, lambda i, l: (0, 0, 0, 0)), held, held, held, *far],
            out_specs=[held for _ in shifts],
        ),
        out_shape=[jax.ShapeDtypeStruct((depth, HEAD_DIM), F32) for _ in shifts],
        compiler_params=pltpu.CompilerParams(vmem_limit_bytes=VMEM_HALF),
        name="fold",
    )(place, grads, *pieces)


def along_x(shift):
    return [(y * SIDE + x, y * SIDE + (x + shift) % SIDE) for y in range(SIDE) for x in range(SIDE)]


def along_y(shift):
    return [(y * SIDE + x, ((y + shift) % SIDE) * SIDE + x) for y in range(SIDE) for x in range(SIDE)]


X_GROUPS = [[y * SIDE + x for x in range(SIDE)] for y in range(SIDE)]
Y_GROUPS = [[y * SIDE + x for y in range(SIDE)] for x in range(SIDE)]


def move(array, perm):
    return lax.ppermute(array, "seq", perm)


def around(block, along):
    half = block.shape[0] // 2
    left, right = move(block, along(1)), move(block, along(-1))
    far_low, far_high = move(left[:half], along(1)), move(right[half:], along(-1))
    return ((0, 0, block), (-1, 0, left), (1, 0, right), (2, 0, far_low), (2, half, far_high))


def ring_sum(parts, along, sent, ready=None):
    half = parts[0].shape[0] // 2
    lows = {shift: part[:half] for shift, part in parts.items()}
    highs = {shift: part[half:] for shift, part in parts.items()}

    def shifted(term, shift):
        return move(term.astype(sent), along(shift))

    if ready is None:
        ready = [(highs if high else lows)[shift] for shift, high in FIRST_STEP]
    far = shifted(ready[0], 1), shifted(ready[1], -1)
    left_high, right_low = shifted(ready[2], 1), shifted(ready[3], -1)
    far_low, far_high = lax.optimization_barrier(far)
    near = (lows[1] + far_low.astype(F32)).astype(sent), (highs[-1] + far_high.astype(F32)).astype(sent)
    near_low, near_high = lax.optimization_barrier(near)
    left_low, right_high = shifted(near_low, 1), shifted(near_high, -1)
    low = lows[0] + right_low.astype(F32) + left_low.astype(F32)
    high = highs[0] + left_high.astype(F32) + right_high.astype(F32)
    return low.astype(BF16), high.astype(BF16)


def per_device(queries, d_out, image_feats, key_weight, value_weight, image_lists, owner):
    me = lax.axis_index("seq")
    line, column = me // SIDE, me % SIDE
    blocks = image_lists.shape[0]
    feats = image_feats[0].T
    depth, tokens = feats.shape
    tiles = tokens // TILE

    image_ids = lax.broadcasted_iota(jnp.int32, (*image_lists.shape, owner.shape[0]), 2)
    places = jnp.sum(jnp.where(image_lists[..., None] == image_ids, owner[None, None, :], 0), axis=-1)

    part = project(feats, key_weight, value_weight)
    queries_late, d_out_late, feats_late, part = lax.optimization_barrier((queries, d_out, feats, part))
    summed = lax.psum_scatter(part, "tp", scatter_dimension=0, tiled=True)

    def turned(array):
        return array.reshape(blocks, BLOCK, GROUP, HEAD_DIM).transpose(0, 3, 2, 1).reshape(blocks, HEAD_DIM, ROWS)

    text = jnp.stack([turned(queries_late), turned(d_out_late)], axis=1)
    text_left = move(text, along_x(1))
    text_right = move(text, along_x(-1))
    far_a = move(text_left[: blocks // 2], along_x(1))
    far_b = move(text_right[blocks // 2 :], along_x(-1))
    row_text = jnp.concatenate([text, text_left, text_right, far_a, far_b], axis=0)

    tiled = jnp.concatenate([feats_late, jnp.zeros((depth, TILE), BF16)], axis=1)
    buffer = jnp.zeros((tiles + 1, depth, TILE), BF16)
    for shift in range(SIDE):
        target = (column + shift) % SIDE
        first = (target + column) % SIDE
        slab = jnp.stack(
            [
                lax.dynamic_slice_in_dim(tiled, first * TILE, TILE, 1),
                lax.dynamic_slice_in_dim(tiled, (first + SIDE) * TILE, TILE, 1),
            ]
        )
        if shift:
            slab = move(slab, along_x(shift))
        source = (column - shift) % SIDE
        first = (column + source) % SIDE
        slot = (7 * source + first - column) // SIDE
        second = jnp.where(first + SIDE < tiles, slot + 1, tiles)
        buffer = lax.dynamic_update_slice_in_dim(buffer, slab[1:], second, 0)
        buffer = lax.dynamic_update_slice_in_dim(buffer, slab[:1], slot, 0)
    own_feats = buffer[:tiles]
    summed, row_text, own_feats = lax.optimization_barrier((summed, row_text, own_feats))
    pair = summed[0].astype(BF16)
    keys, values = pair[:, :HEAD_DIM], pair[:, HEAD_DIM:]

    key_row = jnp.zeros((SIDE, tokens, HEAD_DIM), BF16)
    for shift, offset, piece in around(keys, along_x):
        key_row = lax.dynamic_update_slice(key_row, piece[None], ((column + shift) % SIDE, offset, 0))
    value_line = jnp.zeros((SIDE, tokens, HEAD_DIM), BF16)
    for shift, offset, piece in around(values, along_y):
        value_line = lax.dynamic_update_slice(value_line, piece[None], ((line + shift) % SIDE, offset, 0))
    keys = jnp.zeros((SIDE, SIDE, tokens, HEAD_DIM), BF16)
    for shift, offset, piece in around(key_row, along_y):
        keys = lax.dynamic_update_slice(keys, piece[None], ((line + shift) % SIDE, offset, 0, 0))
    values = jnp.zeros((SIDE, SIDE, tokens, HEAD_DIM), BF16)
    for shift, offset, piece in around(value_line, along_x):
        values = lax.dynamic_update_slice(values, piece[:, None], (offset, (column + shift) % SIDE, 0, 0))
    keys, values, own_feats = lax.optimization_barrier((keys, values, own_feats))
    feats_up = move(own_feats, along_y(1))
    feats_down = move(own_feats, along_y(-1))

    images = (SIDE * SIDE, tokens, HEAD_DIM)
    attended, d_queries, stats = attend(places, queries, d_out, keys.reshape(images), values.reshape(images))

    row_stats = jnp.concatenate(
        [stats] + [move(stats, along_x(shift)) for shift in (1, -1, 2)],
        axis=0,
    )
    row_places = row_stats[:, 2:, 0].astype(jnp.int32)
    split = (-1, SIDE, TILE, HEAD_DIM)
    place = jnp.stack([line, column])
    grads, *ready = spread(row_places, place, row_text, row_stats, keys.reshape(split), values.reshape(split))
    grads, feats_up, feats_down, *ready = lax.optimization_barrier((grads, feats_up, feats_down, *ready))

    parts = {
        shift: lax.dynamic_index_in_dim(grads, (line + shift) % SIDE, 0, False) for shift in (1, -1, 0)
    }
    own = jnp.concatenate(ring_sum(parts, along_y, BF16, ready))
    cut = (tiles + 1) // 2
    own, up_cut, down_cut = lax.optimization_barrier((own, feats_up[:cut], feats_down[cut:]))
    all_heads = lax.all_gather(own[None], "tp", axis=0, tiled=True)
    feats_far_a = move(up_cut, along_y(1))
    feats_far_b = move(down_cut, along_y(-1))
    pieces = (own_feats, feats_up, feats_down, feats_far_a, feats_far_b)
    parts = {}
    for shifts in ((2, 1), (-1, 0)):
        parts.update(zip(shifts, fold(shifts, place, all_heads, pieces)))
    rows = ring_sum(parts, along_x, F32)

    half = HEAD_DIM // 2
    side = line % 2
    swap = [(y * SIDE + x, (y ^ 1) * SIDE + x) for y in range(SIDE) for x in range(SIDE)]
    given = [jnp.where(side == 0, r[:, half:], r[:, :half]) for r in rows]
    taken = move(jnp.concatenate(given, axis=1), swap)
    taken = taken[:, :half], taken[:, half:]
    kept = [jnp.where(side == 0, r[:, :half], r[:, half:]) for r in rows]
    d_projection = jnp.concatenate(
        [
            jnp.concatenate([jnp.where(side == 0, k, t), jnp.where(side == 0, t, k)], axis=1)
            for k, t in zip(kept, taken)
        ]
    ).T
    return attended, d_queries, d_projection


def solution(mesh):
    return jax.shard_map(
        per_device,
        mesh=mesh,
        in_specs=(
            P(("dp", "seq"), "tp"),
            P(("dp", "seq"), "tp"),
            P(("dp", "seq"), None, "tp"),
            P("tp", None),
            P("tp", None),
            P(("dp", "seq"), None),
            P("dp"),
        ),
        out_specs=(P(("dp", "seq"), "tp"), P(("dp", "seq"), "tp"), P(("dp", "seq"), "tp")),
        check_vma=False,
    )
```

```python
import functools
import math

import jax
import jax.numpy as jnp
from jax import lax
from jax.experimental import pallas as pl
from jax.experimental.pallas import tpu as pltpu
from jax.sharding import PartitionSpec as P

QHEADS = 64
KVHEADS = 8
GROUP = QHEADS // KVHEADS
HEAD_DIM = 128
BLOCK = 64
ROWS = BLOCK * GROUP
TILE = 128
SIDE = 4
SCALE = HEAD_DIM ** -0.5
LOG2E = math.log2(math.e)
LN2 = math.log(2.0)
BF16 = jnp.bfloat16
F32 = jnp.float32
FIRST_STEP = ((2, 0), (2, 1), (1, 1), (-1, 0))
NT = (((1,), (1,)), ((), ()))
VMEM_LIMIT = 56 * 1024 * 1024
VMEM_HALF = 28 * 1024 * 1024


def matmul(a, b):
    return jnp.dot(a, b, preferred_element_type=F32)


def matmul_nt(a, b):
    return lax.dot_general(a, b, NT, preferred_element_type=F32)


def project_kernel(feats_ref, key_ref, value_ref, out_ref, turned_ref):
    @pl.when(pl.program_id(0) == 0)
    def _():
        turned_ref[...] = jnp.transpose(feats_ref[...])

    feats = turned_ref[...]
    for part, weight_ref in enumerate((key_ref, value_ref)):
        lanes = slice(part * HEAD_DIM, (part + 1) * HEAD_DIM)
        for head in range(0, out_ref.shape[0], 2):
            both = matmul(feats, weight_ref[:, head * HEAD_DIM : (head + 2) * HEAD_DIM])
            out_ref[head, :, lanes] = both[:, :HEAD_DIM]
            out_ref[head + 1, :, lanes] = both[:, HEAD_DIM:]


def project(feats, key_weight, value_weight):
    depth, tokens = feats.shape
    weight_spec = pl.BlockSpec((depth, KVHEADS // 2 * HEAD_DIM), lambda i: (0, i))
    return pl.pallas_call(
        project_kernel,
        grid=(2,),
        in_specs=[pl.BlockSpec((depth, tokens), lambda i: (0, 0)), weight_spec, weight_spec],
        out_specs=pl.BlockSpec((KVHEADS // 2, tokens, 2 * HEAD_DIM), lambda i: (i, 0, 0)),
        out_shape=jax.ShapeDtypeStruct((KVHEADS, tokens, 2 * HEAD_DIM), F32),
        scratch_shapes=[pltpu.VMEM((tokens, depth), BF16)],
        compiler_params=pltpu.CompilerParams(vmem_limit_bytes=VMEM_LIMIT),
        name="project",
    )(feats, key_weight, value_weight)


def attend_kernel(
    places_ref, query_ref, grad_ref, key0_ref, key1_ref, value0_ref, value1_ref, out_ref, dq_ref, stat_ref
):
    pairs = ((key0_ref, value0_ref), (key1_ref, value1_ref))
    heads = GROUP
    rows = heads * BLOCK
    lane = lax.broadcasted_iota(jnp.int32, (rows, HEAD_DIM), 1)
    chains = []
    for first in range(0, GROUP, heads):
        cols = [slice(g * HEAD_DIM, (g + 1) * HEAD_DIM) for g in range(first, first + heads)]
        query = jnp.concatenate([query_ref[:, c] for c in cols], axis=0)
        grad = jnp.concatenate([grad_ref[:, c] for c in cols], axis=0)
        scores = [matmul_nt(query, key[0]) * (SCALE * LOG2E) for key, _ in pairs]
        prob_grads = [matmul_nt(grad, value[0]) for _, value in pairs]
        chains.append((cols, grad, scores, prob_grads))
    for index, (cols, grad, scores, prob_grads) in enumerate(chains):
        maxima = [jnp.max(s, axis=1, keepdims=True) for s in scores]
        weights = [jnp.exp2(s - m) for s, m in zip(scores, maxima)]
        totals = [jnp.sum(w, axis=1, keepdims=True) for w in weights]
        partials = [
            matmul(w.astype(BF16), value[0]).astype(BF16).astype(F32) for w, (_, value) in zip(weights, pairs)
        ]
        top = jnp.maximum(maxima[0], maxima[1])
        factors = [jnp.exp2(m - top) for m in maxima]
        denominator = factors[0] * totals[0] + factors[1] * totals[1]
        numerator = factors[0] * partials[0] + factors[1] * partials[1]
        output = (numerator / denominator).astype(BF16)
        lse = top + jnp.log2(denominator)
        delta = jnp.sum(grad.astype(F32) * output.astype(F32), axis=1, keepdims=True)
        dq = []
        for (key, _), weight, factor, prob_grad in zip(pairs, weights, factors, prob_grads):
            score_grad = weight * (factor / denominator) * (prob_grad - delta)
            part = matmul(score_grad.astype(BF16), key[0]) * SCALE
            dq.append(part.astype(BF16).astype(F32))
        total = (dq[0] + dq[1]).astype(BF16)
        for g, c in enumerate(cols):
            out_ref[:, c] = output[g * BLOCK : (g + 1) * BLOCK]
            dq_ref[:, c] = total[g * BLOCK : (g + 1) * BLOCK]
        stats = jnp.transpose(jnp.where(lane == 0, lse, delta))
        stat_ref[0, 0:2, index * rows : (index + 1) * rows] = stats[:2]
    for entry in range(2):
        place = places_ref[pl.program_id(0), entry].astype(F32)
        stat_ref[0, 2 + entry : 3 + entry] = jnp.full((1, ROWS), place, F32)


def attend(places, queries, d_out, keys, values):
    blocks = places.shape[0]
    tokens = keys.shape[1]
    text = pl.BlockSpec((BLOCK, GROUP * HEAD_DIM), lambda c, p: (c, 0))

    def image(entry):
        return pl.BlockSpec((1, tokens, HEAD_DIM), lambda c, p: (p[c, entry], 0, 0))

    return pl.pallas_call(
        attend_kernel,
        grid_spec=pltpu.PrefetchScalarGridSpec(
            num_scalar_prefetch=1,
            grid=(blocks,),
            in_specs=[text, text, image(0), image(1), image(0), image(1)],
            out_specs=[text, text, pl.BlockSpec((1, 4, ROWS), lambda c, p: (c, 0, 0))],
        ),
        out_shape=[
            jax.ShapeDtypeStruct(queries.shape, BF16),
            jax.ShapeDtypeStruct(queries.shape, BF16),
            jax.ShapeDtypeStruct((blocks, 4, ROWS), F32),
        ],
        compiler_params=pltpu.CompilerParams(vmem_limit_bytes=VMEM_LIMIT),
        name="attend",
    )(places, queries, d_out, keys, keys, values, values)


def spread_kernel(unroll, places_ref, place_ref, text_ref, stat_ref, key_ref, value_ref, out_ref, *sent_refs):
    line, column = place_ref[0], place_ref[1]
    blocks = text_ref.shape[0]
    tiles = key_ref.shape[0]
    half = HEAD_DIM // 2

    def clear(m, carry):
        out_ref[:, m] = jnp.zeros((4, half, TILE), F32)
        return carry

    lax.fori_loop(0, tiles, clear, 0)

    def one(block):
        query = text_ref[block, 0]
        grad = text_ref[block, 1]
        lse = stat_ref[block, 0:1, :]
        delta = stat_ref[block, 1:2, :]
        for entry in range(2):
            place = places_ref[block, entry]
            row, spot = place // SIDE, place % SIDE
            begin = (7 * spot - column + SIDE - 1) // SIDE
            end = (7 * spot + 7 - column + SIDE - 1) // SIDE
            first = row * 7 + begin
            second = jnp.minimum(first + 1, tiles - 1)
            shut = jnp.where(end - begin == 2, 0.0, 1e30).astype(F32)
            keys = jnp.concatenate([key_ref[first, 0], key_ref[second, 0]], axis=0)
            values = jnp.concatenate([value_ref[first, 0], value_ref[second, 0]], axis=0)
            scores = matmul(keys, query) * (SCALE * LOG2E)
            prob = jnp.concatenate(
                [jnp.exp2(scores[:TILE] - lse), jnp.exp2(scores[TILE:] - (lse + shut))], axis=0
            )
            prob_grad = matmul(values, grad)
            score_grad = prob * (prob_grad - delta)
            d_value = matmul_nt(grad, prob.astype(BF16))
            d_key = matmul_nt(query, score_grad.astype(BF16))
            for i, tile in enumerate((first, second)):
                lanes = slice(i * TILE, (i + 1) * TILE)
                out_ref[0, tile] += d_key[:half, lanes]
                out_ref[1, tile] += d_key[half:, lanes]
                out_ref[2, tile] += d_value[:half, lanes]
                out_ref[3, tile] += d_value[half:, lanes]

    def several(step, carry):
        for u in range(unroll):
            one(step * unroll + u)
        return carry

    lax.fori_loop(0, blocks // unroll, several, 0)

    def scale(m, carry):
        out_ref[0, m] = out_ref[0, m] * SCALE
        out_ref[1, m] = out_ref[1, m] * SCALE
        return carry

    lax.fori_loop(0, tiles, scale, 0)

    part = tiles // 2
    for sent_ref, (shift, high) in zip(sent_refs, FIRST_STEP):
        target = lax.rem(line + SIDE + shift, SIDE)

        def send(m, carry):
            sent_ref[m] = out_ref[target, high * part + m].astype(BF16)
            return carry

        lax.fori_loop(0, part, send, 0)


def spread(places, place, text, stats, keys, values):
    tiles = keys.shape[0]
    half = HEAD_DIM // 2
    image = pl.BlockSpec((tiles, 1, TILE, HEAD_DIM), lambda i, p, c: (0, c[1], 0, 0))
    return pl.pallas_call(
        functools.partial(spread_kernel, 2 * SIDE),
        grid_spec=pltpu.PrefetchScalarGridSpec(
            num_scalar_prefetch=2,
            grid=(1,),
            in_specs=[
                pl.BlockSpec(text.shape, lambda i, p, c: (0, 0, 0, 0)),
                pl.BlockSpec(stats.shape, lambda i, p, c: (0, 0, 0)),
                image,
                image,
            ],
            out_specs=[
                pl.BlockSpec((4, tiles, half, TILE), lambda i, p, c: (0, 0, 0, 0)),
                *[pl.BlockSpec((tiles // 2, half, TILE), lambda i, p, c: (0, 0, 0)) for _ in FIRST_STEP],
            ],
        ),
        out_shape=[
            jax.ShapeDtypeStruct((4, tiles, half, TILE), F32),
            *[jax.ShapeDtypeStruct((tiles // 2, half, TILE), BF16) for _ in FIRST_STEP],
        ],
        compiler_params=pltpu.CompilerParams(vmem_limit_bytes=VMEM_LIMIT),
        name="spread",
    )(places, place, text, stats, keys, values)


def fold_kernel(
    shifts, place_ref, grads_ref, own_ref, up_ref, down_ref, far_a_ref, far_b_ref, *out_refs
):
    line, column = place_ref[0], place_ref[1]
    span = own_ref.shape[0]
    first = far_a_ref.shape[0]
    pieces = (
        (own_ref, 0, 0),
        (up_ref, SIDE - 1, 0),
        (down_ref, 1, 0),
        (far_a_ref, 2, 0),
        (far_b_ref, 2, first),
    )
    targets = [lax.rem(column + SIDE + shift, SIDE) for shift in shifts]
    order = [head for target in targets for head in (target, target + SIDE)]
    total = None
    for ref, shift, skip in pieces:
        begin = lax.rem(line + shift, SIDE) * span + skip
        count = ref.shape[0]
        grads = jnp.concatenate(
            [
                jnp.concatenate([grads_ref[head, begin + k] for head in order], axis=0)
                for k in range(count)
            ],
            axis=1,
        )
        feats = jnp.concatenate([ref[k] for k in range(count)], axis=1)
        part = matmul_nt(feats, grads)
        total = part if total is None else total + part
    for index, out_ref in enumerate(out_refs):
        out_ref[...] = total[:, index * HEAD_DIM : (index + 1) * HEAD_DIM]


def fold(shifts, place, grads, pieces):
    depth = pieces[0].shape[1]
    held = pl.BlockSpec(memory_space=pltpu.VMEM)
    far = [pl.BlockSpec(p.shape, lambda i, l: (0, 0, 0)) for p in pieces[3:]]
    return pl.pallas_call(
        functools.partial(fold_kernel, shifts),
        grid_spec=pltpu.PrefetchScalarGridSpec(
            num_scalar_prefetch=1,
            grid=(1,),
            in_specs=[pl.BlockSpec(grads.shape, lambda i, l: (0, 0, 0, 0)), held, held, held, *far],
            out_specs=[held for _ in shifts],
        ),
        out_shape=[jax.ShapeDtypeStruct((depth, HEAD_DIM), F32) for _ in shifts],
        compiler_params=pltpu.CompilerParams(vmem_limit_bytes=VMEM_HALF),
        name="fold",
    )(place, grads, *pieces)


def along_x(shift):
    return [(y * SIDE + x, y * SIDE + (x + shift) % SIDE) for y in range(SIDE) for x in range(SIDE)]


def along_y(shift):
    return [(y * SIDE + x, ((y + shift) % SIDE) * SIDE + x) for y in range(SIDE) for x in range(SIDE)]


X_GROUPS = [[y * SIDE + x for x in range(SIDE)] for y in range(SIDE)]
Y_GROUPS = [[y * SIDE + x for y in range(SIDE)] for x in range(SIDE)]


def move(array, perm):
    return lax.ppermute(array, "seq", perm)


def around(block, along):
    half = block.shape[0] // 2
    left, right = move(block, along(1)), move(block, along(-1))
    far_low, far_high = move(left[:half], along(1)), move(right[half:], along(-1))
    return ((0, 0, block), (-1, 0, left), (1, 0, right), (2, 0, far_low), (2, half, far_high))


def ring_sum(parts, along, sent, ready=None):
    half = parts[0].shape[0] // 2
    lows = {shift: part[:half] for shift, part in parts.items()}
    highs = {shift: part[half:] for shift, part in parts.items()}

    def shifted(term, shift):
        return move(term.astype(sent), along(shift))

    if ready is None:
        ready = [(highs if high else lows)[shift] for shift, high in FIRST_STEP]
    far = shifted(ready[0], 1), shifted(ready[1], -1)
    left_high, right_low = shifted(ready[2], 1), shifted(ready[3], -1)
    far_low, far_high = lax.optimization_barrier(far)
    near = (lows[1] + far_low.astype(F32)).astype(sent), (highs[-1] + far_high.astype(F32)).astype(sent)
    near_low, near_high = lax.optimization_barrier(near)
    left_low, right_high = shifted(near_low, 1), shifted(near_high, -1)
    low = lows[0] + right_low.astype(F32) + left_low.astype(F32)
    high = highs[0] + left_high.astype(F32) + right_high.astype(F32)
    return low.astype(BF16), high.astype(BF16)


def per_device(queries, d_out, image_feats, key_weight, value_weight, image_lists, owner):
    me = lax.axis_index("seq")
    line, column = me // SIDE, me % SIDE
    blocks = image_lists.shape[0]
    feats = image_feats[0].T
    depth, tokens = feats.shape
    tiles = tokens // TILE

    image_ids = lax.broadcasted_iota(jnp.int32, (*image_lists.shape, owner.shape[0]), 2)
    places = jnp.sum(jnp.where(image_lists[..., None] == image_ids, owner[None, None, :], 0), axis=-1)

    part = project(feats, key_weight, value_weight)
    queries_late, d_out_late, feats_late, part = lax.optimization_barrier((queries, d_out, feats, part))
    summed = lax.psum_scatter(part, "tp", scatter_dimension=0, tiled=True)

    def turned(array):
        return array.reshape(blocks, BLOCK, GROUP, HEAD_DIM).transpose(0, 3, 2, 1).reshape(blocks, HEAD_DIM, ROWS)

    text = jnp.stack([turned(queries_late), turned(d_out_late)], axis=1)
    text_left = move(text, along_x(1))
    text_right = move(text, along_x(-1))
    far_a = move(text_left[: blocks // 2], along_x(1))
    far_b = move(text_right[blocks // 2 :], along_x(-1))
    row_text = jnp.concatenate([text, text_left, text_right, far_a, far_b], axis=0)

    tiled = jnp.concatenate([feats_late, jnp.zeros((depth, TILE), BF16)], axis=1)
    buffer = jnp.zeros((tiles + 1, depth, TILE), BF16)
    for shift in range(SIDE):
        target = (column + shift) % SIDE
        first = (target + column) % SIDE
        slab = jnp.stack(
            [
                lax.dynamic_slice_in_dim(tiled, first * TILE, TILE, 1),
                lax.dynamic_slice_in_dim(tiled, (first + SIDE) * TILE, TILE, 1),
            ]
        )
        if shift:
            slab = move(slab, along_x(shift))
        source = (column - shift) % SIDE
        first = (column + source) % SIDE
        slot = (7 * source + first - column) // SIDE
        second = jnp.where(first + SIDE < tiles, slot + 1, tiles)
        buffer = lax.dynamic_update_slice_in_dim(buffer, slab[1:], second, 0)
        buffer = lax.dynamic_update_slice_in_dim(buffer, slab[:1], slot, 0)
    own_feats = buffer[:tiles]
    summed, row_text, own_feats = lax.optimization_barrier((summed, row_text, own_feats))
    pair = summed[0].astype(BF16)
    keys, values = pair[:, :HEAD_DIM], pair[:, HEAD_DIM:]

    key_row = jnp.zeros((SIDE, tokens, HEAD_DIM), BF16)
    for shift, offset, piece in around(keys, along_x):
        key_row = lax.dynamic_update_slice(key_row, piece[None], ((column + shift) % SIDE, offset, 0))
    value_line = jnp.zeros((SIDE, tokens, HEAD_DIM), BF16)
    for shift, offset, piece in around(values, along_y):
        value_line = lax.dynamic_update_slice(value_line, piece[None], ((line + shift) % SIDE, offset, 0))
    keys = jnp.zeros((SIDE, SIDE, tokens, HEAD_DIM), BF16)
    for shift, offset, piece in around(key_row, along_y):
        keys = lax.dynamic_update_slice(keys, piece[None], ((line + shift) % SIDE, offset, 0, 0))
    values = jnp.zeros((SIDE, SIDE, tokens, HEAD_DIM), BF16)
    for shift, offset, piece in around(value_line, along_x):
        values = lax.dynamic_update_slice(values, piece[:, None], (offset, (column + shift) % SIDE, 0, 0))
    keys, values, own_feats = lax.optimization_barrier((keys, values, own_feats))
    feats_up = move(own_feats, along_y(1))
    feats_down = move(own_feats, along_y(-1))

    images = (SIDE * SIDE, tokens, HEAD_DIM)
    attended, d_queries, stats = attend(places, queries, d_out, keys.reshape(images), values.reshape(images))

    row_stats = jnp.concatenate(
        [stats] + [move(stats, along_x(shift)) for shift in (1, -1, 2)],
        axis=0,
    )
    row_places = row_stats[:, 2:, 0].astype(jnp.int32)
    split = (-1, SIDE, TILE, HEAD_DIM)
    place = jnp.stack([line, column])
    grads, *ready = spread(row_places, place, row_text, row_stats, keys.reshape(split), values.reshape(split))
    grads, feats_up, feats_down, *ready = lax.optimization_barrier((grads, feats_up, feats_down, *ready))

    parts = {
        shift: lax.dynamic_index_in_dim(grads, (line + shift) % SIDE, 0, False) for shift in (1, -1, 0)
    }
    own = jnp.concatenate(ring_sum(parts, along_y, BF16, ready))
    cut = (tiles + 1) // 2
    own, up_cut, down_cut = lax.optimization_barrier((own, feats_up[:cut], feats_down[cut:]))
    all_heads = lax.all_gather(own[None], "tp", axis=0, tiled=True)
    feats_far_a = move(up_cut, along_y(1))
    feats_far_b = move(down_cut, along_y(-1))
    pieces = (own_feats, feats_up, feats_down, feats_far_a, feats_far_b)
    parts = {}
    for shifts in ((2, 1), (-1, 0)):
        parts.update(zip(shifts, fold(shifts, place, all_heads, pieces)))
    rows = ring_sum(parts, along_x, F32)

    half = HEAD_DIM // 2
    side = line % 2
    swap = [(y * SIDE + x, (y ^ 1) * SIDE + x) for y in range(SIDE) for x in range(SIDE)]
    given = [jnp.where(side == 0, r[:, half:], r[:, :half]) for r in rows]
    taken = move(jnp.concatenate(given, axis=1), swap)
    taken = taken[:, :half], taken[:, half:]
    kept = [jnp.where(side == 0, r[:, :half], r[:, half:]) for r in rows]
    d_projection = jnp.concatenate(
        [
            jnp.concatenate([jnp.where(side == 0, k, t), jnp.where(side == 0, t, k)], axis=1)
            for k, t in zip(kept, taken)
        ]
    ).T
    return attended, d_queries, d_projection


def solution(mesh):
    return jax.shard_map(
        per_device,
        mesh=mesh,
        in_specs=(
            P(("dp", "seq"), "tp"),
            P(("dp", "seq"), "tp"),
            P(("dp", "seq"), None, "tp"),
            P("tp", None),
            P("tp", None),
            P(("dp", "seq"), None),
            P("dp"),
        ),
        out_specs=(P(("dp", "seq"), "tp"), P(("dp", "seq"), "tp"), P(("dp", "seq"), "tp")),
        check_vma=False,
    )
```
